32 devices in a mesh: grp: 2 (over y), tile: 4 (over z), row: 2 (over x), sub: 2 (over core).
Axes of the slice: x: 2, y: 2, z: 4, core: 2. Of those that a mesh axis runs over, the one named last changes fastest.
Arguments:
- velocity: float32 [2, 480, 960], P(None, ('grp', 'row'), ('tile', 'sub')), parts along dimension 1, may hold values from -10 to 10, as said below
- wet_bits: int32 [16, 960], P(('grp', 'row'), ('tile', 'sub')), parts along dimension 0, may hold values from 0 to 1073741823, as said below
- east_face: int32 [4], replicated, may hold values from 0 to 3, as said below
- seam_turn: int32 [4], replicated, may hold values from 0 to 3
Outputs:
- forcing: float32 [2, 120, 240], P(None, ('grp', 'row'), ('tile', 'sub')), parts along dimension 1
The draws below stay inside these ranges and needn't reach their ends.
There are 2 independent parts, one for each index of `grp`. The reference program is written for one: setup_inputs(seed, part) draws one part's arguments, and reference() takes and returns one part's arrays. A program takes and returns all parts, laid end to end along the dimension named above; an argument that names none is the same for every part. Nothing has to cross between parts.
Inputs may be any that keep to these rules, and one draw needn't show every extreme that they name: `velocity`: gentle combinations of a few waves plus independent cell-to-cell parts. Bit b of wet_bits[j, x] is 1 where cell (30 j + b, x) is wet and 0 on land. `east_face`: each face is east of exactly one face.
All inputs are finite; a program needn't handle non-finite values.
Results may differ from the reference program's by a relative error of at most 0.000098.
Values sent between devices are 32-bit elements; how exact they have to be, the bound alone decides.
A program may use at most 64 MiB of HBM per device.

```python
import jax
import jax.numpy as jnp
from jax import lax

CX = 120
R = 32
FACES = 4
NY = 240
NX = 960
N_SUB = 2


def draw_velocity(key, part):
    keys = jax.random.split(key, 5)
    full_shape = (2, NY, NX)
    rough = jnp.clip(jax.random.normal(keys[0], full_shape, jnp.float32), -4.0, 4.0)
    row_index = jnp.arange(NY, dtype=jnp.float32)[:, None]
    col_index = jnp.arange(NX, dtype=jnp.float32)[None, :]
    wave_x = jax.random.randint(keys[1], (2, 4), 1, 5).astype(jnp.float32)
    wave_y = jax.random.randint(keys[2], (2, 4), 1, 5).astype(jnp.float32)
    phases = jax.random.uniform(keys[3], (2, 4), jnp.float32, -3.14159, 3.14159)
    amplitude = jax.random.uniform(keys[4], (2, 4), jnp.float32, -1.5, 1.5)
    smooth = jnp.zeros(full_shape, jnp.float32)
    for mode in range(4):
        angle = 6.2831853 * (wave_x[:, mode, None, None] * col_index / 256.0 + wave_y[:, mode, None, None] * row_index / 256.0) + phases[:, mode, None, None]
        smooth = smooth + amplitude[:, mode, None, None] * jnp.sin(angle)
    return (rough + smooth).astype(jnp.float32)


def draw_wet_bits(key, part):
    row_index = jnp.arange(NY, dtype=jnp.int32)[:, None]
    col_index = jnp.arange(NX, dtype=jnp.int32)[None, :]
    land = jax.random.randint(jax.random.fold_in(key, 99), (NY, NX), 0, 20) == 0
    for box_index in range(10):
        box_key = jax.random.split(jax.random.fold_in(key, box_index), 4)
        top = jax.random.randint(box_key[0], (), 0, NY)
        height = jax.random.randint(box_key[1], (), NY // 10, NY // 2)
        left = jax.random.randint(box_key[2], (), 0, NX)
        breadth = jax.random.randint(box_key[3], (), NX // 20, NX // 4)
        inside = (row_index >= top) & (row_index < top + height) & (col_index >= left) & (col_index < left + breadth)
        land = land | inside
    wet = jnp.where(land, 0, 1).astype(jnp.int32)
    shifts = jnp.left_shift(jnp.ones((30,), jnp.int32), jnp.arange(30, dtype=jnp.int32))
    packed = jnp.sum(wet.reshape(NY // 30, 30, NX) * shifts[None, :, None], axis=1)
    return packed.astype(jnp.int32)


def draw_east_face(key, part):
    keys = jax.random.split(key, 2)
    perm = jax.random.permutation(keys[0], FACES).astype(jnp.int32)
    start = jax.random.randint(keys[1], (), 0, FACES).astype(jnp.int32)
    target = ((start + FACES // 2) % FACES).astype(jnp.int32)
    positions = jnp.arange(FACES, dtype=jnp.int32)
    where_target = jnp.sum(jnp.where(perm == target, positions, 0)).astype(jnp.int32)
    previous = perm[start]
    return perm.at[where_target].set(previous).at[start].set(target).astype(jnp.int32)


def place_ends(values, rng, low, high):
    shape = values.shape
    index_at = [jax.random.randint(jax.random.fold_in(rng, axis), (), 0, shape[axis]) for axis in range(len(shape))]
    values = values.at[tuple(index_at)].set(low)
    longest = shape.index(max(shape))
    index_at[longest] = (index_at[longest] + 1) % shape[longest]
    return values.at[tuple(index_at)].set(high)


def setup_inputs(seed: int = 0, part: int = 0) -> dict:
    key_list = jax.random.split(jax.random.key(seed), 5)
    part_keys = jax.random.split(jax.random.fold_in(key_list[4], part), 5)
    return {
        "velocity": draw_velocity(jax.random.fold_in(jax.random.fold_in(key_list[4], part), 71), part),
        "wet_bits": draw_wet_bits(jax.random.fold_in(jax.random.fold_in(key_list[4], part), 71), part),
        "east_face": draw_east_face(jax.random.fold_in(key_list[4], 71), part),
        "seam_turn": place_ends(jax.random.randint(key_list[3], (FACES,), 0, 4), jax.random.fold_in(key_list[3], 1), 0, 3).astype(jnp.int32),
    }


deriv_scale = 8.0


def unpack(wet_bits):
    repeated = jnp.repeat(wet_bits, 30, axis=0)
    shifts = lax.broadcasted_iota(jnp.int32, repeated.shape, 0) % 30
    return (jnp.right_shift(repeated, shifts) & 1).astype(jnp.float32)


def banded(n_in, n_out):
    offset = jnp.arange(n_in, dtype=jnp.int32)[:, None] - jnp.arange(n_out, dtype=jnp.int32)[None, :]
    spread = R * 1.0
    centred = (offset - R).astype(jnp.float32)
    taps = (jnp.arange(2 * R + 1, dtype=jnp.int32) - R).astype(jnp.float32)
    weight_sum = jnp.sum(jnp.exp(-0.5 * (taps / spread) ** 2))
    inside = (offset >= 0) & (offset <= 2 * R)
    return jnp.where(inside, jnp.exp(-0.5 * (centred / spread) ** 2) / weight_sum, jnp.float32(0.0)).astype(jnp.float32)


def rotate(strip, turn):
    cosine = jnp.where(turn == 0, 1.0, jnp.where(turn == 2, -1.0, 0.0)).astype(jnp.float32)
    sine_part = jnp.where(turn == 1, 1.0, jnp.where(turn == 3, -1.0, 0.0)).astype(jnp.float32)
    return jnp.stack([cosine * strip[0] - sine_part * strip[1], sine_part * strip[0] + cosine * strip[1]])


def derive(padded):
    centre = padded[:, 1:-1, ..., 1:-1]
    grad_x = deriv_scale * (padded[:, 1:-1, ..., 2:] - padded[:, 1:-1, ..., :-2])
    grad_y = deriv_scale * (padded[:, 2:, ..., 1:-1] - padded[:, :-2, ..., 1:-1])
    advect = centre[0] * grad_x + centre[1] * grad_y
    return jnp.concatenate([centre, grad_x, grad_y, advect], axis=0)


def combine(smooth):
    east_part = smooth[6] - (smooth[0] * smooth[2] + smooth[1] * smooth[4])
    north_part = smooth[7] - (smooth[0] * smooth[3] + smooth[1] * smooth[5])
    return jnp.stack([east_part, north_part])


def reference(velocity, wet_bits, east_face, seam_turn):
    wet = unpack(wet_bits)
    field = velocity * wet[None]
    face_width = N_SUB * CX
    grid = field.reshape(2, NY, FACES, face_width)
    order = jnp.arange(FACES, dtype=jnp.int32)
    west_face = jnp.zeros((FACES,), jnp.int32).at[east_face].set(order)
    west_turn = (4 - seam_turn[west_face]) % 4
    rim_width = R + 1
    from_west = rotate(grid[:, :, west_face, face_width - rim_width:], west_turn[:, None])
    from_east = rotate(grid[:, :, east_face, :rim_width], seam_turn[:, None])
    padded = jnp.concatenate([from_west, grid, from_east], axis=3)
    padded = jnp.pad(padded, ((0, 0), (1, 1), (0, 0), (0, 0)))
    channels = derive(padded)
    along = jnp.einsum("cyfx,xj->cyfj", channels, banded(face_width + 2 * R, face_width), precision=lax.Precision.HIGHEST)
    along = jnp.pad(along, ((0, 0), (R, R), (0, 0), (0, 0)))
    smooth = jnp.einsum("ki,ckfx->cifx", banded(NY + 2 * R, NY), along, precision=lax.Precision.HIGHEST)
    fine = combine(smooth) * wet.reshape(NY, FACES, face_width)[None]
    coarse = fine.reshape(2, NY // 4, 4, FACES, face_width // 4, 4).mean(axis=(2, 5))
    return coarse.reshape(2, NY // 4, NX // 4)
```

```python
import functools
import math

import jax
import jax.numpy as jnp
from jax import lax
from jax.experimental import pallas as pl
from jax.experimental.pallas import tpu as pltpu
from jax.sharding import PartitionSpec as P

R = 32
RIM = R + 1
LANES = 128
RING = 2 * LANES
DERIV_SCALE = 8.0
POOL = 4
WORD_ROWS = 30
MESH = pl.DeviceIdType.MESH

WEIGHT_SUM = sum(math.exp(-0.5 * (k / R) ** 2) for k in range(-R, R + 1))


def ceil_to(value, step):
    return -(-value // step) * step


def gaussian(distance, keep):
    d = distance.astype(jnp.float32) * (1.0 / R)
    weight = jnp.exp(-0.5 * d * d) * (1.0 / WEIGHT_SUM)
    return jnp.where(keep & (jnp.abs(distance) <= R), weight, 0.0)


def split(value):
    high = value.astype(jnp.bfloat16)
    low = (value - high.astype(jnp.float32)).astype(jnp.bfloat16)
    return high, low


def dot(a, b):
    return jnp.dot(a, b, preferred_element_type=jnp.float32)


def roll(value, shift, axis=1):
    size = value.shape[axis]
    shift = shift % size
    return value if shift == 0 else pltpu.roll(value, shift, axis)


def kernel(
    face_ref, turn_ref, vel_hbm, bits_hbm, out_ref,
    vel, bits, ext, strips, seams, ring, pooled,
    load_sem, row_send, row_recv, strip_send, strip_recv,
):
    tiles, rows = lax.axis_size("tile"), lax.axis_size("row")
    grp, tile, row, sub = (lax.axis_index(a) for a in ("grp", "tile", "row", "sub"))
    n_rows, n_cols = vel.shape[1], vel.shape[2]
    halo = ceil_to(RIM, 8)
    has_up, has_down = row > 0, row < rows - 1
    other = 1 - sub

    loads = [
        pltpu.make_async_copy(vel_hbm, vel, load_sem.at[0]),
        pltpu.make_async_copy(bits_hbm, bits, load_sem.at[1]),
    ]
    for load in loads:
        load.start()

    barrier = pltpu.get_barrier_semaphore()

    def greet(t, r, s):
        pl.semaphore_signal(barrier, inc=1, device_id=(grp, t, r, s), device_id_type=MESH)

    for k in range(tiles):
        t = lax.rem(tile + k, tiles)
        greet(t, row, other)

        @pl.when(has_up)
        def _():
            greet(t, row - 1, other)

        @pl.when(has_down)
        def _():
            greet(t, row + 1, other)

    @pl.when(has_up)
    def _():
        greet(tile, row - 1, sub)

    @pl.when(has_down)
    def _():
        greet(tile, row + 1, sub)

    for load in loads:
        load.wait()

    row_id = lax.broadcasted_iota(jnp.int32, (n_rows, n_cols), 0)
    words = bits[...]
    word = jnp.broadcast_to(words[0:1], (n_rows, n_cols))
    bit = row_id
    for j in range(1, words.shape[0]):
        here = row_id >= j * WORD_ROWS
        word = jnp.where(here, words[j : j + 1], word)
        bit = jnp.where(here, row_id - j * WORD_ROWS, bit)
    wet = (jnp.right_shift(word, bit) & 1).astype(jnp.float32)
    for c in range(2):
        ext[c, halo : halo + n_rows, 0:n_cols] = vel[c] * wet

    lane = lax.broadcasted_iota(jnp.int32, (halo, LANES), 1)

    def pack(start):
        def block(c, g, place):
            rows_at = halo + g * halo
            return roll(ext[c, rows_at : rows_at + halo, :], place * RIM - start)

        def join(a, b, c):
            rest = jnp.where(lane < 3 * RIM, c, 0.0)
            return jnp.where(lane < RIM, a, jnp.where(lane < 2 * RIM, b, rest))

        first = join(block(0, 0, 0), block(1, 0, 1), block(0, 1, 2))
        last = join(block(0, 2, 0), block(1, 2, 1), block(1, 1, 2))
        return first, last

    west_cols, east_cols = pack(0), pack(n_cols - RIM)
    at_west = sub == 0
    for i in range(2):
        at = slice(i * halo, (i + 1) * halo)
        strips[0, at, :] = jnp.where(at_west, west_cols[i], east_cols[i])
        strips[1, at, :] = jnp.where(at_west, east_cols[i], west_cols[i])

    @pl.when(jnp.logical_not(has_up))
    def _():
        ext[:, 0:halo, :] = jnp.zeros((2, halo, LANES), jnp.float32)
        seams[:, 0:halo, :] = jnp.zeros((tiles + 1, halo, LANES), jnp.float32)

    @pl.when(jnp.logical_not(has_down))
    def _():
        ext[:, halo + n_rows :, :] = jnp.zeros((2, halo, LANES), jnp.float32)
        seams[:, 3 * halo :, :] = jnp.zeros((tiles + 1, halo, LANES), jnp.float32)

    n_beside = has_up.astype(jnp.int32) + has_down.astype(jnp.int32)
    pl.semaphore_wait(barrier, tiles + n_beside * (tiles + 1))

    def strip_copy(which, slot, part, k, t, r):
        source = ((0, 2 * halo), (halo, halo), (0, halo))[part]
        target = (halo, 0, 3 * halo)[part]
        return pltpu.make_async_remote_copy(
            src_ref=strips.at[which, pl.ds(*source)],
            dst_ref=seams.at[slot, pl.ds(target, source[1])],
            send_sem=strip_send.at[part, k],
            recv_sem=strip_recv.at[part, slot],
            device_id=(grp, t, r, other),
            device_id_type=MESH,
        )

    def row_copy(part, r):
        source = (halo + n_rows - halo, halo)[part - 1]
        target = (0, halo + n_rows)[part - 1]
        return pltpu.make_async_remote_copy(
            src_ref=ext.at[:, pl.ds(source, halo)],
            dst_ref=ext.at[:, pl.ds(target, halo)],
            send_sem=row_send.at[part - 1],
            recv_sem=row_recv.at[part - 1],
            device_id=(grp, tile, r, sub),
            device_id_type=MESH,
        )

    def sends(act, part, r):
        for k in reversed(range(tiles)):
            act(strip_copy(0, tile, part, k, lax.rem(tile + k, tiles), r))
        act(strip_copy(1, tiles, part, tiles, tile, r))
        if part:
            act(row_copy(part, r))

    def all_sends(act):
        sends(act, 0, row)

        @pl.when(has_down)
        def _():
            sends(act, 1, row + 1)

        @pl.when(has_up)
        def _():
            sends(act, 2, row - 1)

    all_sends(lambda copy: copy.start())

    place = lax.broadcasted_iota(jnp.int32, (RING, LANES), 0)
    x_out = lax.broadcasted_iota(jnp.int32, (RING, LANES), 1)
    x_in = jnp.where(place < (n_cols + RING) // 2, place, place - RING)
    x_high, x_low = split(gaussian(x_in - x_out, x_out < n_cols))
    top = halo - R
    span = ceil_to(n_rows + 2 * R, 16)
    span_out = ceil_to(n_rows, 16)
    y_out = lax.broadcasted_iota(jnp.int32, (span_out, span), 0)
    y_in = lax.broadcasted_iota(jnp.int32, (span_out, span), 1) - R
    y_global = y_in + row * n_rows
    inside = (y_global >= 0) & (y_global < rows * n_rows) & (y_out < n_rows)
    y_high, y_low = split(gaussian(y_in - y_out, inside))

    west = jnp.int32(0)
    for i in range(tiles):
        west = jnp.where(face_ref[i] == tile, i, west)
    east_turn = turn_ref[tile]
    west_turn = turn_ref[west]
    west_turn = jnp.where(west_turn == 0, 0, 4 - west_turn)
    beside = jnp.where(at_west, west, face_ref[tile])
    turn = jnp.where(at_west, west_turn, east_turn)

    def choose(a, b):
        return jnp.where(turn == a, 1.0, jnp.where(turn == b, -1.0, 0.0)).astype(jnp.float32)

    cosine, sine = choose(0, 2), choose(1, 3)

    def arrived(part):
        for slot in range(tiles + 1):
            strip_copy(0, slot, part, 0, tile, row).wait_recv()
        if part:
            row_copy(part, row).wait_recv()

    arrived(0)

    @pl.when(has_up)
    def _():
        arrived(1)

    @pl.when(has_down)
    def _():
        arrived(2)

    def unpack(packed, shift):
        a, b, c, d = (packed[i * halo : (i + 1) * halo] for i in range(4))
        places = (((a, 0), (b, 0), (b, 2), (c, 0), (d, 0)), ((a, 1), (b, 1), (c, 2), (c, 1), (d, 1)))
        return [
            jnp.concatenate([roll(v, shift - p * RIM) for v, p in blocks], axis=0) for blocks in places
        ]

    seam, inner = seams[beside], seams[tiles]
    east_u, east_v = unpack(jnp.where(at_west, inner, seam), n_cols)
    west_u, west_v = unpack(jnp.where(at_west, seam, inner), LANES - RIM)
    east_c = jnp.where(at_west, 1.0, cosine).astype(jnp.float32)
    east_s = jnp.where(at_west, 0.0, sine).astype(jnp.float32)
    west_c = jnp.where(at_west, cosine, 1.0).astype(jnp.float32)
    west_s = jnp.where(at_west, sine, 0.0).astype(jnp.float32)
    east_uv = (east_c * east_u - east_s * east_v, east_s * east_u + east_c * east_v)
    west_uv = (west_c * west_u - west_s * west_v, west_s * west_u + west_c * west_v)

    n_ext = ext.shape[1]
    lane = lax.broadcasted_iota(jnp.int32, (n_ext, LANES), 1)
    for c in range(2):
        ring[c, 0:n_ext, 0:LANES] = jnp.where(lane < n_cols, ext[c], east_uv[c])
        rest = jnp.where(lane >= LANES - RIM, west_uv[c], 0.0)
        ring[c, 0:n_ext, LANES:] = jnp.where(lane < n_cols + RIM - LANES, east_uv[c], rest)
        ring[c, n_ext:, :] = jnp.zeros((ring.shape[1] - n_ext, RING), jnp.float32)

    def derive(c):
        centre = ring[c, top : top + span, :]
        grad_x = DERIV_SCALE * (roll(centre, -1) - roll(centre, 1))
        grad_y = DERIV_SCALE * (ring[c, top + 1 : top + 1 + span, :] - ring[c, top - 1 : top - 1 + span, :])
        return centre, grad_x, grad_y

    u, u_x, u_y = derive(0)
    v, v_x, v_y = derive(1)
    channels = (u, v, u_x, v_x, u_y, v_y, u * u_x + v * u_y, u * v_x + v * v_y)

    def smoothed(first, second):
        along = []
        for channel in (first, second):
            high, low = split(channel)
            along.append(dot(high, x_high) + (dot(low, x_high) + dot(high, x_low)))
        high, low = split(jnp.concatenate(along, axis=1))
        both = dot(y_high, high) + (dot(y_high, low) + dot(y_low, high))
        return both[:n_rows, :n_cols], both[:n_rows, LANES : LANES + n_cols]

    smooth = []
    for i in range(0, 8, 2):
        smooth += smoothed(channels[i], channels[i + 1])
    fine = (
        smooth[6] - (smooth[0] * smooth[2] + smooth[1] * smooth[4]),
        smooth[7] - (smooth[0] * smooth[3] + smooth[1] * smooth[5]),
    )

    n_out = n_rows // POOL
    m_out = n_cols // POOL
    col = lax.broadcasted_iota(jnp.int32, (LANES, m_out), 0)
    block_at = lax.broadcasted_iota(jnp.int32, (LANES, m_out), 1) * POOL
    mean = jnp.where((col >= block_at) & (col < block_at + POOL), 1.0 / POOL**2, 0.0)
    mean = mean.astype(jnp.bfloat16)
    for c in range(2):
        pooled[c] = jnp.zeros((n_rows, LANES), jnp.float32)
        pooled[c, :, 0:n_cols] = fine[c] * wet
        total = pooled[c, pl.ds(0, n_out, stride=POOL), :]
        for k in range(1, POOL):
            total = total + pooled[c, pl.ds(k, n_out, stride=POOL), :]
        high, low = split(total)
        out_ref[c] = dot(high, mean) + dot(low, mean)

    all_sends(lambda copy: copy.wait_send())


def on_device(velocity, wet_bits, east_face, seam_turn):
    _, n_rows, n_cols = velocity.shape
    tiles = lax.axis_size("tile")
    halo = ceil_to(RIM, 8)
    assert n_rows == 3 * halo and lax.axis_size("sub") == 2
    assert RIM <= n_cols <= LANES and n_cols + 2 * RIM <= RING and 3 * RIM <= LANES
    n_ext = n_rows + 2 * halo
    f32 = jnp.float32
    return pl.pallas_call(
        kernel,
        out_shape=jax.ShapeDtypeStruct((2, n_rows // POOL, n_cols // POOL), f32),
        in_specs=[
            pl.BlockSpec(memory_space=pltpu.SMEM),
            pl.BlockSpec(memory_space=pltpu.SMEM),
            pl.BlockSpec(memory_space=pl.ANY),
            pl.BlockSpec(memory_space=pl.ANY),
        ],
        out_specs=pl.BlockSpec(memory_space=pltpu.VMEM),
        scratch_shapes=[
            pltpu.VMEM(velocity.shape, f32),
            pltpu.VMEM(wet_bits.shape, jnp.int32),
            pltpu.VMEM((2, n_ext, LANES), f32),
            pltpu.VMEM((2, 2 * halo, LANES), f32),
            pltpu.VMEM((tiles + 1, 4 * halo, LANES), f32),
            pltpu.VMEM((2, n_ext + 8, RING), f32),
            pltpu.VMEM((2, n_rows, LANES), f32),
            pltpu.SemaphoreType.DMA((2,)),
            pltpu.SemaphoreType.DMA((2,)),
            pltpu.SemaphoreType.DMA((2,)),
            pltpu.SemaphoreType.DMA((3, tiles + 1)),
            pltpu.SemaphoreType.DMA((3, tiles + 1)),
        ],
        compiler_params=pltpu.CompilerParams(
            collective_id=0, has_side_effects=True, vmem_limit_bytes=32 * 1024 * 1024
        ),
    )(east_face, seam_turn, velocity, wet_bits)


def solution(mesh):
    placed = (
        P(None, ("grp", "row"), ("tile", "sub")),
        P(("grp", "row"), ("tile", "sub")),
        P(),
        P(),
    )
    return jax.shard_map(
        on_device,
        mesh=mesh,
        in_specs=placed,
        out_specs=P(None, ("grp", "row"), ("tile", "sub")),
        check_vma=False,
    )
```

```python
import functools
import math

import jax
import jax.numpy as jnp
from jax import lax
from jax.experimental import pallas as pl
from jax.experimental.pallas import tpu as pltpu
from jax.sharding import PartitionSpec as P

R = 32
RIM = R + 1
LANES = 128
EDGE = 2
DERIV_SCALE = 8.0
POOL = 4
WORD_ROWS = 30
MESH = pl.DeviceIdType.MESH

WEIGHT_SUM = sum(math.exp(-0.5 * (k / R) ** 2) for k in range(-R, R + 1))


def ceil_to(value, step):
    return -(-value // step) * step


def gaussian(distance, keep):
    d = distance.astype(jnp.float32) * (1.0 / R)
    weight = jnp.exp(-0.5 * d * d) * (1.0 / WEIGHT_SUM)
    return jnp.where(keep & (jnp.abs(distance) <= R), weight, 0.0)


def split(value):
    high = value.astype(jnp.bfloat16)
    low = (value - high.astype(jnp.float32)).astype(jnp.bfloat16)
    return high, low


def dot(a, b):
    return jnp.dot(a, b, preferred_element_type=jnp.float32)


def roll(value, shift, axis=1):
    size = value.shape[axis]
    shift = shift % size
    return value if shift == 0 else pltpu.roll(value, shift, axis)


def kernel(
    face_hbm, turn_hbm, vel_hbm, bits_hbm, out_ref,
    face_ref, turn_ref, vel, bits, ext, strips, seams, ring, inner_sum, pooled,
    load_sem, row_send, row_recv, strip_send, strip_recv,
):
    tiles, rows = lax.axis_size("tile"), lax.axis_size("row")
    grp, tile, row, sub = (lax.axis_index(a) for a in ("grp", "tile", "row", "sub"))
    n_rows, n_cols = vel.shape[1], vel.shape[2]
    halo = ceil_to(RIM, 8)
    has_up, has_down = row > 0, row < rows - 1
    other = 1 - sub

    loads = [
        pltpu.make_async_copy(vel_hbm, vel, load_sem.at[0]),
        pltpu.make_async_copy(bits_hbm, bits, load_sem.at[1]),
        pltpu.make_async_copy(face_hbm, face_ref, load_sem.at[2]),
        pltpu.make_async_copy(turn_hbm, turn_ref, load_sem.at[3]),
    ]
    for load in loads:
        load.start()

    barrier = pltpu.get_barrier_semaphore()

    def greet(t, r, s):
        pl.semaphore_signal(barrier, inc=1, device_id=(grp, t, r, s), device_id_type=MESH)

    for k in range(tiles):
        t = lax.rem(tile + k, tiles)
        greet(t, row, other)

        @pl.when(has_up)
        def _():
            greet(t, row - 1, other)

        @pl.when(has_down)
        def _():
            greet(t, row + 1, other)

    @pl.when(has_up)
    def _():
        greet(tile, row - 1, sub)

    @pl.when(has_down)
    def _():
        greet(tile, row + 1, sub)

    for load in loads:
        load.wait()

    row_id = lax.broadcasted_iota(jnp.int32, (n_rows, n_cols), 0)
    words = bits[...]
    word = jnp.broadcast_to(words[0:1], (n_rows, n_cols))
    bit = row_id
    for j in range(1, words.shape[0]):
        here = row_id >= j * WORD_ROWS
        word = jnp.where(here, words[j : j + 1], word)
        bit = jnp.where(here, row_id - j * WORD_ROWS, bit)
    wet = (jnp.right_shift(word, bit) & 1).astype(jnp.float32)
    for c in range(2):
        ext[c, halo : halo + n_rows, :] = jnp.zeros((n_rows, LANES), jnp.float32)
        ext[c, halo : halo + n_rows, 0:n_cols] = vel[c] * wet
        ext[c, n_rows + 2 * halo :, :] = jnp.zeros((8, LANES), jnp.float32)

    lane = lax.broadcasted_iota(jnp.int32, (halo, LANES), 1)

    def pack(start):
        def block(c, g, place):
            rows_at = halo + g * halo
            return roll(ext[c, rows_at : rows_at + halo, :], place * RIM - start)

        def join(a, b, c):
            rest = jnp.where(lane < 3 * RIM, c, 0.0)
            return jnp.where(lane < RIM, a, jnp.where(lane < 2 * RIM, b, rest))

        first = join(block(0, 0, 0), block(1, 0, 1), block(0, 1, 2))
        last = join(block(0, 2, 0), block(1, 2, 1), block(1, 1, 2))
        return first, last

    west_cols, east_cols = pack(0), pack(n_cols - RIM)
    at_west = sub == 0
    for i in range(2):
        at = slice(i * halo, (i + 1) * halo)
        strips[0, at, :] = jnp.where(at_west, west_cols[i], east_cols[i])
        strips[1, at, :] = jnp.where(at_west, east_cols[i], west_cols[i])

    @pl.when(jnp.logical_not(has_up))
    def _():
        ext[:, 0:halo, :] = jnp.zeros((2, halo, LANES), jnp.float32)
        seams[:, 0:halo, :] = jnp.zeros((tiles + 1, halo, LANES), jnp.float32)

    @pl.when(jnp.logical_not(has_down))
    def _():
        ext[:, halo + n_rows : n_rows + 2 * halo, :] = jnp.zeros((2, halo, LANES), jnp.float32)
        seams[:, 3 * halo :, :] = jnp.zeros((tiles + 1, halo, LANES), jnp.float32)

    n_beside = has_up.astype(jnp.int32) + has_down.astype(jnp.int32)
    pl.semaphore_wait(barrier, tiles + n_beside * (tiles + 1))

    def strip_copy(which, slot, part, k, t, r):
        source = ((0, 2 * halo), (halo, halo), (0, halo))[part]
        target = (halo, 0, 3 * halo)[part]
        return pltpu.make_async_remote_copy(
            src_ref=strips.at[which, pl.ds(*source)],
            dst_ref=seams.at[slot, pl.ds(target, source[1])],
            send_sem=strip_send.at[part, k],
            recv_sem=strip_recv.at[part, slot],
            device_id=(grp, t, r, other),
            device_id_type=MESH,
        )

    def row_copy(part, r):
        source = (halo + n_rows - halo, halo)[part - 1]
        target = (0, halo + n_rows)[part - 1]
        return pltpu.make_async_remote_copy(
            src_ref=ext.at[:, pl.ds(source, halo)],
            dst_ref=ext.at[:, pl.ds(target, halo)],
            send_sem=row_send.at[part - 1],
            recv_sem=row_recv.at[part - 1],
            device_id=(grp, tile, r, sub),
            device_id_type=MESH,
        )

    def sends(act, part, r):
        for k in reversed(range(tiles)):
            act(strip_copy(0, tile, part, k, lax.rem(tile + k, tiles), r))
        act(strip_copy(1, tiles, part, tiles, tile, r))
        if part:
            act(row_copy(part, r))

    def all_sends(act):
        sends(act, 0, row)

        @pl.when(has_down)
        def _():
            sends(act, 1, row + 1)

        @pl.when(has_up)
        def _():
            sends(act, 2, row - 1)

    all_sends(lambda copy: copy.start())

    west_lane = LANES - EDGE - RIM
    place = lax.broadcasted_iota(jnp.int32, (LANES, LANES), 0)
    x_out = lax.broadcasted_iota(jnp.int32, (LANES, LANES), 1)

    def x_weights(x_in, keep):
        high, low = split(gaussian(x_in - x_out, keep & (x_out < n_cols)))
        above = jnp.concatenate([high, low], axis=1)
        below = jnp.concatenate([high, jnp.zeros_like(low)], axis=1)
        return jnp.concatenate([above, below], axis=0)

    x_own = x_weights(place, (place >= 1) & (place <= n_cols - 2))
    at_east = place < LANES // 2
    x_edge = x_weights(
        jnp.where(at_east, place + (n_cols - EDGE), place - (west_lane + RIM)),
        ((place >= 1) & (place <= RIM)) | ((place > west_lane) & (place <= west_lane + RIM)),
    )
    top = halo - R
    span = ceil_to(n_rows + 2 * R, 16)
    span_out = ceil_to(n_rows, 16)
    y_out = lax.broadcasted_iota(jnp.int32, (span_out, span), 0)
    y_in = lax.broadcasted_iota(jnp.int32, (span_out, span), 1) - R
    y_global = y_in + row * n_rows
    inside = (y_global >= 0) & (y_global < rows * n_rows) & (y_out < n_rows)
    y_high, y_low = split(gaussian(y_in - y_out, inside))

    west = jnp.int32(0)
    for i in range(tiles):
        west = jnp.where(face_ref[i] == tile, i, west)
    east_turn = turn_ref[tile]
    west_turn = turn_ref[west]
    west_turn = jnp.where(west_turn == 0, 0, 4 - west_turn)
    beside = jnp.where(at_west, west, face_ref[tile])
    turn = jnp.where(at_west, west_turn, east_turn)

    def choose(a, b):
        return jnp.where(turn == a, 1.0, jnp.where(turn == b, -1.0, 0.0)).astype(jnp.float32)

    cosine, sine = choose(0, 2), choose(1, 3)

    def arrived(part):
        for slot in range(tiles + 1):
            strip_copy(0, slot, part, 0, tile, row).wait_recv()

    def derive(field, c):
        centre = field[c, top : top + span, :]
        grad_x = DERIV_SCALE * (roll(centre, -1) - roll(centre, 1))
        grad_y = DERIV_SCALE * (field[c, top + 1 : top + 1 + span, :] - field[c, top - 1 : top - 1 + span, :])
        return centre, grad_x, grad_y

    def derived(field):
        u, u_x, u_y = derive(field, 0)
        v, v_x, v_y = derive(field, 1)
        return u, v, u_x, v_x, u_y, v_y, u * u_x + v * u_y, u * v_x + v * v_y

    def along(channel, weights):
        both = dot(jnp.concatenate(split(channel), axis=1), weights)
        return both[:, :LANES] + both[:, LANES:]

    @pl.when(has_up)
    def _():
        row_copy(1, row).wait_recv()

    @pl.when(has_down)
    def _():
        row_copy(2, row).wait_recv()

    for i, channel in enumerate(derived(ext)):
        inner_sum[i] = along(channel, x_own)

    n_ext = n_rows + 2 * halo
    lane = lax.broadcasted_iota(jnp.int32, (n_ext, LANES), 1)
    for c in range(2):
        own = ext[c, 0:n_ext, :]
        rest = jnp.where(lane >= LANES - EDGE, roll(own, -EDGE), 0.0)
        ring[c, 0:n_ext, :] = jnp.where(lane < EDGE, roll(own, EDGE - n_cols), rest)
        ring[c, n_ext:, :] = jnp.zeros((8, LANES), jnp.float32)

    arrived(0)

    @pl.when(has_up)
    def _():
        arrived(1)

    @pl.when(has_down)
    def _():
        arrived(2)

    def unpack(packed, shift):
        a, b, c, d = (packed[i * halo : (i + 1) * halo] for i in range(4))
        places = (((a, 0), (b, 0), (b, 2), (c, 0), (d, 0)), ((a, 1), (b, 1), (c, 2), (c, 1), (d, 1)))
        return [
            jnp.concatenate([roll(v, shift - p * RIM) for v, p in blocks], axis=0) for blocks in places
        ]

    seam, inner = seams[beside], seams[tiles]
    east_u, east_v = unpack(jnp.where(at_west, inner, seam), EDGE)
    west_u, west_v = unpack(jnp.where(at_west, seam, inner), west_lane)
    east_c = jnp.where(at_west, 1.0, cosine).astype(jnp.float32)
    east_s = jnp.where(at_west, 0.0, sine).astype(jnp.float32)
    west_c = jnp.where(at_west, cosine, 1.0).astype(jnp.float32)
    west_s = jnp.where(at_west, sine, 0.0).astype(jnp.float32)
    east_uv = (east_c * east_u - east_s * east_v, east_s * east_u + east_c * east_v)
    west_uv = (west_c * west_u - west_s * west_v, west_s * west_u + west_c * west_v)

    for c in range(2):
        here = jnp.where((lane >= EDGE) & (lane < EDGE + RIM), east_uv[c], ring[c, 0:n_ext, :])
        ring[c, 0:n_ext, :] = jnp.where((lane >= west_lane) & (lane < west_lane + RIM), west_uv[c], here)

    channels = derived(ring)

    def smoothed(i):
        sums = [inner_sum[j] + along(channels[j], x_edge) for j in (i, i + 1)]
        high, low = split(jnp.concatenate(sums, axis=1))
        both = dot(y_high, high) + (dot(y_high, low) + dot(y_low, high))
        return both[:n_rows, :n_cols], both[:n_rows, LANES : LANES + n_cols]

    smooth = []
    for i in range(0, 8, 2):
        smooth += smoothed(i)
    fine = (
        smooth[6] - (smooth[0] * smooth[2] + smooth[1] * smooth[4]),
        smooth[7] - (smooth[0] * smooth[3] + smooth[1] * smooth[5]),
    )

    n_out = n_rows // POOL
    m_out = n_cols // POOL
    col = lax.broadcasted_iota(jnp.int32, (LANES, m_out), 0)
    block_at = lax.broadcasted_iota(jnp.int32, (LANES, m_out), 1) * POOL
    mean = jnp.where((col >= block_at) & (col < block_at + POOL), 1.0 / POOL**2, 0.0)
    mean = mean.astype(jnp.bfloat16)
    for c in range(2):
        pooled[c] = jnp.zeros((n_rows, LANES), jnp.float32)
        pooled[c, :, 0:n_cols] = fine[c] * wet
        total = pooled[c, pl.ds(0, n_out, stride=POOL), :]
        for k in range(1, POOL):
            total = total + pooled[c, pl.ds(k, n_out, stride=POOL), :]
        high, low = split(total)
        out_ref[c] = dot(high, mean) + dot(low, mean)

    all_sends(lambda copy: copy.wait_send())


def on_device(velocity, wet_bits, east_face, seam_turn):
    _, n_rows, n_cols = velocity.shape
    tiles = lax.axis_size("tile")
    halo = ceil_to(RIM, 8)
    assert n_rows == 3 * halo and lax.axis_size("sub") == 2
    assert RIM <= n_cols <= LANES and 3 * RIM <= LANES
    n_ext = n_rows + 2 * halo
    f32 = jnp.float32
    return pl.pallas_call(
        kernel,
        out_shape=jax.ShapeDtypeStruct((2, n_rows // POOL, n_cols // POOL), f32),
        in_specs=[pl.BlockSpec(memory_space=pltpu.HBM)] * 4,
        out_specs=pl.BlockSpec(memory_space=pltpu.VMEM),
        scratch_shapes=[
            pltpu.SMEM(east_face.shape, jnp.int32),
            pltpu.SMEM(seam_turn.shape, jnp.int32),
            pltpu.VMEM(velocity.shape, f32),
            pltpu.VMEM(wet_bits.shape, jnp.int32),
            pltpu.VMEM((2, n_ext + 8, LANES), f32),
            pltpu.VMEM((2, 2 * halo, LANES), f32),
            pltpu.VMEM((tiles + 1, 4 * halo, LANES), f32),
            pltpu.VMEM((2, n_ext + 8, LANES), f32),
            pltpu.VMEM((8, ceil_to(n_rows + 2 * R, 16), LANES), f32),
            pltpu.VMEM((2, n_rows, LANES), f32),
            pltpu.SemaphoreType.DMA((4,)),
            pltpu.SemaphoreType.DMA((2,)),
            pltpu.SemaphoreType.DMA((2,)),
            pltpu.SemaphoreType.DMA((3, tiles + 1)),
            pltpu.SemaphoreType.DMA((3, tiles + 1)),
        ],
        compiler_params=pltpu.CompilerParams(
            collective_id=0, has_side_effects=True, vmem_limit_bytes=60 * 1024 * 1024
        ),
    )(east_face, seam_turn, velocity, wet_bits)


def solution(mesh):
    placed = (
        P(None, ("grp", "row"), ("tile", "sub")),
        P(("grp", "row"), ("tile", "sub")),
        P(),
        P(),
    )
    return jax.shard_map(
        on_device,
        mesh=mesh,
        in_specs=placed,
        out_specs=P(None, ("grp", "row"), ("tile", "sub")),
        check_vma=False,
    )
```

```python
import functools
import math

import jax
import jax.numpy as jnp
from jax import lax
from jax.experimental import pallas as pl
from jax.experimental.pallas import tpu as pltpu
from jax.sharding import PartitionSpec as P

R = 32
RIM = R + 1
LANES = 128
EDGE = 2
DERIV_SCALE = 8.0
POOL = 4
WORD_ROWS = 30
MESH = pl.DeviceIdType.MESH

WEIGHT_SUM = sum(math.exp(-0.5 * (k / R) ** 2) for k in range(-R, R + 1))


def ceil_to(value, step):
    return -(-value // step) * step


def gaussian(distance, keep):
    d = distance.astype(jnp.float32) * (1.0 / R)
    weight = jnp.exp(-0.5 * d * d) * (1.0 / WEIGHT_SUM)
    return jnp.where(keep & (jnp.abs(distance) <= R), weight, 0.0)


def split(value):
    high = value.astype(jnp.bfloat16)
    low = (value - high.astype(jnp.float32)).astype(jnp.bfloat16)
    return high, low


def dot(a, b):
    return jnp.dot(a, b, preferred_element_type=jnp.float32)


def roll(value, shift, axis=1):
    size = value.shape[axis]
    shift = shift % size
    return value if shift == 0 else pltpu.roll(value, shift, axis)


def kernel(
    face_hbm, turn_hbm, vel_hbm, bits_hbm, out_ref,
    face_ref, turn_ref, vel, bits, ext, strips, seams, ring, inner_field, inner_advect, pooled,
    load_sem, row_send, row_recv, strip_send, strip_recv,
):
    tiles, rows = lax.axis_size("tile"), lax.axis_size("row")
    grp, tile, row, sub = (lax.axis_index(a) for a in ("grp", "tile", "row", "sub"))
    n_rows, n_cols = vel.shape[1], vel.shape[2]
    halo = ceil_to(RIM, 8)
    has_up, has_down = row > 0, row < rows - 1
    other = 1 - sub

    loads = [
        pltpu.make_async_copy(vel_hbm, vel, load_sem.at[0]),
        pltpu.make_async_copy(bits_hbm, bits, load_sem.at[1]),
        pltpu.make_async_copy(face_hbm, face_ref, load_sem.at[2]),
        pltpu.make_async_copy(turn_hbm, turn_ref, load_sem.at[3]),
    ]
    for load in loads:
        load.start()

    barrier = pltpu.get_barrier_semaphore()

    def greet(t, r, s):
        pl.semaphore_signal(barrier, inc=1, device_id=(grp, t, r, s), device_id_type=MESH)

    for k in range(tiles):
        t = lax.rem(tile + k, tiles)
        greet(t, row, other)

        @pl.when(has_up)
        def _():
            greet(t, row - 1, other)

        @pl.when(has_down)
        def _():
            greet(t, row + 1, other)

    @pl.when(has_up)
    def _():
        greet(tile, row - 1, sub)

    @pl.when(has_down)
    def _():
        greet(tile, row + 1, sub)

    for load in loads:
        load.wait()

    row_id = lax.broadcasted_iota(jnp.int32, (n_rows, n_cols), 0)
    words = bits[...]
    word = jnp.broadcast_to(words[0:1], (n_rows, n_cols))
    bit = row_id
    for j in range(1, words.shape[0]):
        here = row_id >= j * WORD_ROWS
        word = jnp.where(here, words[j : j + 1], word)
        bit = jnp.where(here, row_id - j * WORD_ROWS, bit)
    wet = (jnp.right_shift(word, bit) & 1).astype(jnp.float32)
    for c in range(2):
        ext[c, halo : halo + n_rows, :] = jnp.zeros((n_rows, LANES), jnp.float32)
        ext[c, halo : halo + n_rows, 0:n_cols] = vel[c] * wet
        ext[c, n_rows + 2 * halo :, :] = jnp.zeros((8, LANES), jnp.float32)

    lane = lax.broadcasted_iota(jnp.int32, (halo, LANES), 1)

    def pack(start):
        def block(c, g, place):
            rows_at = halo + g * halo
            return roll(ext[c, rows_at : rows_at + halo, :], place * RIM - start)

        def join(a, b, c):
            rest = jnp.where(lane < 3 * RIM, c, 0.0)
            return jnp.where(lane < RIM, a, jnp.where(lane < 2 * RIM, b, rest))

        first = join(block(0, 0, 0), block(1, 0, 1), block(0, 1, 2))
        last = join(block(0, 2, 0), block(1, 2, 1), block(1, 1, 2))
        return first, last

    west_cols, east_cols = pack(0), pack(n_cols - RIM)
    at_west = sub == 0
    for i in range(2):
        at = slice(i * halo, (i + 1) * halo)
        strips[0, at, :] = jnp.where(at_west, west_cols[i], east_cols[i])
        strips[1, at, :] = jnp.where(at_west, east_cols[i], west_cols[i])

    @pl.when(jnp.logical_not(has_up))
    def _():
        ext[:, 0:halo, :] = jnp.zeros((2, halo, LANES), jnp.float32)
        seams[:, 0:halo, :] = jnp.zeros((tiles + 1, halo, LANES), jnp.float32)

    @pl.when(jnp.logical_not(has_down))
    def _():
        ext[:, halo + n_rows : n_rows + 2 * halo, :] = jnp.zeros((2, halo, LANES), jnp.float32)
        seams[:, 3 * halo :, :] = jnp.zeros((tiles + 1, halo, LANES), jnp.float32)

    n_beside = has_up.astype(jnp.int32) + has_down.astype(jnp.int32)
    pl.semaphore_wait(barrier, tiles + n_beside * (tiles + 1))

    def strip_copy(which, slot, part, k, t, r):
        source = ((0, 2 * halo), (halo, halo), (0, halo))[part]
        target = (halo, 0, 3 * halo)[part]
        return pltpu.make_async_remote_copy(
            src_ref=strips.at[which, pl.ds(*source)],
            dst_ref=seams.at[slot, pl.ds(target, source[1])],
            send_sem=strip_send.at[part, k],
            recv_sem=strip_recv.at[part, slot],
            device_id=(grp, t, r, other),
            device_id_type=MESH,
        )

    def row_copy(part, r):
        source = (halo + n_rows - halo, halo)[part - 1]
        target = (0, halo + n_rows)[part - 1]
        return pltpu.make_async_remote_copy(
            src_ref=ext.at[:, pl.ds(source, halo)],
            dst_ref=ext.at[:, pl.ds(target, halo)],
            send_sem=row_send.at[part - 1],
            recv_sem=row_recv.at[part - 1],
            device_id=(grp, tile, r, sub),
            device_id_type=MESH,
        )

    def sends(act, part, r):
        for k in reversed(range(tiles)):
            act(strip_copy(0, tile, part, k, lax.rem(tile + k, tiles), r))
        act(strip_copy(1, tiles, part, tiles, tile, r))
        if part:
            act(row_copy(part, r))

    def all_sends(act):
        sends(act, 0, row)

        @pl.when(has_down)
        def _():
            sends(act, 1, row + 1)

        @pl.when(has_up)
        def _():
            sends(act, 2, row - 1)

    all_sends(lambda copy: copy.start())

    west_lane = LANES - EDGE - RIM
    place = lax.broadcasted_iota(jnp.int32, (LANES, LANES), 0)
    x_out = lax.broadcasted_iota(jnp.int32, (LANES, LANES), 1)

    def field_weights(distance, keep, axis):
        weight = gaussian(distance, keep(0))
        slope = DERIV_SCALE * (gaussian(distance - 1, keep(-1)) - gaussian(distance + 1, keep(1)))
        return split(jnp.concatenate([weight, slope], axis=axis))

    def x_field_weights(x_in, keep):
        high, low = field_weights(x_in - x_out, lambda step: keep & (x_out < n_cols), 1)
        return jnp.concatenate([high, high], axis=0), low

    def x_advect_weights(x_in, keep):
        high, low = split(gaussian(x_in - x_out, keep & (x_out < n_cols)))
        above = jnp.concatenate([high, low], axis=1)
        below = jnp.concatenate([high, jnp.zeros_like(low)], axis=1)
        return jnp.concatenate([above, below], axis=0)

    x_own_field = x_field_weights(place, place < n_cols)
    x_own_advect = x_advect_weights(place, (place >= 1) & (place <= n_cols - 2))
    at_east = place < LANES // 2
    x_edge = jnp.where(at_east, place + (n_cols - EDGE), place - (west_lane + RIM))
    x_edge_field = x_field_weights(
        x_edge, ((place >= EDGE) & (place <= RIM + 1)) | ((place >= west_lane) & (place < west_lane + RIM))
    )
    x_edge_advect = x_advect_weights(
        x_edge, ((place >= 1) & (place <= RIM)) | ((place > west_lane) & (place <= west_lane + RIM))
    )
    top = halo - R
    span = ceil_to(n_rows + 2 * R, 16)
    n_ext = n_rows + 2 * halo
    n_field = ext.shape[1]
    span_out = ceil_to(n_rows, 16)

    def y_places(length, start):
        y_out = lax.broadcasted_iota(jnp.int32, (span_out, length), 0)
        y_in = lax.broadcasted_iota(jnp.int32, (span_out, length), 1) + start

        def keep(step):
            y_global = y_in + step + row * n_rows
            return (y_global >= 0) & (y_global < rows * n_rows) & (y_out < n_rows)

        return y_in - y_out, keep

    y_field_high, y_field_low = field_weights(*y_places(n_field, -halo), 0)
    distance, keep = y_places(span, -R)
    y_high, y_low = split(gaussian(distance, keep(0)))

    west = jnp.int32(0)
    for i in range(tiles):
        west = jnp.where(face_ref[i] == tile, i, west)
    east_turn = turn_ref[tile]
    west_turn = turn_ref[west]
    west_turn = jnp.where(west_turn == 0, 0, 4 - west_turn)
    beside = jnp.where(at_west, west, face_ref[tile])
    turn = jnp.where(at_west, west_turn, east_turn)

    def choose(a, b):
        return jnp.where(turn == a, 1.0, jnp.where(turn == b, -1.0, 0.0)).astype(jnp.float32)

    cosine, sine = choose(0, 2), choose(1, 3)

    def arrived(part):
        for slot in range(tiles + 1):
            strip_copy(0, slot, part, 0, tile, row).wait_recv()

    def derive(field, c):
        centre = field[c, top : top + span, :]
        grad_x = DERIV_SCALE * (roll(centre, -1) - roll(centre, 1))
        grad_y = DERIV_SCALE * (field[c, top + 1 : top + 1 + span, :] - field[c, top - 1 : top - 1 + span, :])
        return centre, grad_x, grad_y

    def advected(field):
        u, u_x, u_y = derive(field, 0)
        v, v_x, v_y = derive(field, 1)
        return u * u_x + v * u_y, u * v_x + v * v_y

    def along_field(value, weights):
        high, low = split(value)
        return dot(jnp.concatenate([high, low], axis=1), weights[0]) + dot(high, weights[1])

    def along_advect(value, weights):
        both = dot(jnp.concatenate(split(value), axis=1), weights)
        return both[:, :LANES] + both[:, LANES:]

    @pl.when(has_up)
    def _():
        row_copy(1, row).wait_recv()

    @pl.when(has_down)
    def _():
        row_copy(2, row).wait_recv()

    for c, advect in enumerate(advected(ext)):
        inner_field[c] = along_field(ext[c], x_own_field)
        inner_advect[c] = along_advect(advect, x_own_advect)

    lane = lax.broadcasted_iota(jnp.int32, (n_ext, LANES), 1)
    for c in range(2):
        own = ext[c, 0:n_ext, :]
        rest = jnp.where(lane >= LANES - EDGE, roll(own, -EDGE), 0.0)
        ring[c, 0:n_ext, :] = jnp.where(lane < EDGE, roll(own, EDGE - n_cols), rest)
        ring[c, n_ext:, :] = jnp.zeros((8, LANES), jnp.float32)

    arrived(0)

    @pl.when(has_up)
    def _():
        arrived(1)

    @pl.when(has_down)
    def _():
        arrived(2)

    def unpack(packed, shift):
        a, b, c, d = (packed[i * halo : (i + 1) * halo] for i in range(4))
        places = (((a, 0), (b, 0), (b, 2), (c, 0), (d, 0)), ((a, 1), (b, 1), (c, 2), (c, 1), (d, 1)))
        return [
            jnp.concatenate([roll(v, shift - p * RIM) for v, p in blocks], axis=0) for blocks in places
        ]

    seam, inner = seams[beside], seams[tiles]
    east_u, east_v = unpack(jnp.where(at_west, inner, seam), EDGE)
    west_u, west_v = unpack(jnp.where(at_west, seam, inner), west_lane)
    east_c = jnp.where(at_west, 1.0, cosine).astype(jnp.float32)
    east_s = jnp.where(at_west, 0.0, sine).astype(jnp.float32)
    west_c = jnp.where(at_west, cosine, 1.0).astype(jnp.float32)
    west_s = jnp.where(at_west, sine, 0.0).astype(jnp.float32)
    east_uv = (east_c * east_u - east_s * east_v, east_s * east_u + east_c * east_v)
    west_uv = (west_c * west_u - west_s * west_v, west_s * west_u + west_c * west_v)

    for c in range(2):
        here = jnp.where((lane >= EDGE) & (lane < EDGE + RIM), east_uv[c], ring[c, 0:n_ext, :])
        ring[c, 0:n_ext, :] = jnp.where((lane >= west_lane) & (lane < west_lane + RIM), west_uv[c], here)

    def smoothed(value, high, low):
        value_high, value_low = split(value)
        return dot(high, value_high) + (dot(high, value_low) + dot(low, value_high))

    smooth = []
    for c in range(2):
        field = inner_field[c] + along_field(ring[c], x_edge_field)
        both = smoothed(field, y_field_high, y_field_low)
        smooth.append((both[:span_out, :LANES], both[:span_out, LANES:], both[span_out:, :LANES]))
    advect = [inner_advect[c] + along_advect(a, x_edge_advect) for c, a in enumerate(advected(ring))]
    advect = smoothed(jnp.concatenate(advect, axis=1), y_high, y_low)
    (u, u_x, u_y), (v, v_x, v_y) = smooth
    fine = (
        advect[:, :LANES] - (u * u_x + v * u_y),
        advect[:, LANES:] - (u * v_x + v * v_y),
    )

    n_out = n_rows // POOL
    m_out = n_cols // POOL
    col = lax.broadcasted_iota(jnp.int32, (LANES, m_out), 0)
    block_at = lax.broadcasted_iota(jnp.int32, (LANES, m_out), 1) * POOL
    mean = jnp.where((col >= block_at) & (col < block_at + POOL), 1.0 / POOL**2, 0.0)
    mean = mean.astype(jnp.bfloat16)
    for c in range(2):
        pooled[c] = jnp.zeros((n_rows, LANES), jnp.float32)
        pooled[c, :, 0:n_cols] = fine[c][:n_rows, :n_cols] * wet
        total = pooled[c, pl.ds(0, n_out, stride=POOL), :]
        for k in range(1, POOL):
            total = total + pooled[c, pl.ds(k, n_out, stride=POOL), :]
        high, low = split(total)
        out_ref[c] = dot(high, mean) + dot(low, mean)

    all_sends(lambda copy: copy.wait_send())


def on_device(velocity, wet_bits, east_face, seam_turn):
    _, n_rows, n_cols = velocity.shape
    tiles = lax.axis_size("tile")
    halo = ceil_to(RIM, 8)
    assert n_rows == 3 * halo and lax.axis_size("sub") == 2
    assert RIM <= n_cols <= LANES and 3 * RIM <= LANES
    n_ext = n_rows + 2 * halo
    f32 = jnp.float32
    return pl.pallas_call(
        kernel,
        out_shape=pltpu.VMEM((2, n_rows // POOL, n_cols // POOL), f32),
        in_specs=[pl.BlockSpec(memory_space=pltpu.HBM)] * 4,
        out_specs=pl.BlockSpec(memory_space=pltpu.VMEM),
        scratch_shapes=[
            pltpu.SMEM(east_face.shape, jnp.int32),
            pltpu.SMEM(seam_turn.shape, jnp.int32),
            pltpu.VMEM(velocity.shape, f32),
            pltpu.VMEM(wet_bits.shape, jnp.int32),
            pltpu.VMEM((2, n_ext + 8, LANES), f32),
            pltpu.VMEM((2, 2 * halo, LANES), f32),
            pltpu.VMEM((tiles + 1, 4 * halo, LANES), f32),
            pltpu.VMEM((2, n_ext + 8, LANES), f32),
            pltpu.VMEM((2, n_ext + 8, 2 * LANES), f32),
            pltpu.VMEM((2, ceil_to(n_rows + 2 * R, 16), LANES), f32),
            pltpu.VMEM((2, n_rows, LANES), f32),
            pltpu.SemaphoreType.DMA((4,)),
            pltpu.SemaphoreType.DMA((2,)),
            pltpu.SemaphoreType.DMA((2,)),
            pltpu.SemaphoreType.DMA((3, tiles + 1)),
            pltpu.SemaphoreType.DMA((3, tiles + 1)),
        ],
        compiler_params=pltpu.CompilerParams(
            collective_id=0, has_side_effects=True, vmem_limit_bytes=60 * 1024 * 1024
        ),
    )(east_face, seam_turn, velocity, wet_bits)


def solution(mesh):
    placed = (
        P(None, ("grp", "row"), ("tile", "sub")),
        P(("grp", "row"), ("tile", "sub")),
        P(),
        P(),
    )
    return jax.shard_map(
        on_device,
        mesh=mesh,
        in_specs=placed,
        out_specs=P(None, ("grp", "row"), ("tile", "sub")),
        check_vma=False,
    )
```

```python
import functools
import math

import jax
import jax.numpy as jnp
from jax import lax
from jax.experimental import pallas as pl
from jax.experimental.pallas import tpu as pltpu
from jax.sharding import PartitionSpec as P

R = 32
RIM = R + 1
LANES = 128
EDGE = 2
DERIV_SCALE = 8.0
POOL = 4
WORD_ROWS = 30
MESH = pl.DeviceIdType.MESH

WEIGHT_SUM = sum(math.exp(-0.5 * (k / R) ** 2) for k in range(-R, R + 1))


def ceil_to(value, step):
    return -(-value // step) * step


def gaussian(distance, keep):
    d = distance.astype(jnp.float32) * (1.0 / R)
    weight = jnp.exp(-0.5 * d * d) * (1.0 / WEIGHT_SUM)
    return jnp.where(keep & (jnp.abs(distance) <= R), weight, 0.0)


def split(value):
    high = value.astype(jnp.bfloat16)
    low = (value - high.astype(jnp.float32)).astype(jnp.bfloat16)
    return high, low


def dot(a, b):
    return jnp.dot(a, b, preferred_element_type=jnp.float32)


def roll(value, shift, axis=1):
    size = value.shape[axis]
    shift = shift % size
    return value if shift == 0 else pltpu.roll(value, shift, axis)


def kernel(
    face_hbm, turn_hbm, vel_hbm, bits_hbm, out_ref,
    face_ref, turn_ref, vel, bits, ext, strips, pieces, picked, seam, beside,
    ring, inner_field, inner_advect, pooled,
    load_sem, row_send, row_recv, beside_send, beside_recv,
    piece_send, piece_recv, seam_send, seam_recv, rim_send, rim_recv,
):
    tiles, rows = lax.axis_size("tile"), lax.axis_size("row")
    grp, tile, row, sub = (lax.axis_index(a) for a in ("grp", "tile", "row", "sub"))
    n_rows, n_cols = vel.shape[1], vel.shape[2]
    halo = ceil_to(RIM, 8)
    piece = pieces.shape[1]
    part_rows = tiles // 2 * piece
    has_up, has_down = row > 0, row < rows - 1
    other = 1 - sub

    loads = [
        pltpu.make_async_copy(vel_hbm, vel, load_sem.at[0]),
        pltpu.make_async_copy(bits_hbm, bits, load_sem.at[1]),
        pltpu.make_async_copy(face_hbm, face_ref, load_sem.at[2]),
        pltpu.make_async_copy(turn_hbm, turn_ref, load_sem.at[3]),
    ]
    for load in loads:
        load.start()

    barrier = pltpu.get_barrier_semaphore()

    def greet(t, r, s):
        pl.semaphore_signal(barrier, inc=1, device_id=(grp, t, r, s), device_id_type=MESH)

    for k in range(tiles):
        t = lax.rem(tile + k, tiles)
        greet(t, row, other)
        if k:
            greet(t, row, sub)

        @pl.when(has_up)
        def _():
            greet(t, row - 1, sub)

        @pl.when(has_down)
        def _():
            greet(t, row + 1, sub)

    @pl.when(has_up)
    def _():
        greet(tile, row - 1, other)

    @pl.when(has_down)
    def _():
        greet(tile, row + 1, other)

    for load in loads:
        load.wait()

    row_id = lax.broadcasted_iota(jnp.int32, (n_rows, n_cols), 0)
    words = bits[...]
    word = jnp.broadcast_to(words[0:1], (n_rows, n_cols))
    bit = row_id
    for j in range(1, words.shape[0]):
        here = row_id >= j * WORD_ROWS
        word = jnp.where(here, words[j : j + 1], word)
        bit = jnp.where(here, row_id - j * WORD_ROWS, bit)
    wet = (jnp.right_shift(word, bit) & 1).astype(jnp.float32)
    for c in range(2):
        ext[c, halo : halo + n_rows, :] = jnp.zeros((n_rows, LANES), jnp.float32)
        ext[c, halo : halo + n_rows, 0:n_cols] = vel[c] * wet
        ext[c, n_rows + 2 * halo :, :] = jnp.zeros((8, LANES), jnp.float32)

    lane = lax.broadcasted_iota(jnp.int32, (halo, LANES), 1)

    def pack(start):
        def block(c, g, place):
            rows_at = halo + g * halo
            return roll(ext[c, rows_at : rows_at + halo, :], place * RIM - start)

        def join(a, b, c):
            rest = jnp.where(lane < 3 * RIM, c, 0.0)
            return jnp.where(lane < RIM, a, jnp.where(lane < 2 * RIM, b, rest))

        first = join(block(0, 0, 0), block(1, 0, 1), block(0, 1, 2))
        last = join(block(0, 2, 0), block(1, 2, 1), block(1, 1, 2))
        return first, last

    west_cols, east_cols = pack(0), pack(n_cols - RIM)
    at_west = sub == 0
    for i in range(2):
        at = slice(i * part_rows, i * part_rows + halo)
        strips[0, at, :] = jnp.where(at_west, west_cols[i], east_cols[i])
        strips[1, at, :] = jnp.where(at_west, east_cols[i], west_cols[i])

    @pl.when(jnp.logical_not(has_up))
    def _():
        ext[:, 0:halo, :] = jnp.zeros((2, halo, LANES), jnp.float32)
        seam[0:halo, :] = jnp.zeros((halo, LANES), jnp.float32)
        beside[0:halo, :] = jnp.zeros((halo, LANES), jnp.float32)

    @pl.when(jnp.logical_not(has_down))
    def _():
        ext[:, halo + n_rows : n_rows + 2 * halo, :] = jnp.zeros((2, halo, LANES), jnp.float32)
        seam[3 * part_rows : 3 * part_rows + halo, :] = jnp.zeros((halo, LANES), jnp.float32)
        beside[3 * part_rows : 3 * part_rows + halo, :] = jnp.zeros((halo, LANES), jnp.float32)

    n_beside = has_up.astype(jnp.int32) + has_down.astype(jnp.int32)
    pl.semaphore_wait(barrier, 2 * tiles - 1 + n_beside * (tiles + 1))

    def piece_rows(group, q):
        return pl.ds(pl.multiple_of(group * part_rows + q // 2 * piece, 8), piece)

    def piece_copy(slot, k, q):
        return pltpu.make_async_remote_copy(
            src_ref=strips.at[0, piece_rows(lax.rem(q, 2), q)],
            dst_ref=pieces.at[slot],
            send_sem=piece_send.at[k],
            recv_sem=piece_recv.at[slot],
            device_id=(grp, q, row, other),
            device_id_type=MESH,
        )

    def seam_copy(q, k, t):
        return pltpu.make_async_remote_copy(
            src_ref=picked.at[k],
            dst_ref=seam.at[piece_rows(1 + lax.rem(q, 2), q)],
            send_sem=seam_send.at[k],
            recv_sem=seam_recv.at[q],
            device_id=(grp, t, row, sub),
            device_id_type=MESH,
        )

    def rim_copy(q, group, k, t, r):
        return pltpu.make_async_remote_copy(
            src_ref=picked.at[k],
            dst_ref=seam.at[piece_rows(group, q)],
            send_sem=rim_send.at[k],
            recv_sem=rim_recv.at[q],
            device_id=(grp, t, r, sub),
            device_id_type=MESH,
        )

    def beside_copy(part, r):
        source = ((0, 2 * part_rows), (part_rows, halo), (0, halo))[part]
        target = (part_rows, 0, 3 * part_rows)[part]
        return pltpu.make_async_remote_copy(
            src_ref=strips.at[1, pl.ds(*source)],
            dst_ref=beside.at[pl.ds(target, source[1])],
            send_sem=beside_send.at[part],
            recv_sem=beside_recv.at[part],
            device_id=(grp, tile, r, other),
            device_id_type=MESH,
        )

    def row_copy(part, r):
        source = (halo + n_rows - halo, halo)[part - 1]
        target = (0, halo + n_rows)[part - 1]
        return pltpu.make_async_remote_copy(
            src_ref=ext.at[:, pl.ds(source, halo)],
            dst_ref=ext.at[:, pl.ds(target, halo)],
            send_sem=row_send.at[part - 1],
            recv_sem=row_recv.at[part - 1],
            device_id=(grp, tile, r, sub),
            device_id_type=MESH,
        )

    def first_sends(act):
        for k in reversed(range(tiles)):
            act(piece_copy(tile, k, lax.rem(tile + k, tiles)))

        @pl.when(has_down)
        def _():
            act(row_copy(1, row + 1))
            act(beside_copy(1, row + 1))

        @pl.when(has_up)
        def _():
            act(row_copy(2, row - 1))
            act(beside_copy(2, row - 1))

        act(beside_copy(0, row))

    odd = lax.rem(tile, 2) == 1
    rim_row = jnp.where(odd, row + 1, row - 1)
    rim_group = jnp.where(odd, 0, 3)
    has_rim = (rim_row >= 0) & (rim_row < rows)

    def second_sends(act):
        for k in reversed(range(1, tiles)):
            act(seam_copy(tile, k, lax.rem(tile + k, tiles)))

        @pl.when(has_rim)
        def _():
            for k in reversed(range(tiles)):
                act(rim_copy(tile, rim_group, k, lax.rem(tile + k, tiles), rim_row))

    first_sends(lambda copy: copy.start())

    west_lane = LANES - EDGE - RIM
    place = lax.broadcasted_iota(jnp.int32, (LANES, LANES), 0)
    x_out = lax.broadcasted_iota(jnp.int32, (LANES, LANES), 1)

    def field_weights(distance, keep, axis):
        weight = gaussian(distance, keep(0))
        slope = DERIV_SCALE * (gaussian(distance - 1, keep(-1)) - gaussian(distance + 1, keep(1)))
        return split(jnp.concatenate([weight, slope], axis=axis))

    def x_field_weights(x_in, keep):
        high, low = field_weights(x_in - x_out, lambda step: keep & (x_out < n_cols), 1)
        return jnp.concatenate([high, high], axis=0), low

    def x_advect_weights(x_in, keep):
        high, low = split(gaussian(x_in - x_out, keep & (x_out < n_cols)))
        above = jnp.concatenate([high, low], axis=1)
        below = jnp.concatenate([high, jnp.zeros_like(low)], axis=1)
        return jnp.concatenate([above, below], axis=0)

    x_own_field = x_field_weights(place, place < n_cols)
    x_own_advect = x_advect_weights(place, (place >= 1) & (place <= n_cols - 2))
    at_east = place < LANES // 2
    x_edge = jnp.where(at_east, place + (n_cols - EDGE), place - (west_lane + RIM))
    x_edge_field = x_field_weights(
        x_edge, ((place >= EDGE) & (place <= RIM + 1)) | ((place >= west_lane) & (place < west_lane + RIM))
    )
    x_edge_advect = x_advect_weights(
        x_edge, ((place >= 1) & (place <= RIM)) | ((place > west_lane) & (place <= west_lane + RIM))
    )
    top = halo - R
    span = ceil_to(n_rows + 2 * R, 16)
    n_ext = n_rows + 2 * halo
    n_field = ext.shape[1]
    span_out = ceil_to(n_rows, 16)

    def y_places(length, start):
        y_out = lax.broadcasted_iota(jnp.int32, (span_out, length), 0)
        y_in = lax.broadcasted_iota(jnp.int32, (span_out, length), 1) + start

        def keep(step):
            y_global = y_in + step + row * n_rows
            return (y_global >= 0) & (y_global < rows * n_rows) & (y_out < n_rows)

        return y_in - y_out, keep

    y_field_high, y_field_low = field_weights(*y_places(n_field, -halo), 0)
    distance, keep = y_places(span, -R)
    y_high, y_low = split(gaussian(distance, keep(0)))

    def west_of(t):
        west = jnp.int32(0)
        for i in range(tiles):
            west = jnp.where(face_ref[i] == t, i, west)
        return west

    west = west_of(tile)
    east_turn = turn_ref[tile]
    west_turn = turn_ref[west]
    west_turn = jnp.where(west_turn == 0, 0, 4 - west_turn)
    turn = jnp.where(at_west, west_turn, east_turn)

    def choose(a, b):
        return jnp.where(turn == a, 1.0, jnp.where(turn == b, -1.0, 0.0)).astype(jnp.float32)

    cosine, sine = choose(0, 2), choose(1, 3)

    for slot in range(tiles):
        piece_copy(slot, 0, tile).wait_recv()
    for k in range(tiles):
        t = lax.rem(tile + k, tiles)
        picked[k] = pieces[jnp.where(at_west, west_of(t), face_ref[t])]
    second_sends(lambda copy: copy.start())
    seam[piece_rows(1 + lax.rem(tile, 2), tile), :] = picked[0]

    def derive(field, c):
        centre = field[c, top : top + span, :]
        grad_x = DERIV_SCALE * (roll(centre, -1) - roll(centre, 1))
        grad_y = DERIV_SCALE * (field[c, top + 1 : top + 1 + span, :] - field[c, top - 1 : top - 1 + span, :])
        return centre, grad_x, grad_y

    def advected(field):
        u, u_x, u_y = derive(field, 0)
        v, v_x, v_y = derive(field, 1)
        return u * u_x + v * u_y, u * v_x + v * v_y

    def along_field(value, weights):
        high, low = split(value)
        return dot(jnp.concatenate([high, low], axis=1), weights[0]) + dot(high, weights[1])

    def along_advect(value, weights):
        both = dot(jnp.concatenate(split(value), axis=1), weights)
        return both[:, :LANES] + both[:, LANES:]

    @pl.when(has_up)
    def _():
        row_copy(1, row).wait_recv()

    @pl.when(has_down)
    def _():
        row_copy(2, row).wait_recv()

    for c, advect in enumerate(advected(ext)):
        inner_field[c] = along_field(ext[c], x_own_field)
        inner_advect[c] = along_advect(advect, x_own_advect)

    lane = lax.broadcasted_iota(jnp.int32, (n_ext, LANES), 1)
    for c in range(2):
        own = ext[c, 0:n_ext, :]
        rest = jnp.where(lane >= LANES - EDGE, roll(own, -EDGE), 0.0)
        ring[c, 0:n_ext, :] = jnp.where(lane < EDGE, roll(own, EDGE - n_cols), rest)
        ring[c, n_ext:, :] = jnp.zeros((8, LANES), jnp.float32)

    beside_copy(0, row).wait_recv()
    for k in range(1, tiles):
        seam_copy(lax.rem(tile + k, tiles), 0, tile).wait_recv()

    @pl.when(has_up)
    def _():
        beside_copy(1, row).wait_recv()
        for q in range(1, tiles, 2):
            rim_copy(q, 0, 0, tile, row).wait_recv()

    @pl.when(has_down)
    def _():
        beside_copy(2, row).wait_recv()
        for q in range(0, tiles, 2):
            rim_copy(q, 3, 0, tile, row).wait_recv()

    def unpack(packed, shift):
        a, b, c, d = (packed[i * part_rows : i * part_rows + halo] for i in range(4))
        places = (((a, 0), (b, 0), (b, 2), (c, 0), (d, 0)), ((a, 1), (b, 1), (c, 2), (c, 1), (d, 1)))
        return [
            jnp.concatenate([roll(v, shift - p * RIM) for v, p in blocks], axis=0) for blocks in places
        ]

    outer, inner = seam[...], beside[...]
    east_u, east_v = unpack(jnp.where(at_west, inner, outer), EDGE)
    west_u, west_v = unpack(jnp.where(at_west, outer, inner), west_lane)
    east_c = jnp.where(at_west, 1.0, cosine).astype(jnp.float32)
    east_s = jnp.where(at_west, 0.0, sine).astype(jnp.float32)
    west_c = jnp.where(at_west, cosine, 1.0).astype(jnp.float32)
    west_s = jnp.where(at_west, sine, 0.0).astype(jnp.float32)
    east_uv = (east_c * east_u - east_s * east_v, east_s * east_u + east_c * east_v)
    west_uv = (west_c * west_u - west_s * west_v, west_s * west_u + west_c * west_v)

    for c in range(2):
        here = jnp.where((lane >= EDGE) & (lane < EDGE + RIM), east_uv[c], ring[c, 0:n_ext, :])
        ring[c, 0:n_ext, :] = jnp.where((lane >= west_lane) & (lane < west_lane + RIM), west_uv[c], here)

    def smoothed(value, high, low):
        value_high, value_low = split(value)
        return dot(high, value_high) + (dot(high, value_low) + dot(low, value_high))

    smooth = []
    for c in range(2):
        field = inner_field[c] + along_field(ring[c], x_edge_field)
        both = smoothed(field, y_field_high, y_field_low)
        smooth.append((both[:span_out, :LANES], both[:span_out, LANES:], both[span_out:, :LANES]))
    advect = [inner_advect[c] + along_advect(a, x_edge_advect) for c, a in enumerate(advected(ring))]
    advect = smoothed(jnp.concatenate(advect, axis=1), y_high, y_low)
    (u, u_x, u_y), (v, v_x, v_y) = smooth
    fine = (
        advect[:, :LANES] - (u * u_x + v * u_y),
        advect[:, LANES:] - (u * v_x + v * v_y),
    )

    n_out = n_rows // POOL
    m_out = n_cols // POOL
    col = lax.broadcasted_iota(jnp.int32, (LANES, m_out), 0)
    block_at = lax.broadcasted_iota(jnp.int32, (LANES, m_out), 1) * POOL
    mean = jnp.where((col >= block_at) & (col < block_at + POOL), 1.0 / POOL**2, 0.0)
    mean = mean.astype(jnp.bfloat16)
    for c in range(2):
        pooled[c] = jnp.zeros((n_rows, LANES), jnp.float32)
        pooled[c, :, 0:n_cols] = fine[c][:n_rows, :n_cols] * wet
        total = pooled[c, pl.ds(0, n_out, stride=POOL), :]
        for k in range(1, POOL):
            total = total + pooled[c, pl.ds(k, n_out, stride=POOL), :]
        high, low = split(total)
        out_ref[c] = dot(high, mean) + dot(low, mean)

    first_sends(lambda copy: copy.wait_send())
    second_sends(lambda copy: copy.wait_send())


def on_device(velocity, wet_bits, east_face, seam_turn):
    _, n_rows, n_cols = velocity.shape
    tiles = lax.axis_size("tile")
    halo = ceil_to(RIM, 8)
    assert n_rows == 3 * halo and lax.axis_size("sub") == 2 and tiles % 2 == 0
    assert RIM <= n_cols <= LANES and 3 * RIM <= LANES
    n_ext = n_rows + 2 * halo
    piece = ceil_to(-(-halo // (tiles // 2)), 8)
    part_rows = tiles // 2 * piece
    f32 = jnp.float32
    return pl.pallas_call(
        kernel,
        out_shape=pltpu.VMEM((2, n_rows // POOL, n_cols // POOL), f32),
        in_specs=[pl.BlockSpec(memory_space=pltpu.HBM)] * 4,
        out_specs=pl.BlockSpec(memory_space=pltpu.VMEM),
        scratch_shapes=[
            pltpu.SMEM(east_face.shape, jnp.int32),
            pltpu.SMEM(seam_turn.shape, jnp.int32),
            pltpu.VMEM(velocity.shape, f32),
            pltpu.VMEM(wet_bits.shape, jnp.int32),
            pltpu.VMEM((2, n_ext + 8, LANES), f32),
            pltpu.VMEM((2, 2 * part_rows, LANES), f32),
            pltpu.VMEM((tiles, piece, LANES), f32),
            pltpu.VMEM((tiles, piece, LANES), f32),
            pltpu.VMEM((4 * part_rows, LANES), f32),
            pltpu.VMEM((4 * part_rows, LANES), f32),
            pltpu.VMEM((2, n_ext + 8, LANES), f32),
            pltpu.VMEM((2, n_ext + 8, 2 * LANES), f32),
            pltpu.VMEM((2, ceil_to(n_rows + 2 * R, 16), LANES), f32),
            pltpu.VMEM((2, n_rows, LANES), f32),
            pltpu.SemaphoreType.DMA((4,)),
            pltpu.SemaphoreType.DMA((2,)),
            pltpu.SemaphoreType.DMA((2,)),
            pltpu.SemaphoreType.DMA((3,)),
            pltpu.SemaphoreType.DMA((3,)),
        ]
        + [pltpu.SemaphoreType.DMA((tiles,))] * 6,
        compiler_params=pltpu.CompilerParams(
            collective_id=0, has_side_effects=True, vmem_limit_bytes=60 * 1024 * 1024
        ),
    )(east_face, seam_turn, velocity, wet_bits)


def solution(mesh):
    placed = (
        P(None, ("grp", "row"), ("tile", "sub")),
        P(("grp", "row"), ("tile", "sub")),
        P(),
        P(),
    )
    return jax.shard_map(
        on_device,
        mesh=mesh,
        in_specs=placed,
        out_specs=P(None, ("grp", "row"), ("tile", "sub")),
        check_vma=False,
    )
```

```python
import functools
import math

import jax
import jax.numpy as jnp
from jax import lax
from jax.experimental import pallas as pl
from jax.experimental.pallas import tpu as pltpu
from jax.sharding import PartitionSpec as P

R = 32
RIM = R + 1
LANES = 128
EDGE = 2
DERIV_SCALE = 8.0
POOL = 4
WORD_ROWS = 30
MESH = pl.DeviceIdType.MESH

WEIGHT_SUM = sum(math.exp(-0.5 * (k / R) ** 2) for k in range(-R, R + 1))


def ceil_to(value, step):
    return -(-value // step) * step


def gaussian(distance, keep):
    d = distance.astype(jnp.float32) * (1.0 / R)
    weight = jnp.exp(-0.5 * d * d) * (1.0 / WEIGHT_SUM)
    return jnp.where(keep & (jnp.abs(distance) <= R), weight, 0.0)


def split(value):
    high = value.astype(jnp.bfloat16)
    low = (value - high.astype(jnp.float32)).astype(jnp.bfloat16)
    return high, low


def dot(a, b):
    return jnp.dot(a, b, preferred_element_type=jnp.float32)


def roll(value, shift, axis=1):
    size = value.shape[axis]
    shift = shift % size
    return value if shift == 0 else pltpu.roll(value, shift, axis)


def kernel(
    face_hbm, turn_hbm, vel_hbm, bits_hbm, out_ref,
    face_ref, turn_ref, vel, bits, ext, strips, passing, seam, beside,
    ring, inner_field, inner_advect, pooled,
    load_sem, row_send, row_recv, beside_send, beside_recv,
    right_send, left_send, across_send, pass_recv, rim_send, rim_recv,
):
    tiles, rows = lax.axis_size("tile"), lax.axis_size("row")
    grp, tile, row, sub = (lax.axis_index(a) for a in ("grp", "tile", "row", "sub"))
    n_rows, n_cols = vel.shape[1], vel.shape[2]
    halo = ceil_to(RIM, 8)
    has_up, has_down = row > 0, row < rows - 1
    has_left, has_right = tile > 0, tile < tiles - 1
    other = 1 - sub

    loads = [
        pltpu.make_async_copy(vel_hbm, vel, load_sem.at[0]),
        pltpu.make_async_copy(bits_hbm, bits, load_sem.at[1]),
        pltpu.make_async_copy(face_hbm, face_ref, load_sem.at[2]),
        pltpu.make_async_copy(turn_hbm, turn_ref, load_sem.at[3]),
    ]
    for load in loads:
        load.start()

    barrier = pltpu.get_barrier_semaphore()

    def greet(t, r, s):
        pl.semaphore_signal(barrier, inc=1, device_id=(grp, t, r, s), device_id_type=MESH)

    greet(tile, row, other)
    for there, t in ((has_left, tile - 1), (has_right, tile + 1)):

        @pl.when(there)
        def _():
            greet(t, row, other)
            greet(t, row, sub)

    for there, r in ((has_up, row - 1), (has_down, row + 1)):

        @pl.when(there)
        def _():
            greet(tile, r, other)
            greet(tile, r, sub)

    west_lane = LANES - EDGE - RIM
    place = lax.broadcasted_iota(jnp.int32, (LANES, LANES), 0)
    x_out = lax.broadcasted_iota(jnp.int32, (LANES, LANES), 1)

    def field_weights(distance, keep, axis):
        weight = gaussian(distance, keep(0))
        slope = DERIV_SCALE * (gaussian(distance - 1, keep(-1)) - gaussian(distance + 1, keep(1)))
        return split(jnp.concatenate([weight, slope], axis=axis))

    def x_field_weights(x_in, keep):
        high, low = field_weights(x_in - x_out, lambda step: keep & (x_out < n_cols), 1)
        return jnp.concatenate([high, high], axis=0), low

    def x_advect_weights(x_in, keep):
        high, low = split(gaussian(x_in - x_out, keep & (x_out < n_cols)))
        above = jnp.concatenate([high, low], axis=1)
        below = jnp.concatenate([high, jnp.zeros_like(low)], axis=1)
        return jnp.concatenate([above, below], axis=0)

    x_own_field = x_field_weights(place, place < n_cols)
    x_own_advect = x_advect_weights(place, (place >= 1) & (place <= n_cols - 2))
    at_east = place < LANES // 2
    x_edge = jnp.where(at_east, place + (n_cols - EDGE), place - (west_lane + RIM))
    x_edge_field = x_field_weights(
        x_edge, ((place >= EDGE) & (place <= RIM + 1)) | ((place >= west_lane) & (place < west_lane + RIM))
    )
    x_edge_advect = x_advect_weights(
        x_edge, ((place >= 1) & (place <= RIM)) | ((place > west_lane) & (place <= west_lane + RIM))
    )
    top = halo - R
    span = ceil_to(n_rows + 2 * R, 16)
    n_ext = n_rows + 2 * halo
    n_field = ext.shape[1]
    span_out = ceil_to(n_rows, 16)

    def y_places(length, start):
        y_out = lax.broadcasted_iota(jnp.int32, (span_out, length), 0)
        y_in = lax.broadcasted_iota(jnp.int32, (span_out, length), 1) + start

        def keep(step):
            y_global = y_in + step + row * n_rows
            return (y_global >= 0) & (y_global < rows * n_rows) & (y_out < n_rows)

        return y_in - y_out, keep

    y_field_high, y_field_low = field_weights(*y_places(n_field, -halo), 0)
    distance, keep = y_places(span, -R)
    y_high, y_low = split(gaussian(distance, keep(0)))

    for load in loads:
        load.wait()

    row_id = lax.broadcasted_iota(jnp.int32, (n_rows, n_cols), 0)
    words = bits[...]
    word = jnp.broadcast_to(words[0:1], (n_rows, n_cols))
    bit = row_id
    for j in range(1, words.shape[0]):
        here = row_id >= j * WORD_ROWS
        word = jnp.where(here, words[j : j + 1], word)
        bit = jnp.where(here, row_id - j * WORD_ROWS, bit)
    wet = (jnp.right_shift(word, bit) & 1).astype(jnp.float32)
    for c in range(2):
        ext[c, halo : halo + n_rows, :] = jnp.zeros((n_rows, LANES), jnp.float32)
        ext[c, halo : halo + n_rows, 0:n_cols] = vel[c] * wet
        ext[c, n_rows + 2 * halo :, :] = jnp.zeros((8, LANES), jnp.float32)

    lane = lax.broadcasted_iota(jnp.int32, (halo, LANES), 1)

    def pack(start):
        def block(c, g, place):
            rows_at = halo + g * halo
            return roll(ext[c, rows_at : rows_at + halo, :], place * RIM - start)

        def join(a, b, c):
            rest = jnp.where(lane < 3 * RIM, c, 0.0)
            return jnp.where(lane < RIM, a, jnp.where(lane < 2 * RIM, b, rest))

        first = join(block(0, 0, 0), block(1, 0, 1), block(0, 1, 2))
        last = join(block(0, 2, 0), block(1, 2, 1), block(1, 1, 2))
        return first, last

    west_cols, east_cols = pack(0), pack(n_cols - RIM)
    at_west = sub == 0
    for i in range(2):
        at = slice(i * halo, i * halo + halo)
        strips[0, at, :] = jnp.where(at_west, west_cols[i], east_cols[i])
        strips[1, at, :] = jnp.where(at_west, east_cols[i], west_cols[i])

    @pl.when(jnp.logical_not(has_up))
    def _():
        ext[:, 0:halo, :] = jnp.zeros((2, halo, LANES), jnp.float32)
        seam[0:halo, :] = jnp.zeros((halo, LANES), jnp.float32)
        beside[0:halo, :] = jnp.zeros((halo, LANES), jnp.float32)

    @pl.when(jnp.logical_not(has_down))
    def _():
        ext[:, halo + n_rows : n_rows + 2 * halo, :] = jnp.zeros((2, halo, LANES), jnp.float32)
        seam[3 * halo : 3 * halo + halo, :] = jnp.zeros((halo, LANES), jnp.float32)
        beside[3 * halo : 3 * halo + halo, :] = jnp.zeros((halo, LANES), jnp.float32)

    n_beside = sum(there.astype(jnp.int32) for there in (has_up, has_down, has_left, has_right))
    pl.semaphore_wait(barrier, 1 + 2 * n_beside)

    def pass_copy(source, slot, chunk, send, t, to):
        at = pl.ds(chunk * halo, halo)
        return pltpu.make_async_remote_copy(
            src_ref=source.at[at],
            dst_ref=passing.at[slot, at],
            send_sem=send,
            recv_sem=pass_recv.at[slot, chunk],
            device_id=(grp, t, row, to),
            device_id_type=MESH,
        )

    def pass_right(source, slot, chunk, to):
        return pass_copy(source, slot, chunk, right_send.at[slot, chunk], tile + 1, to)

    def pass_left(source, slot, chunk, to):
        return pass_copy(source, slot, chunk, left_send.at[slot, chunk], tile - 1, to)

    def rim_copy(part, r):
        source = (2 * halo, halo)[part - 1]
        target = (0, 3 * halo)[part - 1]
        return pltpu.make_async_remote_copy(
            src_ref=seam.at[pl.ds(source, halo)],
            dst_ref=seam.at[pl.ds(target, halo)],
            send_sem=rim_send.at[part - 1],
            recv_sem=rim_recv.at[part - 1],
            device_id=(grp, tile, r, sub),
            device_id_type=MESH,
        )

    def beside_copy(part, r):
        source = ((0, 2 * halo), (halo, halo), (0, halo))[part]
        target = (halo, 0, 3 * halo)[part]
        return pltpu.make_async_remote_copy(
            src_ref=strips.at[1, pl.ds(*source)],
            dst_ref=beside.at[pl.ds(target, source[1])],
            send_sem=beside_send.at[part],
            recv_sem=beside_recv.at[part],
            device_id=(grp, tile, r, other),
            device_id_type=MESH,
        )

    def row_copy(part, r):
        source = (halo + n_rows - halo, halo)[part - 1]
        target = (0, halo + n_rows)[part - 1]
        return pltpu.make_async_remote_copy(
            src_ref=ext.at[:, pl.ds(source, halo)],
            dst_ref=ext.at[:, pl.ds(target, halo)],
            send_sem=row_send.at[part - 1],
            recv_sem=row_recv.at[part - 1],
            device_id=(grp, tile, r, sub),
            device_id_type=MESH,
        )

    def first_sends(act):
        @pl.when(has_left)
        def _():
            for chunk in range(2):
                act(pass_left(strips.at[0], tile, chunk, other))

        @pl.when(has_right)
        def _():
            for chunk in range(2):
                act(pass_right(strips.at[0], tile, chunk, other))

        @pl.when(has_down)
        def _():
            act(row_copy(1, row + 1))
            act(beside_copy(1, row + 1))

        @pl.when(has_up)
        def _():
            act(row_copy(2, row - 1))
            act(beside_copy(2, row - 1))

        act(beside_copy(0, row))
        for chunk in range(2):
            act(pass_copy(strips.at[0], tile, chunk, across_send.at[chunk], tile, other))

    def pass_on(step, act):
        for chunk in range(2):
            for slot, there, more, onward in (
                (tile + step, tile + step < tiles, has_left, pass_left),
                (tile - step, tile - step >= 0, has_right, pass_right),
            ):

                @pl.when(there)
                def _():
                    act(slot, chunk, more, onward)

    def receive(slot, chunk, more, onward):
        pass_copy(passing.at[slot], slot, chunk, across_send.at[0], tile, other).wait_recv()

        @pl.when(more)
        def _():
            onward(passing.at[slot], slot, chunk, sub).start()

    def sent(slot, chunk, more, onward):
        @pl.when(more)
        def _():
            onward(passing.at[slot], slot, chunk, sub).wait_send()

    def rim_sends(act):
        @pl.when(has_down)
        def _():
            act(rim_copy(1, row + 1))

        @pl.when(has_up)
        def _():
            act(rim_copy(2, row - 1))

    first_sends(lambda copy: copy.start())

    west = jnp.int32(0)
    for i in range(tiles):
        west = jnp.where(face_ref[i] == tile, i, west)
    across_seam = jnp.where(at_west, west, face_ref[tile])
    east_turn = turn_ref[tile]
    west_turn = turn_ref[west]
    west_turn = jnp.where(west_turn == 0, 0, 4 - west_turn)
    turn = jnp.where(at_west, west_turn, east_turn)

    def choose(a, b):
        return jnp.where(turn == a, 1.0, jnp.where(turn == b, -1.0, 0.0)).astype(jnp.float32)

    cosine, sine = choose(0, 2), choose(1, 3)

    def derive(field, c):
        centre = field[c, top : top + span, :]
        grad_x = DERIV_SCALE * (roll(centre, -1) - roll(centre, 1))
        grad_y = DERIV_SCALE * (field[c, top + 1 : top + 1 + span, :] - field[c, top - 1 : top - 1 + span, :])
        return centre, grad_x, grad_y

    def advected(field):
        u, u_x, u_y = derive(field, 0)
        v, v_x, v_y = derive(field, 1)
        return u * u_x + v * u_y, u * v_x + v * v_y

    def along_field(value, weights):
        high, low = split(value)
        return dot(jnp.concatenate([high, low], axis=1), weights[0]) + dot(high, weights[1])

    def along_advect(value, weights):
        both = dot(jnp.concatenate(split(value), axis=1), weights)
        return both[:, :LANES] + both[:, LANES:]

    @pl.when(has_up)
    def _():
        row_copy(1, row).wait_recv()

    @pl.when(has_down)
    def _():
        row_copy(2, row).wait_recv()

    for c, advect in enumerate(advected(ext)):
        inner_field[c] = along_field(ext[c], x_own_field)
        inner_advect[c] = along_advect(advect, x_own_advect)

    lane = lax.broadcasted_iota(jnp.int32, (n_ext, LANES), 1)
    for c in range(2):
        own = ext[c, 0:n_ext, :]
        rest = jnp.where(lane >= LANES - EDGE, roll(own, -EDGE), 0.0)
        ring[c, 0:n_ext, :] = jnp.where(lane < EDGE, roll(own, EDGE - n_cols), rest)
        ring[c, n_ext:, :] = jnp.zeros((8, LANES), jnp.float32)

    for step in range(1, tiles):
        pass_on(step, receive)
    for chunk in range(2):
        pass_copy(passing.at[tile], tile, chunk, across_send.at[0], tile, other).wait_recv()
    seam[halo : 3 * halo, :] = passing[across_seam]
    rim_sends(lambda copy: copy.start())

    east_c = jnp.where(at_west, 1.0, cosine).astype(jnp.float32)
    east_s = jnp.where(at_west, 0.0, sine).astype(jnp.float32)
    west_c = jnp.where(at_west, cosine, 1.0).astype(jnp.float32)
    west_s = jnp.where(at_west, sine, 0.0).astype(jnp.float32)
    lane = lax.broadcasted_iota(jnp.int32, (halo, LANES), 1)
    in_east = (lane >= EDGE) & (lane < EDGE + RIM)
    in_west = (lane >= west_lane) & (lane < west_lane + RIM)

    def fill(block, u_from, v_from):
        east, west = [], []
        for group, at in (u_from, v_from):
            outer, inner = (held[group * halo : (group + 1) * halo, :] for held in (seam, beside))
            east.append(roll(jnp.where(at_west, inner, outer), EDGE - at * RIM))
            west.append(roll(jnp.where(at_west, outer, inner), west_lane - at * RIM))
        east = (east_c * east[0] - east_s * east[1], east_s * east[0] + east_c * east[1])
        west = (west_c * west[0] - west_s * west[1], west_s * west[0] + west_c * west[1])
        at = slice(block * halo, (block + 1) * halo)
        for c in range(2):
            ring[c, at, :] = jnp.where(in_east, east[c], jnp.where(in_west, west[c], ring[c, at, :]))

    beside_copy(0, row).wait_recv()
    fill(1, (1, 0), (1, 1))
    fill(2, (1, 2), (2, 2))
    fill(3, (2, 0), (2, 1))

    @pl.when(has_up)
    def _():
        beside_copy(1, row).wait_recv()
        rim_copy(1, row).wait_recv()

    @pl.when(has_down)
    def _():
        beside_copy(2, row).wait_recv()
        rim_copy(2, row).wait_recv()

    fill(0, (0, 0), (0, 1))
    fill(4, (3, 0), (3, 1))

    def smoothed(value, high, low):
        value_high, value_low = split(value)
        return dot(high, value_high) + (dot(high, value_low) + dot(low, value_high))

    smooth = []
    for c in range(2):
        field = inner_field[c] + along_field(ring[c], x_edge_field)
        both = smoothed(field, y_field_high, y_field_low)
        smooth.append((both[:span_out, :LANES], both[:span_out, LANES:], both[span_out:, :LANES]))
    advect = [inner_advect[c] + along_advect(a, x_edge_advect) for c, a in enumerate(advected(ring))]
    advect = smoothed(jnp.concatenate(advect, axis=1), y_high, y_low)
    (u, u_x, u_y), (v, v_x, v_y) = smooth
    fine = (
        advect[:, :LANES] - (u * u_x + v * u_y),
        advect[:, LANES:] - (u * v_x + v * v_y),
    )

    n_out = n_rows // POOL
    m_out = n_cols // POOL
    col = lax.broadcasted_iota(jnp.int32, (LANES, m_out), 0)
    block_at = lax.broadcasted_iota(jnp.int32, (LANES, m_out), 1) * POOL
    mean = jnp.where((col >= block_at) & (col < block_at + POOL), 1.0 / POOL**2, 0.0)
    mean = mean.astype(jnp.bfloat16)
    for c in range(2):
        pooled[c] = jnp.zeros((n_rows, LANES), jnp.float32)
        pooled[c, :, 0:n_cols] = fine[c][:n_rows, :n_cols] * wet
        total = pooled[c, pl.ds(0, n_out, stride=POOL), :]
        for k in range(1, POOL):
            total = total + pooled[c, pl.ds(k, n_out, stride=POOL), :]
        high, low = split(total)
        out_ref[c] = dot(high, mean) + dot(low, mean)

    first_sends(lambda copy: copy.wait_send())
    for step in range(1, tiles):
        pass_on(step, sent)
    rim_sends(lambda copy: copy.wait_send())


def on_device(velocity, wet_bits, east_face, seam_turn):
    _, n_rows, n_cols = velocity.shape
    tiles = lax.axis_size("tile")
    halo = ceil_to(RIM, 8)
    assert n_rows == 3 * halo and lax.axis_size("sub") == 2
    assert RIM <= n_cols <= LANES and 3 * RIM <= LANES
    n_ext = n_rows + 2 * halo
    f32 = jnp.float32
    return pl.pallas_call(
        kernel,
        out_shape=pltpu.VMEM((2, n_rows // POOL, n_cols // POOL), f32),
        in_specs=[pl.BlockSpec(memory_space=pltpu.HBM)] * 4,
        out_specs=pl.BlockSpec(memory_space=pltpu.VMEM),
        scratch_shapes=[
            pltpu.SMEM(east_face.shape, jnp.int32),
            pltpu.SMEM(seam_turn.shape, jnp.int32),
            pltpu.VMEM(velocity.shape, f32),
            pltpu.VMEM(wet_bits.shape, jnp.int32),
            pltpu.VMEM((2, n_ext + 8, LANES), f32),
            pltpu.VMEM((2, 2 * halo, LANES), f32),
            pltpu.VMEM((tiles, 2 * halo, LANES), f32),
            pltpu.VMEM((4 * halo, LANES), f32),
            pltpu.VMEM((4 * halo, LANES), f32),
            pltpu.VMEM((2, n_ext + 8, LANES), f32),
            pltpu.VMEM((2, n_ext + 8, 2 * LANES), f32),
            pltpu.VMEM((2, ceil_to(n_rows + 2 * R, 16), LANES), f32),
            pltpu.VMEM((2, n_rows, LANES), f32),
            pltpu.SemaphoreType.DMA((4,)),
            pltpu.SemaphoreType.DMA((2,)),
            pltpu.SemaphoreType.DMA((2,)),
            pltpu.SemaphoreType.DMA((3,)),
            pltpu.SemaphoreType.DMA((3,)),
        ]
        + [pltpu.SemaphoreType.DMA((tiles, 2))] * 2
        + [pltpu.SemaphoreType.DMA((2,)), pltpu.SemaphoreType.DMA((tiles, 2))]
        + [pltpu.SemaphoreType.DMA((2,))] * 2,
        compiler_params=pltpu.CompilerParams(
            collective_id=0, has_side_effects=True, vmem_limit_bytes=60 * 1024 * 1024
        ),
    )(east_face, seam_turn, velocity, wet_bits)


def solution(mesh):
    placed = (
        P(None, ("grp", "row"), ("tile", "sub")),
        P(("grp", "row"), ("tile", "sub")),
        P(),
        P(),
    )
    return jax.shard_map(
        on_device,
        mesh=mesh,
        in_specs=placed,
        out_specs=P(None, ("grp", "row"), ("tile", "sub")),
        check_vma=False,
    )
```

```python
import functools
import math

import jax
import jax.numpy as jnp
from jax import lax
from jax.experimental import pallas as pl
from jax.experimental.pallas import tpu as pltpu
from jax.sharding import PartitionSpec as P

R = 32
RIM = R + 1
LANES = 128
EDGE = 2
DERIV_SCALE = 8.0
POOL = 4
WORD_ROWS = 30
MESH = pl.DeviceIdType.MESH

WEIGHT_SUM = sum(math.exp(-0.5 * (k / R) ** 2) for k in range(-R, R + 1))


def ceil_to(value, step):
    return -(-value // step) * step


def gaussian(distance, keep):
    d = distance.astype(jnp.float32) * (1.0 / R)
    weight = jnp.exp(-0.5 * d * d) * (1.0 / WEIGHT_SUM)
    return jnp.where(keep & (jnp.abs(distance) <= R), weight, 0.0)


def split(value):
    high = value.astype(jnp.bfloat16)
    low = (value - high.astype(jnp.float32)).astype(jnp.bfloat16)
    return high, low


def dot(a, b):
    return jnp.dot(a, b, preferred_element_type=jnp.float32)


def roll(value, shift, axis=1):
    size = value.shape[axis]
    shift = shift % size
    return value if shift == 0 else pltpu.roll(value, shift, axis)


def kernel(
    face_hbm, turn_hbm, vel_hbm, bits_hbm, out_ref,
    face_ref, turn_ref, vel, bits, ext, strip, seams, above, below, beside,
    ring, inner_field, inner_advect, pooled,
    load_sem, row_send, row_recv, beside_send, beside_recv, strip_send, strip_recv,
):
    tiles, rows = lax.axis_size("tile"), lax.axis_size("row")
    grp, tile, row, sub = (lax.axis_index(a) for a in ("grp", "tile", "row", "sub"))
    n_rows, n_cols = vel.shape[1], vel.shape[2]
    halo = ceil_to(RIM, 8)
    has_up, has_down = row > 0, row < rows - 1
    other = 1 - sub

    loads = [
        pltpu.make_async_copy(vel_hbm, vel, load_sem.at[0]),
        pltpu.make_async_copy(bits_hbm, bits, load_sem.at[1]),
        pltpu.make_async_copy(face_hbm, face_ref, load_sem.at[2]),
        pltpu.make_async_copy(turn_hbm, turn_ref, load_sem.at[3]),
    ]
    for load in loads:
        load.start()

    barrier = pltpu.get_barrier_semaphore()

    def greet(t, r, s):
        pl.semaphore_signal(barrier, inc=1, device_id=(grp, t, r, s), device_id_type=MESH)

    for k in range(tiles):
        t = lax.rem(tile + k, tiles)
        greet(t, row, other)
        for there, r in ((has_up, row - 1), (has_down, row + 1)):

            @pl.when(there)
            def _():
                greet(t, r, other)

    for there, r in ((has_up, row - 1), (has_down, row + 1)):

        @pl.when(there)
        def _():
            greet(tile, r, sub)

    west_lane = LANES - EDGE - RIM
    place = lax.broadcasted_iota(jnp.int32, (LANES, LANES), 0)
    x_out = lax.broadcasted_iota(jnp.int32, (LANES, LANES), 1)

    def field_weights(distance, keep, axis):
        weight = gaussian(distance, keep(0))
        slope = DERIV_SCALE * (gaussian(distance - 1, keep(-1)) - gaussian(distance + 1, keep(1)))
        return split(jnp.concatenate([weight, slope], axis=axis))

    def x_field_weights(x_in, keep):
        high, low = field_weights(x_in - x_out, lambda step: keep & (x_out < n_cols), 1)
        return jnp.concatenate([high, high], axis=0), low

    def x_advect_weights(x_in, keep):
        high, low = split(gaussian(x_in - x_out, keep & (x_out < n_cols)))
        above = jnp.concatenate([high, low], axis=1)
        below = jnp.concatenate([high, jnp.zeros_like(low)], axis=1)
        return jnp.concatenate([above, below], axis=0)

    x_own_field = x_field_weights(place, place < n_cols)
    x_own_advect = x_advect_weights(place, (place >= 1) & (place <= n_cols - 2))
    at_east = place < LANES // 2
    x_edge = jnp.where(at_east, place + (n_cols - EDGE), place - (west_lane + RIM))
    x_edge_field = x_field_weights(
        x_edge, ((place >= EDGE) & (place <= RIM + 1)) | ((place >= west_lane) & (place < west_lane + RIM))
    )
    x_edge_advect = x_advect_weights(
        x_edge, ((place >= 1) & (place <= RIM)) | ((place > west_lane) & (place <= west_lane + RIM))
    )
    top = halo - R
    span = ceil_to(n_rows + 2 * R, 16)
    n_ext = n_rows + 2 * halo
    n_field = ext.shape[1]
    span_out = ceil_to(n_rows, 16)

    def y_places(length, start):
        y_out = lax.broadcasted_iota(jnp.int32, (span_out, length), 0)
        y_in = lax.broadcasted_iota(jnp.int32, (span_out, length), 1) + start

        def keep(step):
            y_global = y_in + step + row * n_rows
            return (y_global >= 0) & (y_global < rows * n_rows) & (y_out < n_rows)

        return y_in - y_out, keep

    y_field_high, y_field_low = field_weights(*y_places(n_field, -halo), 0)
    distance, keep = y_places(span, -R)
    y_high, y_low = split(gaussian(distance, keep(0)))

    for load in loads:
        load.wait()

    row_id = lax.broadcasted_iota(jnp.int32, (n_rows, n_cols), 0)
    words = bits[...]
    word = jnp.broadcast_to(words[0:1], (n_rows, n_cols))
    bit = row_id
    for j in range(1, words.shape[0]):
        here = row_id >= j * WORD_ROWS
        word = jnp.where(here, words[j : j + 1], word)
        bit = jnp.where(here, row_id - j * WORD_ROWS, bit)
    wet = (jnp.right_shift(word, bit) & 1).astype(jnp.float32)
    for c in range(2):
        ext[c, halo : halo + n_rows, :] = jnp.zeros((n_rows, LANES), jnp.float32)
        ext[c, halo : halo + n_rows, 0:n_cols] = vel[c] * wet
        ext[c, n_rows + 2 * halo :, :] = jnp.zeros((8, LANES), jnp.float32)

    per_row = LANES // R
    deep = halo // 8
    units = 2 * deep
    group = ceil_to(units + 2, per_row) // per_row
    group_rows = group * 8
    strip_rows = strip.shape[0]
    lane = lax.broadcasted_iota(jnp.int32, (8, LANES), 1)

    def place_of(part, i):
        last = (group - 1, units % per_row * R + i)
        if part == "first":
            return divmod(i, per_row), last
        if part == "last":
            at, unit = divmod(i, per_row)
            return (group + at, unit), (group + last[0], last[1])
        last = (last[0], last[1] + units)
        if i < 2:
            return (i * group + group - 1, units % per_row + 1), last
        at, unit = divmod(i - 2, per_row)
        return (2 * group + at, unit), last

    at_west = sub == 0
    lines = [jnp.zeros((8, LANES), jnp.float32)] * (strip_rows // 8)
    for c in range(2):
        own = ext[c, halo : halo + n_rows, :]
        own = jnp.where(at_west, own, roll(own, RIM - n_cols))
        for p, part in enumerate(("first", "middle", "last")):
            for d in range(deep):
                unit = own[(p * deep + d) * 8 : (p * deep + d + 1) * 8]
                (line, at), (last_line, last) = place_of(part, c * deep + d)
                lines[line] = jnp.where(lane // R == at, roll(unit, at * R), lines[line])
                lines[last_line] = jnp.where(lane == last, roll(unit, last - R), lines[last_line])
    for i, line in enumerate(lines):
        strip[i * 8 : (i + 1) * 8, :] = line

    @pl.when(jnp.logical_not(has_up))
    def _():
        ext[:, 0:halo, :] = jnp.zeros((2, halo, LANES), jnp.float32)
        beside[:, 0:halo, :] = jnp.zeros((2, halo, LANES), jnp.float32)
        above[...] = jnp.zeros((tiles, group_rows, LANES), jnp.float32)

    @pl.when(jnp.logical_not(has_down))
    def _():
        ext[:, halo + n_rows : n_rows + 2 * halo, :] = jnp.zeros((2, halo, LANES), jnp.float32)
        beside[:, halo + n_rows :, :] = jnp.zeros((2, halo, LANES), jnp.float32)
        below[...] = jnp.zeros((tiles, group_rows, LANES), jnp.float32)

    n_beside = has_up.astype(jnp.int32) + has_down.astype(jnp.int32)
    pl.semaphore_wait(barrier, tiles + n_beside * (tiles + 1))

    def strip_copy(part, slot, k, t, r):
        source, size = ((0, strip_rows), (group_rows, group_rows), (0, group_rows))[part]
        return pltpu.make_async_remote_copy(
            src_ref=strip.at[pl.ds(source, size)],
            dst_ref=(seams, above, below)[part].at[slot],
            send_sem=strip_send.at[part, k],
            recv_sem=strip_recv.at[part, slot],
            device_id=(grp, t, r, other),
            device_id_type=MESH,
        )

    def beside_copy(part, r):
        source, size = ((halo, n_rows), (n_rows, halo), (halo, halo))[part]
        target = (halo, 0, halo + n_rows)[part]
        return pltpu.make_async_remote_copy(
            src_ref=ext.at[:, pl.ds(source, size)],
            dst_ref=beside.at[:, pl.ds(target, size)],
            send_sem=beside_send.at[part],
            recv_sem=beside_recv.at[part],
            device_id=(grp, tile, r, other),
            device_id_type=MESH,
        )

    def row_copy(part, r):
        source = (halo + n_rows - halo, halo)[part - 1]
        target = (0, halo + n_rows)[part - 1]
        return pltpu.make_async_remote_copy(
            src_ref=ext.at[:, pl.ds(source, halo)],
            dst_ref=ext.at[:, pl.ds(target, halo)],
            send_sem=row_send.at[part - 1],
            recv_sem=row_recv.at[part - 1],
            device_id=(grp, tile, r, sub),
            device_id_type=MESH,
        )

    def strip_sends(act, part, r):
        for k in reversed(range(tiles)):
            act(strip_copy(part, tile, k, lax.rem(tile + k, tiles), r))

    def all_sends(act):
        strip_sends(act, 0, row)
        act(beside_copy(0, row))
        for part, there, r in ((1, has_down, row + 1), (2, has_up, row - 1)):

            @pl.when(there)
            def _():
                act(row_copy(part, r))
                act(beside_copy(part, r))
                strip_sends(act, part, r)

    all_sends(lambda copy: copy.start())

    west = jnp.int32(0)
    for i in range(tiles):
        west = jnp.where(face_ref[i] == tile, i, west)
    across_seam = jnp.where(at_west, west, face_ref[tile])
    east_turn = turn_ref[tile]
    west_turn = turn_ref[west]
    west_turn = jnp.where(west_turn == 0, 0, 4 - west_turn)
    turn = jnp.where(at_west, west_turn, east_turn)

    def choose(a, b):
        return jnp.where(turn == a, 1.0, jnp.where(turn == b, -1.0, 0.0)).astype(jnp.float32)

    cosine, sine = choose(0, 2), choose(1, 3)

    def derive(field, c, start, length):
        centre = field[c, start : start + length, :]
        grad_x = DERIV_SCALE * (roll(centre, -1) - roll(centre, 1))
        grad_y = DERIV_SCALE * (field[c, start + 1 : start + 1 + length, :] - field[c, start - 1 : start - 1 + length, :])
        return centre, grad_x, grad_y

    def advected(field, start, length):
        u, u_x, u_y = derive(field, 0, start, length)
        v, v_x, v_y = derive(field, 1, start, length)
        return u * u_x + v * u_y, u * v_x + v * v_y

    def along_field(value, weights):
        high, low = split(value)
        return dot(jnp.concatenate([high, low], axis=1), weights[0]) + dot(high, weights[1])

    def along_advect(value, weights):
        both = dot(jnp.concatenate(split(value), axis=1), weights)
        return both[:, :LANES] + both[:, LANES:]

    beside_copy(0, row).wait_recv()
    for part, there in ((1, has_up), (2, has_down)):

        @pl.when(there)
        def _():
            row_copy(part, row).wait_recv()
            beside_copy(part, row).wait_recv()

    for c, advect in enumerate(advected(ext, top, span)):
        inner_field[c] = along_field(ext[c], x_own_field)
        inner_advect[c] = along_advect(advect, x_own_advect)

    lane = lax.broadcasted_iota(jnp.int32, (n_ext, LANES), 1)
    inner_at = jnp.where(at_west, EDGE, west_lane)
    in_inner = (lane >= inner_at) & (lane < inner_at + RIM)
    for c in range(2):
        own, inner = ext[c, 0:n_ext, :], beside[c]
        inner = jnp.where(at_west, roll(inner, EDGE), roll(inner, west_lane + RIM - n_cols))
        rest = jnp.where(lane >= LANES - EDGE, roll(own, -EDGE), jnp.where(in_inner, inner, 0.0))
        ring[c, 0:n_ext, :] = jnp.where(lane < EDGE, roll(own, EDGE - n_cols), rest)
        ring[c, n_ext:, :] = jnp.zeros((8, LANES), jnp.float32)

    outer_at = jnp.where(at_west, west_lane, EDGE)
    lane = lax.broadcasted_iota(jnp.int32, (8, LANES), 1)
    in_unit = lane < outer_at + R
    in_outer = (lane >= outer_at) & (lane < outer_at + RIM)

    def lines_of(strips):
        held = strips[across_seam]
        held = jnp.where(at_west, roll(held, west_lane), roll(held, EDGE))
        return [held[i * 8 : (i + 1) * 8] for i in range(held.shape[0] // 8)]

    def fill(lines, part, block):
        for d in range(deep):
            uv = []
            for c in range(2):
                (line, unit), (last_line, last) = place_of(part, c * deep + d)
                uv.append(jnp.where(in_unit, roll(lines[line], -unit * R), roll(lines[last_line], R - last)))
            turned = (cosine * uv[0] - sine * uv[1], sine * uv[0] + cosine * uv[1])
            at = slice((block * deep + d) * 8, (block * deep + d + 1) * 8)
            for c in range(2):
                ring[c, at, :] = jnp.where(in_outer, turned[c], ring[c, at, :])

    def add_field(start, length):
        for c in range(2):
            inner_field[c, start : start + length, :] += along_field(ring[c, start : start + length, :], x_edge_field)

    def add_advect(start, length):
        for c, advect in enumerate(advected(ring, start, length)):
            inner_advect[c, start - top : start - top + length, :] += along_advect(advect, x_edge_advect)

    for slot in range(tiles):
        strip_copy(0, slot, 0, tile, row).wait_recv()
    lines = lines_of(seams)
    fill(lines, "first", 1)
    fill(lines, "middle", 2)
    fill(lines, "last", 3)
    add_field(halo, n_rows)
    add_advect(halo + 8, n_rows - 16)

    for part, there in ((1, has_up), (2, has_down)):

        @pl.when(there)
        def _():
            for slot in range(tiles):
                strip_copy(part, slot, 0, tile, row).wait_recv()

    fill([None] * group + lines_of(above), "last", 0)
    fill(lines_of(below), "first", 4)
    add_field(0, halo)
    add_field(halo + n_rows, n_field - halo - n_rows)
    add_advect(top, halo + 8 - top)
    add_advect(halo + n_rows - 8, top + span - (halo + n_rows - 8))

    def smoothed(value, high, low):
        value_high, value_low = split(value)
        return dot(high, value_high) + (dot(high, value_low) + dot(low, value_high))

    smooth = []
    for c in range(2):
        both = smoothed(inner_field[c], y_field_high, y_field_low)
        smooth.append((both[:span_out, :LANES], both[:span_out, LANES:], both[span_out:, :LANES]))
    advect = smoothed(jnp.concatenate([inner_advect[0], inner_advect[1]], axis=1), y_high, y_low)
    (u, u_x, u_y), (v, v_x, v_y) = smooth
    fine = (
        advect[:, :LANES] - (u * u_x + v * u_y),
        advect[:, LANES:] - (u * v_x + v * v_y),
    )

    n_out = n_rows // POOL
    m_out = n_cols // POOL
    col = lax.broadcasted_iota(jnp.int32, (LANES, m_out), 0)
    block_at = lax.broadcasted_iota(jnp.int32, (LANES, m_out), 1) * POOL
    mean = jnp.where((col >= block_at) & (col < block_at + POOL), 1.0 / POOL**2, 0.0)
    mean = mean.astype(jnp.bfloat16)
    for c in range(2):
        pooled[c] = jnp.zeros((n_rows, LANES), jnp.float32)
        pooled[c, :, 0:n_cols] = fine[c][:n_rows, :n_cols] * wet
        total = pooled[c, pl.ds(0, n_out, stride=POOL), :]
        for k in range(1, POOL):
            total = total + pooled[c, pl.ds(k, n_out, stride=POOL), :]
        high, low = split(total)
        out_ref[c] = dot(high, mean) + dot(low, mean)

    all_sends(lambda copy: copy.wait_send())


def on_device(velocity, wet_bits, east_face, seam_turn):
    _, n_rows, n_cols = velocity.shape
    tiles = lax.axis_size("tile")
    halo = ceil_to(RIM, 8)
    assert n_rows == 3 * halo and lax.axis_size("sub") == 2
    assert 2 * RIM <= n_cols <= LANES and LANES % R == 0
    per_row, units = LANES // R, 2 * halo // 8
    group_rows = ceil_to(units + 2, per_row) // per_row * 8
    strip_rows = 2 * group_rows + ceil_to(units - 2, per_row) // per_row * 8
    assert units % per_row < per_row - 1 and 2 * units <= R
    n_ext = n_rows + 2 * halo
    f32 = jnp.float32
    return pl.pallas_call(
        kernel,
        out_shape=pltpu.VMEM((2, n_rows // POOL, n_cols // POOL), f32),
        in_specs=[pl.BlockSpec(memory_space=pltpu.HBM)] * 4,
        out_specs=pl.BlockSpec(memory_space=pltpu.VMEM),
        scratch_shapes=[
            pltpu.SMEM(east_face.shape, jnp.int32),
            pltpu.SMEM(seam_turn.shape, jnp.int32),
            pltpu.VMEM(velocity.shape, f32),
            pltpu.VMEM(wet_bits.shape, jnp.int32),
            pltpu.VMEM((2, n_ext + 8, LANES), f32),
            pltpu.VMEM((strip_rows, LANES), f32),
            pltpu.VMEM((tiles, strip_rows, LANES), f32),
            pltpu.VMEM((tiles, group_rows, LANES), f32),
            pltpu.VMEM((tiles, group_rows, LANES), f32),
            pltpu.VMEM((2, n_ext, LANES), f32),
            pltpu.VMEM((2, n_ext + 8, LANES), f32),
            pltpu.VMEM((2, n_ext + 8, 2 * LANES), f32),
            pltpu.VMEM((2, ceil_to(n_rows + 2 * R, 16), LANES), f32),
            pltpu.VMEM((2, n_rows, LANES), f32),
            pltpu.SemaphoreType.DMA((4,)),
            pltpu.SemaphoreType.DMA((2,)),
            pltpu.SemaphoreType.DMA((2,)),
            pltpu.SemaphoreType.DMA((3,)),
            pltpu.SemaphoreType.DMA((3,)),
        ]
        + [pltpu.SemaphoreType.DMA((3, tiles))] * 2,
        compiler_params=pltpu.CompilerParams(
            collective_id=0, has_side_effects=True, vmem_limit_bytes=60 * 1024 * 1024
        ),
    )(east_face, seam_turn, velocity, wet_bits)


def solution(mesh):
    placed = (
        P(None, ("grp", "row"), ("tile", "sub")),
        P(("grp", "row"), ("tile", "sub")),
        P(),
        P(),
    )
    return jax.shard_map(
        on_device,
        mesh=mesh,
        in_specs=placed,
        out_specs=P(None, ("grp", "row"), ("tile", "sub")),
        check_vma=False,
    )
```

```python
import functools
import math

import jax
import jax.numpy as jnp
from jax import lax
from jax.experimental import pallas as pl
from jax.experimental.pallas import tpu as pltpu
from jax.sharding import PartitionSpec as P

R = 32
RIM = R + 1
LANES = 128
EDGE = 2
DERIV_SCALE = 8.0
POOL = 4
WORD_ROWS = 30
MESH = pl.DeviceIdType.MESH

WEIGHT_SUM = sum(math.exp(-0.5 * (k / R) ** 2) for k in range(-R, R + 1))


def ceil_to(value, step):
    return -(-value // step) * step


def gaussian(distance, keep):
    d = distance.astype(jnp.float32) * (1.0 / R)
    weight = jnp.exp(-0.5 * d * d) * (1.0 / WEIGHT_SUM)
    return jnp.where(keep & (jnp.abs(distance) <= R), weight, 0.0)


def split(value):
    high = value.astype(jnp.bfloat16)
    low = (value - high.astype(jnp.float32)).astype(jnp.bfloat16)
    return high, low


def dot(a, b):
    return jnp.dot(a, b, preferred_element_type=jnp.float32)


def roll(value, shift, axis=1):
    size = value.shape[axis]
    shift = shift % size
    return value if shift == 0 else pltpu.roll(value, shift, axis)


def kernel(
    face_hbm, turn_hbm, vel_hbm, bits_hbm, out_ref,
    face_ref, turn_ref, vel, bits, ext, strip, seams, above, below, beside,
    ring, field_sum, advect_sum, pooled,
    load_sem, row_send, row_recv, beside_send, beside_recv, strip_send, strip_recv,
):
    tiles, rows = lax.axis_size("tile"), lax.axis_size("row")
    grp, tile, row, sub = (lax.axis_index(a) for a in ("grp", "tile", "row", "sub"))
    n_rows, n_cols = vel.shape[1], vel.shape[2]
    halo = ceil_to(RIM, 8)
    has_up, has_down = row > 0, row < rows - 1
    other = 1 - sub

    barrier = pltpu.get_barrier_semaphore()

    def greet(t, r, s):
        pl.semaphore_signal(barrier, inc=1, device_id=(grp, t, r, s), device_id_type=MESH)

    for k in range(tiles):
        t = lax.rem(tile + k, tiles)
        greet(t, row, other)
        for there, r in ((has_up, row - 1), (has_down, row + 1)):

            @pl.when(there)
            def _():
                greet(t, r, other)

    for there, r in ((has_up, row - 1), (has_down, row + 1)):

        @pl.when(there)
        def _():
            greet(tile, r, sub)

    loads = [
        pltpu.make_async_copy(vel_hbm, vel, load_sem.at[0]),
        pltpu.make_async_copy(bits_hbm, bits, load_sem.at[1]),
        pltpu.make_async_copy(face_hbm, face_ref, load_sem.at[2]),
        pltpu.make_async_copy(turn_hbm, turn_ref, load_sem.at[3]),
    ]
    for load in loads:
        load.start()

    west_lane = LANES - EDGE - RIM
    place = lax.broadcasted_iota(jnp.int32, (LANES, LANES), 0)
    x_out = lax.broadcasted_iota(jnp.int32, (LANES, LANES), 1)

    def field_weights(distance, keep, axis):
        weight = gaussian(distance, keep(0))
        slope = DERIV_SCALE * (gaussian(distance - 1, keep(-1)) - gaussian(distance + 1, keep(1)))
        return split(jnp.concatenate([weight, slope], axis=axis))

    def x_field_weights(x_in, keep):
        high, low = field_weights(x_in - x_out, lambda step: keep & (x_out < n_cols), 1)
        return jnp.concatenate([high, high], axis=0), low

    def x_advect_weights(x_in, keep):
        high, low = split(gaussian(x_in - x_out, keep & (x_out < n_cols)))
        above = jnp.concatenate([high, low], axis=1)
        below = jnp.concatenate([high, jnp.zeros_like(low)], axis=1)
        return jnp.concatenate([above, below], axis=0)

    x_own_field = x_field_weights(place, place < n_cols)
    x_own_advect = x_advect_weights(place, (place >= 1) & (place <= n_cols - 2))
    at_east = place < LANES // 2
    x_edge = jnp.where(at_east, place + (n_cols - EDGE), place - (west_lane + RIM))
    x_edge_field = x_field_weights(
        x_edge, ((place >= EDGE) & (place <= RIM + 1)) | ((place >= west_lane) & (place < west_lane + RIM))
    )
    x_edge_advect = x_advect_weights(
        x_edge, ((place >= 1) & (place <= RIM)) | ((place > west_lane) & (place <= west_lane + RIM))
    )
    top = halo - R
    span = ceil_to(n_rows + 2 * R, 16)
    n_ext = n_rows + 2 * halo
    n_field = ext.shape[1]
    span_out = ceil_to(n_rows, 16)

    for load in loads:
        load.wait()

    row_id = lax.broadcasted_iota(jnp.int32, (n_rows, n_cols), 0)
    words = bits[...]
    word = jnp.broadcast_to(words[0:1], (n_rows, n_cols))
    bit = row_id
    for j in range(1, words.shape[0]):
        here = row_id >= j * WORD_ROWS
        word = jnp.where(here, words[j : j + 1], word)
        bit = jnp.where(here, row_id - j * WORD_ROWS, bit)
    wet = (jnp.right_shift(word, bit) & 1).astype(jnp.float32)
    for c in range(2):
        ext[c, halo : halo + n_rows, :] = jnp.zeros((n_rows, LANES), jnp.float32)
        ext[c, halo : halo + n_rows, 0:n_cols] = vel[c] * wet
        ext[c, n_rows + 2 * halo :, :] = jnp.zeros((8, LANES), jnp.float32)

    per_row = LANES // R
    deep = halo // 8
    units = 2 * deep
    group = ceil_to(units + 2, per_row) // per_row
    group_rows = group * 8
    strip_rows = strip.shape[0]
    lane = lax.broadcasted_iota(jnp.int32, (8, LANES), 1)

    def place_of(part, i):
        last = (group - 1, units % per_row * R + i)
        if part == "first":
            return divmod(i, per_row), last
        if part == "last":
            at, unit = divmod(i, per_row)
            return (group + at, unit), (group + last[0], last[1])
        last = (last[0], last[1] + units)
        if i < 2:
            return (i * group + group - 1, units % per_row + 1), last
        at, unit = divmod(i - 2, per_row)
        return (2 * group + at, unit), last

    at_west = sub == 0
    lines = [jnp.zeros((8, LANES), jnp.float32)] * (strip_rows // 8)
    for c in range(2):
        own = ext[c, halo : halo + n_rows, :]
        own = jnp.where(at_west, own, roll(own, RIM - n_cols))
        for p, part in enumerate(("first", "middle", "last")):
            for d in range(deep):
                unit = own[(p * deep + d) * 8 : (p * deep + d + 1) * 8]
                (line, at), (last_line, last) = place_of(part, c * deep + d)
                lines[line] = jnp.where(lane // R == at, roll(unit, at * R), lines[line])
                lines[last_line] = jnp.where(lane == last, roll(unit, last - R), lines[last_line])
    for i, line in enumerate(lines):
        strip[i * 8 : (i + 1) * 8, :] = line

    @pl.when(jnp.logical_not(has_up))
    def _():
        ext[:, 0:halo, :] = jnp.zeros((2, halo, LANES), jnp.float32)
        beside[:, 0:halo, :] = jnp.zeros((2, halo, LANES), jnp.float32)
        above[...] = jnp.zeros((tiles, group_rows, LANES), jnp.float32)

    @pl.when(jnp.logical_not(has_down))
    def _():
        ext[:, halo + n_rows : n_rows + 2 * halo, :] = jnp.zeros((2, halo, LANES), jnp.float32)
        beside[:, halo + n_rows :, :] = jnp.zeros((2, halo, LANES), jnp.float32)
        below[...] = jnp.zeros((tiles, group_rows, LANES), jnp.float32)

    n_beside = has_up.astype(jnp.int32) + has_down.astype(jnp.int32)
    pl.semaphore_wait(barrier, tiles + n_beside * (tiles + 1))

    def strip_copy(part, slot, k, t, r):
        source, size = ((0, strip_rows), (group_rows, group_rows), (0, group_rows))[part]
        return pltpu.make_async_remote_copy(
            src_ref=strip.at[pl.ds(source, size)],
            dst_ref=(seams, above, below)[part].at[slot],
            send_sem=strip_send.at[part, k],
            recv_sem=strip_recv.at[part, slot],
            device_id=(grp, t, r, other),
            device_id_type=MESH,
        )

    def beside_copy(part, r):
        source, size = ((halo, n_rows), (n_rows, halo), (halo, halo))[part]
        target = (halo, 0, halo + n_rows)[part]
        return pltpu.make_async_remote_copy(
            src_ref=ext.at[:, pl.ds(source, size)],
            dst_ref=beside.at[:, pl.ds(target, size)],
            send_sem=beside_send.at[part],
            recv_sem=beside_recv.at[part],
            device_id=(grp, tile, r, other),
            device_id_type=MESH,
        )

    def row_copy(part, r):
        source = (halo + n_rows - halo, halo)[part - 1]
        target = (0, halo + n_rows)[part - 1]
        return pltpu.make_async_remote_copy(
            src_ref=ext.at[:, pl.ds(source, halo)],
            dst_ref=ext.at[:, pl.ds(target, halo)],
            send_sem=row_send.at[part - 1],
            recv_sem=row_recv.at[part - 1],
            device_id=(grp, tile, r, sub),
            device_id_type=MESH,
        )

    def strip_sends(act, part, r):
        for k in reversed(range(tiles)):
            act(strip_copy(part, tile, k, lax.rem(tile + k, tiles), r))

    def first_sends(act):
        strip_sends(act, 0, row)
        act(beside_copy(0, row))
        for part, there, r in ((1, has_down, row + 1), (2, has_up, row - 1)):

            @pl.when(there)
            def _():
                act(row_copy(part, r))
                act(beside_copy(part, r))

    def rim_sends(act):
        for part, there, r in ((1, has_down, row + 1), (2, has_up, row - 1)):

            @pl.when(there)
            def _():
                strip_sends(act, part, r)

    first_sends(lambda copy: copy.start())
    rim_sends(lambda copy: copy.start())

    def y_places(length, place):
        y_out = lax.broadcasted_iota(jnp.int32, (span_out, length), 0)
        y_in = place(lax.broadcasted_iota(jnp.int32, (span_out, length), 1))

        def keep(step):
            y_global = y_in + step + row * n_rows
            return (y_global >= 0) & (y_global < rows * n_rows) & (y_out < n_rows)

        return y_in - y_out, keep

    def y_field_weights(length, place):
        return field_weights(*y_places(length, place), 0)

    def y_advect_weights(length, place):
        distance, keep = y_places(length, place)
        return split(gaussian(distance, keep(0)))

    y_all_field = y_field_weights(n_field, lambda k: k - halo)
    y_all_advect = y_advect_weights(span, lambda k: k - R)
    y_own_field = y_field_weights(n_rows, lambda k: k)
    y_own_advect = y_advect_weights(n_rows - 16, lambda k: k + 8)
    y_rim_field = y_field_weights(n_field - n_rows, lambda k: jnp.where(k < halo, k - halo, k - halo + n_rows))
    y_rim_advect = y_advect_weights(
        span - n_rows + 16, lambda k: jnp.where(k < R + 8, k - R, k - R + n_rows - 16)
    )

    west = jnp.int32(0)
    for i in range(tiles):
        west = jnp.where(face_ref[i] == tile, i, west)
    across_seam = jnp.where(at_west, west, face_ref[tile])
    east_turn = turn_ref[tile]
    west_turn = turn_ref[west]
    west_turn = jnp.where(west_turn == 0, 0, 4 - west_turn)
    turn = jnp.where(at_west, west_turn, east_turn)

    def choose(a, b):
        return jnp.where(turn == a, 1.0, jnp.where(turn == b, -1.0, 0.0)).astype(jnp.float32)

    cosine, sine = choose(0, 2), choose(1, 3)

    def derive(field, c, start, length):
        centre = field[c, start : start + length, :]
        grad_x = DERIV_SCALE * (roll(centre, -1) - roll(centre, 1))
        grad_y = DERIV_SCALE * (field[c, start + 1 : start + 1 + length, :] - field[c, start - 1 : start - 1 + length, :])
        return centre, grad_x, grad_y

    def advected(field, start, length):
        u, u_x, u_y = derive(field, 0, start, length)
        v, v_x, v_y = derive(field, 1, start, length)
        return u * u_x + v * u_y, u * v_x + v * v_y

    def along_field(value, weights):
        high, low = split(value)
        return dot(jnp.concatenate([high, low], axis=1), weights[0]) + dot(high, weights[1])

    def along_advect(value, weights):
        both = dot(jnp.concatenate(split(value), axis=1), weights)
        return both[:, :LANES] + both[:, LANES:]

    beside_copy(0, row).wait_recv()
    for part, there in ((1, has_up), (2, has_down)):

        @pl.when(there)
        def _():
            row_copy(part, row).wait_recv()
            beside_copy(part, row).wait_recv()

    def smoothed(value, weights):
        (high, low), (value_high, value_low) = weights, split(value)
        return dot(high, value_high) + (dot(high, value_low) + dot(low, value_high))

    def smooth_field(parts, x_weights, y_weights):
        return [smoothed(along_field(part, x_weights), y_weights) for part in parts]

    def smooth_advect(parts, x_weights, y_weights):
        return smoothed(jnp.concatenate([along_advect(part, x_weights) for part in parts], axis=1), y_weights)

    for c, part in enumerate(smooth_field((ext[0], ext[1]), x_own_field, y_all_field)):
        field_sum[c] = part
    advect_sum[...] = smooth_advect(advected(ext, top, span), x_own_advect, y_all_advect)
    for c in range(2):
        pooled[c] = jnp.zeros((n_rows, LANES), jnp.float32)

    lane = lax.broadcasted_iota(jnp.int32, (n_ext, LANES), 1)
    inner_at = jnp.where(at_west, EDGE, west_lane)
    in_inner = (lane >= inner_at) & (lane < inner_at + RIM)
    for c in range(2):
        own, inner = ext[c, 0:n_ext, :], beside[c]
        inner = jnp.where(at_west, roll(inner, EDGE), roll(inner, west_lane + RIM - n_cols))
        rest = jnp.where(lane >= LANES - EDGE, roll(own, -EDGE), jnp.where(in_inner, inner, 0.0))
        ring[c, 0:n_ext, :] = jnp.where(lane < EDGE, roll(own, EDGE - n_cols), rest)
        ring[c, n_ext:, :] = jnp.zeros((8, LANES), jnp.float32)

    outer_at = jnp.where(at_west, west_lane, EDGE)
    lane = lax.broadcasted_iota(jnp.int32, (8, LANES), 1)
    in_unit = lane < outer_at + R
    in_outer = (lane >= outer_at) & (lane < outer_at + RIM)

    def lines_of(strips):
        held = strips[across_seam]
        held = jnp.where(at_west, roll(held, west_lane), roll(held, EDGE))
        return [held[i * 8 : (i + 1) * 8] for i in range(held.shape[0] // 8)]

    def fill(lines, part, block):
        for d in range(deep):
            uv = []
            for c in range(2):
                (line, unit), (last_line, last) = place_of(part, c * deep + d)
                uv.append(jnp.where(in_unit, roll(lines[line], -unit * R), roll(lines[last_line], R - last)))
            turned = (cosine * uv[0] - sine * uv[1], sine * uv[0] + cosine * uv[1])
            at = slice((block * deep + d) * 8, (block * deep + d + 1) * 8)
            for c in range(2):
                ring[c, at, :] = jnp.where(in_outer, turned[c], ring[c, at, :])

    for slot in range(tiles):
        strip_copy(0, slot, 0, tile, row).wait_recv()
    lines = lines_of(seams)
    fill(lines, "first", 1)
    fill(lines, "middle", 2)
    fill(lines, "last", 3)
    own_rows = [ring[c, halo : halo + n_rows, :] for c in range(2)]
    for c, part in enumerate(smooth_field(own_rows, x_edge_field, y_own_field)):
        field_sum[c] += part
    advect_sum[...] += smooth_advect(advected(ring, halo + 8, n_rows - 16), x_edge_advect, y_own_advect)
    first_sends(lambda copy: copy.wait_send())

    for part, there in ((1, has_up), (2, has_down)):

        @pl.when(there)
        def _():
            for slot in range(tiles):
                strip_copy(part, slot, 0, tile, row).wait_recv()

    fill([None] * group + lines_of(above), "last", 0)
    fill(lines_of(below), "first", 4)
    rim = [jnp.concatenate([ring[c, 0:halo, :], ring[c, halo + n_rows :, :]], axis=0) for c in range(2)]
    smooth = []
    for c, part in enumerate(smooth_field(rim, x_edge_field, y_rim_field)):
        both = field_sum[c] + part
        smooth.append((both[:span_out, :LANES], both[:span_out, LANES:], both[span_out:, :LANES]))
    before = advected(ring, top, R + 8)
    behind = advected(ring, halo + n_rows - 8, span - n_rows + 16 - (R + 8))
    rim = [jnp.concatenate(pair, axis=0) for pair in zip(before, behind)]
    advect = advect_sum[...] + smooth_advect(rim, x_edge_advect, y_rim_advect)
    (u, u_x, u_y), (v, v_x, v_y) = smooth
    fine = (
        advect[:, :LANES] - (u * u_x + v * u_y),
        advect[:, LANES:] - (u * v_x + v * v_y),
    )

    n_out = n_rows // POOL
    m_out = n_cols // POOL
    col = lax.broadcasted_iota(jnp.int32, (LANES, m_out), 0)
    block_at = lax.broadcasted_iota(jnp.int32, (LANES, m_out), 1) * POOL
    mean = jnp.where((col >= block_at) & (col < block_at + POOL), 1.0 / POOL**2, 0.0)
    mean = mean.astype(jnp.bfloat16)
    for c in range(2):
        pooled[c, :, 0:n_cols] = fine[c][:n_rows, :n_cols] * wet
        total = pooled[c, pl.ds(0, n_out, stride=POOL), :]
        for k in range(1, POOL):
            total = total + pooled[c, pl.ds(k, n_out, stride=POOL), :]
        high, low = split(total)
        out_ref[c] = dot(high, mean) + dot(low, mean)

    rim_sends(lambda copy: copy.wait_send())


def on_device(velocity, wet_bits, east_face, seam_turn):
    _, n_rows, n_cols = velocity.shape
    tiles = lax.axis_size("tile")
    halo = ceil_to(RIM, 8)
    assert n_rows == 3 * halo and lax.axis_size("sub") == 2
    assert 2 * RIM <= n_cols <= LANES and LANES % R == 0
    per_row, units = LANES // R, 2 * halo // 8
    group_rows = ceil_to(units + 2, per_row) // per_row * 8
    strip_rows = 2 * group_rows + ceil_to(units - 2, per_row) // per_row * 8
    assert units % per_row < per_row - 1 and 2 * units <= R
    n_ext = n_rows + 2 * halo
    f32 = jnp.float32
    return pl.pallas_call(
        kernel,
        out_shape=pltpu.VMEM((2, n_rows // POOL, n_cols // POOL), f32),
        in_specs=[pl.BlockSpec(memory_space=pltpu.HBM)] * 4,
        out_specs=pl.BlockSpec(memory_space=pltpu.VMEM),
        scratch_shapes=[
            pltpu.SMEM(east_face.shape, jnp.int32),
            pltpu.SMEM(seam_turn.shape, jnp.int32),
            pltpu.VMEM(velocity.shape, f32),
            pltpu.VMEM(wet_bits.shape, jnp.int32),
            pltpu.VMEM((2, n_ext + 8, LANES), f32),
            pltpu.VMEM((strip_rows, LANES), f32),
            pltpu.VMEM((tiles, strip_rows, LANES), f32),
            pltpu.VMEM((tiles, group_rows, LANES), f32),
            pltpu.VMEM((tiles, group_rows, LANES), f32),
            pltpu.VMEM((2, n_ext, LANES), f32),
            pltpu.VMEM((2, n_ext + 8, LANES), f32),
            pltpu.VMEM((2, 2 * ceil_to(n_rows, 16), 2 * LANES), f32),
            pltpu.VMEM((ceil_to(n_rows, 16), 2 * LANES), f32),
            pltpu.VMEM((2, n_rows, LANES), f32),
            pltpu.SemaphoreType.DMA((4,)),
            pltpu.SemaphoreType.DMA((2,)),
            pltpu.SemaphoreType.DMA((2,)),
            pltpu.SemaphoreType.DMA((3,)),
            pltpu.SemaphoreType.DMA((3,)),
        ]
        + [pltpu.SemaphoreType.DMA((3, tiles))] * 2,
        compiler_params=pltpu.CompilerParams(
            collective_id=0, has_side_effects=True, vmem_limit_bytes=60 * 1024 * 1024
        ),
    )(east_face, seam_turn, velocity, wet_bits)


def solution(mesh):
    placed = (
        P(None, ("grp", "row"), ("tile", "sub")),
        P(("grp", "row"), ("tile", "sub")),
        P(),
        P(),
    )
    return jax.shard_map(
        on_device,
        mesh=mesh,
        in_specs=placed,
        out_specs=P(None, ("grp", "row"), ("tile", "sub")),
        check_vma=False,
    )
```

```python
import functools
import math

import jax
import jax.numpy as jnp
from jax import lax
from jax.experimental import pallas as pl
from jax.experimental.pallas import tpu as pltpu
from jax.sharding import PartitionSpec as P

R = 32
RIM = R + 1
LANES = 128
EDGE = 2
DERIV_SCALE = 8.0
POOL = 4
WORD_ROWS = 30
MESH = pl.DeviceIdType.MESH

WEIGHT_SUM = sum(math.exp(-0.5 * (k / R) ** 2) for k in range(-R, R + 1))


def ceil_to(value, step):
    return -(-value // step) * step


def gaussian(distance, keep):
    d = distance.astype(jnp.float32) * (1.0 / R)
    weight = jnp.exp(-0.5 * d * d) * (1.0 / WEIGHT_SUM)
    return jnp.where(keep & (jnp.abs(distance) <= R), weight, 0.0)


def split(value):
    high = value.astype(jnp.bfloat16)
    low = (value - high.astype(jnp.float32)).astype(jnp.bfloat16)
    return high, low


def dot(a, b):
    return jnp.dot(a, b, preferred_element_type=jnp.float32)


def roll(value, shift, axis=1):
    size = value.shape[axis]
    shift = shift % size
    return value if shift == 0 else pltpu.roll(value, shift, axis)


def kernel(
    face_hbm, turn_hbm, vel_hbm, bits_hbm, out_ref,
    face_ref, turn_ref, vel, bits, ext, strip, seams, above, below, beside,
    ring, inner_field, inner_advect, pooled,
    load_sem, row_send, row_recv, beside_send, beside_recv, strip_send, strip_recv,
):
    tiles, rows = lax.axis_size("tile"), lax.axis_size("row")
    grp, tile, row, sub = (lax.axis_index(a) for a in ("grp", "tile", "row", "sub"))
    n_rows, n_cols = vel.shape[1], vel.shape[2]
    halo = ceil_to(RIM, 8)
    has_up, has_down = row > 0, row < rows - 1
    other = 1 - sub

    loads = [
        pltpu.make_async_copy(vel_hbm, vel, load_sem.at[0]),
        pltpu.make_async_copy(bits_hbm, bits, load_sem.at[1]),
        pltpu.make_async_copy(face_hbm, face_ref, load_sem.at[2]),
        pltpu.make_async_copy(turn_hbm, turn_ref, load_sem.at[3]),
    ]
    for load in loads:
        load.start()

    barrier = pltpu.get_barrier_semaphore()

    def greet(t, r, s):
        pl.semaphore_signal(barrier, inc=1, device_id=(grp, t, r, s), device_id_type=MESH)

    in_left = tile < tiles // 2
    far_first = [jnp.where(in_left, tiles - 1 - k, k) for k in range(tiles)]
    for t in far_first:
        greet(t, row, other)
        for there, r in ((has_up, row - 1), (has_down, row + 1)):

            @pl.when(there)
            def _():
                greet(t, r, other)

    for there, r in ((has_up, row - 1), (has_down, row + 1)):

        @pl.when(there)
        def _():
            greet(tile, r, sub)

    west_lane = LANES - EDGE - RIM
    place = lax.broadcasted_iota(jnp.int32, (LANES, LANES), 0)
    x_out = lax.broadcasted_iota(jnp.int32, (LANES, LANES), 1)

    def field_weights(distance, keep, axis):
        weight = gaussian(distance, keep(0))
        slope = DERIV_SCALE * (gaussian(distance - 1, keep(-1)) - gaussian(distance + 1, keep(1)))
        return split(jnp.concatenate([weight, slope], axis=axis))

    def x_field_weights(x_in, keep):
        high, low = field_weights(x_in - x_out, lambda step: keep & (x_out < n_cols), 1)
        return jnp.concatenate([high, high], axis=0), low

    def x_advect_weights(x_in, keep):
        high, low = split(gaussian(x_in - x_out, keep & (x_out < n_cols)))
        above = jnp.concatenate([high, low], axis=1)
        below = jnp.concatenate([high, jnp.zeros_like(low)], axis=1)
        return jnp.concatenate([above, below], axis=0)

    x_own_field = x_field_weights(place, place < n_cols)
    x_own_advect = x_advect_weights(place, (place >= 1) & (place <= n_cols - 2))
    at_east = place < LANES // 2
    x_edge = jnp.where(at_east, place + (n_cols - EDGE), place - (west_lane + RIM))
    x_edge_field = x_field_weights(
        x_edge, ((place >= EDGE) & (place <= RIM + 1)) | ((place >= west_lane) & (place < west_lane + RIM))
    )
    x_edge_advect = x_advect_weights(
        x_edge, ((place >= 1) & (place <= RIM)) | ((place > west_lane) & (place <= west_lane + RIM))
    )
    top = halo - R
    span = ceil_to(n_rows + 2 * R, 16)
    n_ext = n_rows + 2 * halo
    n_field = ext.shape[1]
    span_out = ceil_to(n_rows, 16)

    def y_places(length, start):
        y_out = lax.broadcasted_iota(jnp.int32, (span_out, length), 0)
        y_in = lax.broadcasted_iota(jnp.int32, (span_out, length), 1) + start

        def keep(step):
            y_global = y_in + step + row * n_rows
            return (y_global >= 0) & (y_global < rows * n_rows) & (y_out < n_rows)

        return y_in - y_out, keep

    y_field_high, y_field_low = field_weights(*y_places(n_field, -halo), 0)
    distance, keep = y_places(span, -R)
    y_high, y_low = split(gaussian(distance, keep(0)))

    for load in loads:
        load.wait()

    row_id = lax.broadcasted_iota(jnp.int32, (n_rows, n_cols), 0)
    words = bits[...]
    word = jnp.broadcast_to(words[0:1], (n_rows, n_cols))
    bit = row_id
    for j in range(1, words.shape[0]):
        here = row_id >= j * WORD_ROWS
        word = jnp.where(here, words[j : j + 1], word)
        bit = jnp.where(here, row_id - j * WORD_ROWS, bit)
    wet = (jnp.right_shift(word, bit) & 1).astype(jnp.float32)
    for c in range(2):
        ext[c, halo : halo + n_rows, :] = jnp.zeros((n_rows, LANES), jnp.float32)
        ext[c, halo : halo + n_rows, 0:n_cols] = vel[c] * wet
        ext[c, n_rows + 2 * halo :, :] = jnp.zeros((8, LANES), jnp.float32)

    per_row = LANES // R
    deep = halo // 8
    units = 2 * deep
    group = ceil_to(units + 2, per_row) // per_row
    group_rows = group * 8
    strip_rows = strip.shape[0]
    lane = lax.broadcasted_iota(jnp.int32, (8, LANES), 1)

    def place_of(part, i):
        last = (group - 1, units % per_row * R + i)
        if part == "first":
            return divmod(i, per_row), last
        if part == "last":
            at, unit = divmod(i, per_row)
            return (group + at, unit), (group + last[0], last[1])
        last = (last[0], last[1] + units)
        if i < 2:
            return (i * group + group - 1, units % per_row + 1), last
        at, unit = divmod(i - 2, per_row)
        return (2 * group + at, unit), last

    at_west = sub == 0
    lines = [jnp.zeros((8, LANES), jnp.float32)] * (strip_rows // 8)
    for c in range(2):
        own = ext[c, halo : halo + n_rows, :]
        own = jnp.where(at_west, own, roll(own, RIM - n_cols))
        for p, part in enumerate(("first", "middle", "last")):
            for d in range(deep):
                unit = own[(p * deep + d) * 8 : (p * deep + d + 1) * 8]
                (line, at), (last_line, last) = place_of(part, c * deep + d)
                lines[line] = jnp.where(lane // R == at, roll(unit, at * R), lines[line])
                lines[last_line] = jnp.where(lane == last, roll(unit, last - R), lines[last_line])
    for i, line in enumerate(lines):
        strip[i * 8 : (i + 1) * 8, :] = line

    @pl.when(jnp.logical_not(has_up))
    def _():
        ext[:, 0:halo, :] = jnp.zeros((2, halo, LANES), jnp.float32)
        beside[:, 0:halo, :] = jnp.zeros((2, halo, LANES), jnp.float32)
        above[...] = jnp.zeros((tiles, group_rows, LANES), jnp.float32)

    @pl.when(jnp.logical_not(has_down))
    def _():
        ext[:, halo + n_rows : n_rows + 2 * halo, :] = jnp.zeros((2, halo, LANES), jnp.float32)
        beside[:, halo + n_rows :, :] = jnp.zeros((2, halo, LANES), jnp.float32)
        below[...] = jnp.zeros((tiles, group_rows, LANES), jnp.float32)

    n_beside = has_up.astype(jnp.int32) + has_down.astype(jnp.int32)
    pl.semaphore_wait(barrier, tiles + n_beside * (tiles + 1))

    def strip_copy(part, slot, k, t, r):
        source, size = ((0, strip_rows), (group_rows, group_rows), (0, group_rows))[part]
        return pltpu.make_async_remote_copy(
            src_ref=strip.at[pl.ds(source, size)],
            dst_ref=(seams, above, below)[part].at[slot],
            send_sem=strip_send.at[part, k],
            recv_sem=strip_recv.at[part, slot],
            device_id=(grp, t, r, other),
            device_id_type=MESH,
        )

    def beside_copy(part, r):
        source, size = ((halo, n_rows), (n_rows, halo), (halo, halo))[part]
        target = (halo, 0, halo + n_rows)[part]
        return pltpu.make_async_remote_copy(
            src_ref=ext.at[:, pl.ds(source, size)],
            dst_ref=beside.at[:, pl.ds(target, size)],
            send_sem=beside_send.at[part],
            recv_sem=beside_recv.at[part],
            device_id=(grp, tile, r, other),
            device_id_type=MESH,
        )

    def row_copy(part, r):
        source = (halo + n_rows - halo, halo)[part - 1]
        target = (0, halo + n_rows)[part - 1]
        return pltpu.make_async_remote_copy(
            src_ref=ext.at[:, pl.ds(source, halo)],
            dst_ref=ext.at[:, pl.ds(target, halo)],
            send_sem=row_send.at[part - 1],
            recv_sem=row_recv.at[part - 1],
            device_id=(grp, tile, r, sub),
            device_id_type=MESH,
        )

    def strip_sends(act, part, r):
        for k, t in enumerate(far_first):
            act(strip_copy(part, tile, k, t, r))

    def all_sends(act):
        strip_sends(act, 0, row)
        act(beside_copy(0, row))
        for part, there, r in ((1, has_down, row + 1), (2, has_up, row - 1)):

            @pl.when(there)
            def _():
                act(row_copy(part, r))
                act(beside_copy(part, r))
                strip_sends(act, part, r)

    all_sends(lambda copy: copy.start())

    west = jnp.int32(0)
    for i in range(tiles):
        west = jnp.where(face_ref[i] == tile, i, west)
    across_seam = jnp.where(at_west, west, face_ref[tile])
    east_turn = turn_ref[tile]
    west_turn = turn_ref[west]
    west_turn = jnp.where(west_turn == 0, 0, 4 - west_turn)
    turn = jnp.where(at_west, west_turn, east_turn)

    def choose(a, b):
        return jnp.where(turn == a, 1.0, jnp.where(turn == b, -1.0, 0.0)).astype(jnp.float32)

    cosine, sine = choose(0, 2), choose(1, 3)

    def derive(field, c, start, length):
        centre = field[c, start : start + length, :]
        grad_x = DERIV_SCALE * (roll(centre, -1) - roll(centre, 1))
        grad_y = DERIV_SCALE * (field[c, start + 1 : start + 1 + length, :] - field[c, start - 1 : start - 1 + length, :])
        return centre, grad_x, grad_y

    def advected(field, start, length):
        u, u_x, u_y = derive(field, 0, start, length)
        v, v_x, v_y = derive(field, 1, start, length)
        return u * u_x + v * u_y, u * v_x + v * v_y

    def along_field(value, weights):
        high, low = split(value)
        return dot(jnp.concatenate([high, low], axis=1), weights[0]) + dot(high, weights[1])

    def along_advect(value, weights):
        both = dot(jnp.concatenate(split(value), axis=1), weights)
        return both[:, :LANES] + both[:, LANES:]

    beside_copy(0, row).wait_recv()
    for part, there in ((1, has_up), (2, has_down)):

        @pl.when(there)
        def _():
            row_copy(part, row).wait_recv()
            beside_copy(part, row).wait_recv()

    for c, advect in enumerate(advected(ext, top, span)):
        inner_field[c] = along_field(ext[c], x_own_field)
        inner_advect[c] = along_advect(advect, x_own_advect)

    lane = lax.broadcasted_iota(jnp.int32, (n_ext, LANES), 1)
    inner_at = jnp.where(at_west, EDGE, west_lane)
    in_inner = (lane >= inner_at) & (lane < inner_at + RIM)
    for c in range(2):
        own, inner = ext[c, 0:n_ext, :], beside[c]
        inner = jnp.where(at_west, roll(inner, EDGE), roll(inner, west_lane + RIM - n_cols))
        rest = jnp.where(lane >= LANES - EDGE, roll(own, -EDGE), jnp.where(in_inner, inner, 0.0))
        ring[c, 0:n_ext, :] = jnp.where(lane < EDGE, roll(own, EDGE - n_cols), rest)
        ring[c, n_ext:, :] = jnp.zeros((8, LANES), jnp.float32)

    outer_at = jnp.where(at_west, west_lane, EDGE)
    lane = lax.broadcasted_iota(jnp.int32, (8, LANES), 1)
    in_unit = lane < outer_at + R
    in_outer = (lane >= outer_at) & (lane < outer_at + RIM)

    def lines_of(strips):
        held = strips[across_seam]
        held = jnp.where(at_west, roll(held, west_lane), roll(held, EDGE))
        return [held[i * 8 : (i + 1) * 8] for i in range(held.shape[0] // 8)]

    def fill(lines, part, block):
        for d in range(deep):
            uv = []
            for c in range(2):
                (line, unit), (last_line, last) = place_of(part, c * deep + d)
                uv.append(jnp.where(in_unit, roll(lines[line], -unit * R), roll(lines[last_line], R - last)))
            turned = (cosine * uv[0] - sine * uv[1], sine * uv[0] + cosine * uv[1])
            at = slice((block * deep + d) * 8, (block * deep + d + 1) * 8)
            for c in range(2):
                ring[c, at, :] = jnp.where(in_outer, turned[c], ring[c, at, :])

    def add_field(start, length):
        for c in range(2):
            inner_field[c, start : start + length, :] += along_field(ring[c, start : start + length, :], x_edge_field)

    def add_advect(start, length):
        for c, advect in enumerate(advected(ring, start, length)):
            inner_advect[c, start - top : start - top + length, :] += along_advect(advect, x_edge_advect)

    for slot in range(tiles):
        strip_copy(0, slot, 0, tile, row).wait_recv()
    lines = lines_of(seams)
    fill(lines, "first", 1)
    fill(lines, "middle", 2)
    fill(lines, "last", 3)
    add_field(halo, n_rows)
    add_advect(halo + 8, n_rows - 16)

    for part, there in ((1, has_up), (2, has_down)):

        @pl.when(there)
        def _():
            for slot in range(tiles):
                strip_copy(part, slot, 0, tile, row).wait_recv()

    fill([None] * group + lines_of(above), "last", 0)
    fill(lines_of(below), "first", 4)
    add_field(0, halo)
    add_field(halo + n_rows, n_field - halo - n_rows)
    add_advect(top, halo + 8 - top)
    add_advect(halo + n_rows - 8, top + span - (halo + n_rows - 8))

    def smoothed(value, high, low):
        value_high, value_low = split(value)
        return dot(high, value_high) + (dot(high, value_low) + dot(low, value_high))

    smooth = []
    for c in range(2):
        both = smoothed(inner_field[c], y_field_high, y_field_low)
        smooth.append((both[:span_out, :LANES], both[:span_out, LANES:], both[span_out:, :LANES]))
    advect = smoothed(jnp.concatenate([inner_advect[0], inner_advect[1]], axis=1), y_high, y_low)
    (u, u_x, u_y), (v, v_x, v_y) = smooth
    fine = (
        advect[:, :LANES] - (u * u_x + v * u_y),
        advect[:, LANES:] - (u * v_x + v * v_y),
    )

    n_out = n_rows // POOL
    m_out = n_cols // POOL
    col = lax.broadcasted_iota(jnp.int32, (LANES, m_out), 0)
    block_at = lax.broadcasted_iota(jnp.int32, (LANES, m_out), 1) * POOL
    mean = jnp.where((col >= block_at) & (col < block_at + POOL), 1.0 / POOL**2, 0.0)
    mean = mean.astype(jnp.bfloat16)
    for c in range(2):
        pooled[c] = jnp.zeros((n_rows, LANES), jnp.float32)
        pooled[c, :, 0:n_cols] = fine[c][:n_rows, :n_cols] * wet
        total = pooled[c, pl.ds(0, n_out, stride=POOL), :]
        for k in range(1, POOL):
            total = total + pooled[c, pl.ds(k, n_out, stride=POOL), :]
        high, low = split(total)
        out_ref[c] = dot(high, mean) + dot(low, mean)

    all_sends(lambda copy: copy.wait_send())


def on_device(velocity, wet_bits, east_face, seam_turn):
    _, n_rows, n_cols = velocity.shape
    tiles = lax.axis_size("tile")
    halo = ceil_to(RIM, 8)
    assert n_rows == 3 * halo and lax.axis_size("sub") == 2
    assert 2 * RIM <= n_cols <= LANES and LANES % R == 0
    per_row, units = LANES // R, 2 * halo // 8
    group_rows = ceil_to(units + 2, per_row) // per_row * 8
    strip_rows = 2 * group_rows + ceil_to(units - 2, per_row) // per_row * 8
    assert units % per_row < per_row - 1 and 2 * units <= R
    n_ext = n_rows + 2 * halo
    f32 = jnp.float32
    return pl.pallas_call(
        kernel,
        out_shape=pltpu.VMEM((2, n_rows // POOL, n_cols // POOL), f32),
        in_specs=[pl.BlockSpec(memory_space=pltpu.HBM)] * 4,
        out_specs=pl.BlockSpec(memory_space=pltpu.VMEM),
        scratch_shapes=[
            pltpu.SMEM(east_face.shape, jnp.int32),
            pltpu.SMEM(seam_turn.shape, jnp.int32),
            pltpu.VMEM(velocity.shape, f32),
            pltpu.VMEM(wet_bits.shape, jnp.int32),
            pltpu.VMEM((2, n_ext + 8, LANES), f32),
            pltpu.VMEM((strip_rows, LANES), f32),
            pltpu.VMEM((tiles, strip_rows, LANES), f32),
            pltpu.VMEM((tiles, group_rows, LANES), f32),
            pltpu.VMEM((tiles, group_rows, LANES), f32),
            pltpu.VMEM((2, n_ext, LANES), f32),
            pltpu.VMEM((2, n_ext + 8, LANES), f32),
            pltpu.VMEM((2, n_ext + 8, 2 * LANES), f32),
            pltpu.VMEM((2, ceil_to(n_rows + 2 * R, 16), LANES), f32),
            pltpu.VMEM((2, n_rows, LANES), f32),
            pltpu.SemaphoreType.DMA((4,)),
            pltpu.SemaphoreType.DMA((2,)),
            pltpu.SemaphoreType.DMA((2,)),
            pltpu.SemaphoreType.DMA((3,)),
            pltpu.SemaphoreType.DMA((3,)),
        ]
        + [pltpu.SemaphoreType.DMA((3, tiles))] * 2,
        compiler_params=pltpu.CompilerParams(
            collective_id=0, has_side_effects=True, vmem_limit_bytes=60 * 1024 * 1024
        ),
    )(east_face, seam_turn, velocity, wet_bits)


def solution(mesh):
    placed = (
        P(None, ("grp", "row"), ("tile", "sub")),
        P(("grp", "row"), ("tile", "sub")),
        P(),
        P(),
    )
    return jax.shard_map(
        on_device,
        mesh=mesh,
        in_specs=placed,
        out_specs=P(None, ("grp", "row"), ("tile", "sub")),
        check_vma=False,
    )
```

```python
import functools
import math

import jax
import jax.numpy as jnp
from jax import lax
from jax.experimental import pallas as pl
from jax.experimental.pallas import tpu as pltpu
from jax.sharding import PartitionSpec as P

R = 32
RIM = R + 1
LANES = 128
EDGE = 2
DERIV_SCALE = 8.0
POOL = 4
WORD_ROWS = 30
MESH = pl.DeviceIdType.MESH

WEIGHT_SUM = sum(math.exp(-0.5 * (k / R) ** 2) for k in range(-R, R + 1))


def ceil_to(value, step):
    return -(-value // step) * step


def gaussian(distance, keep):
    d = distance.astype(jnp.float32) * (1.0 / R)
    weight = jnp.exp(-0.5 * d * d) * (1.0 / WEIGHT_SUM)
    return jnp.where(keep & (jnp.abs(distance) <= R), weight, 0.0)


def split(value):
    high = value.astype(jnp.bfloat16)
    low = (value - high.astype(jnp.float32)).astype(jnp.bfloat16)
    return high, low


def dot(a, b):
    return jnp.dot(a, b, preferred_element_type=jnp.float32)


def roll(value, shift, axis=1):
    size = value.shape[axis]
    shift = shift % size
    return value if shift == 0 else pltpu.roll(value, shift, axis)


def kernel(
    face_hbm, turn_hbm, vel_hbm, bits_hbm, out_ref,
    face_ref, turn_ref, vel, bits, ext, strip, seams, above, below, beside,
    ring, field_sum, advect_sum, pooled,
    load_sem, row_send, row_recv, beside_send, beside_recv, strip_send, strip_recv,
):
    tiles, rows = lax.axis_size("tile"), lax.axis_size("row")
    grp, tile, row, sub = (lax.axis_index(a) for a in ("grp", "tile", "row", "sub"))
    n_rows, n_cols = vel.shape[1], vel.shape[2]
    halo = ceil_to(RIM, 8)
    has_up, has_down = row > 0, row < rows - 1
    other = 1 - sub

    barrier = pltpu.get_barrier_semaphore()

    def greet(t, r, s):
        pl.semaphore_signal(barrier, inc=1, device_id=(grp, t, r, s), device_id_type=MESH)

    in_left = tile < tiles // 2
    far_first = [jnp.where(in_left, tiles - 1 - k, k) for k in range(tiles)]
    for t in far_first:
        greet(t, row, other)
        for there, r in ((has_up, row - 1), (has_down, row + 1)):

            @pl.when(there)
            def _():
                greet(t, r, other)

    for there, r in ((has_up, row - 1), (has_down, row + 1)):

        @pl.when(there)
        def _():
            greet(tile, r, sub)

    loads = [
        pltpu.make_async_copy(vel_hbm, vel, load_sem.at[0]),
        pltpu.make_async_copy(bits_hbm, bits, load_sem.at[1]),
        pltpu.make_async_copy(face_hbm, face_ref, load_sem.at[2]),
        pltpu.make_async_copy(turn_hbm, turn_ref, load_sem.at[3]),
    ]
    for load in loads:
        load.start()

    west_lane = LANES - EDGE - RIM
    place = lax.broadcasted_iota(jnp.int32, (LANES, LANES), 0)
    x_out = lax.broadcasted_iota(jnp.int32, (LANES, LANES), 1)

    def field_weights(distance, keep, axis):
        weight = gaussian(distance, keep(0))
        slope = DERIV_SCALE * (gaussian(distance - 1, keep(-1)) - gaussian(distance + 1, keep(1)))
        return split(jnp.concatenate([weight, slope], axis=axis))

    def x_field_weights(x_in, keep):
        high, low = field_weights(x_in - x_out, lambda step: keep & (x_out < n_cols), 1)
        return jnp.concatenate([high, high], axis=0), low

    def x_advect_weights(x_in, keep):
        high, low = split(gaussian(x_in - x_out, keep & (x_out < n_cols)))
        above = jnp.concatenate([high, low], axis=1)
        below = jnp.concatenate([high, jnp.zeros_like(low)], axis=1)
        return jnp.concatenate([above, below], axis=0)

    x_own_field = x_field_weights(place, place < n_cols)
    x_own_advect = x_advect_weights(place, (place >= 1) & (place <= n_cols - 2))
    at_east = place < LANES // 2
    x_edge = jnp.where(at_east, place + (n_cols - EDGE), place - (west_lane + RIM))
    x_edge_field = x_field_weights(
        x_edge, ((place >= EDGE) & (place <= RIM + 1)) | ((place >= west_lane) & (place < west_lane + RIM))
    )
    x_edge_advect = x_advect_weights(
        x_edge, ((place >= 1) & (place <= RIM)) | ((place > west_lane) & (place <= west_lane + RIM))
    )
    top = halo - R
    span = ceil_to(n_rows + 2 * R, 16)
    n_ext = n_rows + 2 * halo
    n_field = ext.shape[1]
    span_out = ceil_to(n_rows, 16)

    for load in loads:
        load.wait()

    row_id = lax.broadcasted_iota(jnp.int32, (n_rows, n_cols), 0)
    words = bits[...]
    word = jnp.broadcast_to(words[0:1], (n_rows, n_cols))
    bit = row_id
    for j in range(1, words.shape[0]):
        here = row_id >= j * WORD_ROWS
        word = jnp.where(here, words[j : j + 1], word)
        bit = jnp.where(here, row_id - j * WORD_ROWS, bit)
    wet = (jnp.right_shift(word, bit) & 1).astype(jnp.float32)
    for c in range(2):
        ext[c, halo : halo + n_rows, :] = jnp.zeros((n_rows, LANES), jnp.float32)
        ext[c, halo : halo + n_rows, 0:n_cols] = vel[c] * wet
        ext[c, n_rows + 2 * halo :, :] = jnp.zeros((8, LANES), jnp.float32)

    per_row = LANES // R
    deep = halo // 8
    units = 2 * deep
    group = ceil_to(units + 2, per_row) // per_row
    group_rows = group * 8
    strip_rows = strip.shape[0]
    lane = lax.broadcasted_iota(jnp.int32, (8, LANES), 1)

    def place_of(part, i):
        last = (group - 1, units % per_row * R + i)
        if part == "first":
            return divmod(i, per_row), last
        if part == "last":
            at, unit = divmod(i, per_row)
            return (group + at, unit), (group + last[0], last[1])
        last = (last[0], last[1] + units)
        if i < 2:
            return (i * group + group - 1, units % per_row + 1), last
        at, unit = divmod(i - 2, per_row)
        return (2 * group + at, unit), last

    at_west = sub == 0
    lines = [jnp.zeros((8, LANES), jnp.float32)] * (strip_rows // 8)
    for c in range(2):
        own = ext[c, halo : halo + n_rows, :]
        own = jnp.where(at_west, own, roll(own, RIM - n_cols))
        for p, part in enumerate(("first", "middle", "last")):
            for d in range(deep):
                unit = own[(p * deep + d) * 8 : (p * deep + d + 1) * 8]
                (line, at), (last_line, last) = place_of(part, c * deep + d)
                lines[line] = jnp.where(lane // R == at, roll(unit, at * R), lines[line])
                lines[last_line] = jnp.where(lane == last, roll(unit, last - R), lines[last_line])
    for i, line in enumerate(lines):
        strip[i * 8 : (i + 1) * 8, :] = line

    @pl.when(jnp.logical_not(has_up))
    def _():
        ext[:, 0:halo, :] = jnp.zeros((2, halo, LANES), jnp.float32)
        beside[:, 0:halo, :] = jnp.zeros((2, halo, LANES), jnp.float32)
        above[...] = jnp.zeros((tiles, group_rows, LANES), jnp.float32)

    @pl.when(jnp.logical_not(has_down))
    def _():
        ext[:, halo + n_rows : n_rows + 2 * halo, :] = jnp.zeros((2, halo, LANES), jnp.float32)
        beside[:, halo + n_rows :, :] = jnp.zeros((2, halo, LANES), jnp.float32)
        below[...] = jnp.zeros((tiles, group_rows, LANES), jnp.float32)

    n_beside = has_up.astype(jnp.int32) + has_down.astype(jnp.int32)
    pl.semaphore_wait(barrier, tiles + n_beside * (tiles + 1))

    def strip_copy(part, slot, k, t, r):
        source, size = ((0, strip_rows), (group_rows, group_rows), (0, group_rows))[part]
        return pltpu.make_async_remote_copy(
            src_ref=strip.at[pl.ds(source, size)],
            dst_ref=(seams, above, below)[part].at[slot],
            send_sem=strip_send.at[part, k],
            recv_sem=strip_recv.at[part, slot],
            device_id=(grp, t, r, other),
            device_id_type=MESH,
        )

    def beside_copy(part, r):
        source, size = ((halo, n_rows), (n_rows, halo), (halo, halo))[part]
        target = (halo, 0, halo + n_rows)[part]
        return pltpu.make_async_remote_copy(
            src_ref=ext.at[:, pl.ds(source, size)],
            dst_ref=beside.at[:, pl.ds(target, size)],
            send_sem=beside_send.at[part],
            recv_sem=beside_recv.at[part],
            device_id=(grp, tile, r, other),
            device_id_type=MESH,
        )

    def row_copy(part, r):
        source = (halo + n_rows - halo, halo)[part - 1]
        target = (0, halo + n_rows)[part - 1]
        return pltpu.make_async_remote_copy(
            src_ref=ext.at[:, pl.ds(source, halo)],
            dst_ref=ext.at[:, pl.ds(target, halo)],
            send_sem=row_send.at[part - 1],
            recv_sem=row_recv.at[part - 1],
            device_id=(grp, tile, r, sub),
            device_id_type=MESH,
        )

    def strip_sends(act, part, r):
        for k, t in enumerate(far_first):
            act(strip_copy(part, tile, k, t, r))

    def first_sends(act):
        strip_sends(act, 0, row)
        act(beside_copy(0, row))
        for part, there, r in ((1, has_down, row + 1), (2, has_up, row - 1)):

            @pl.when(there)
            def _():
                act(row_copy(part, r))
                act(beside_copy(part, r))

    def rim_sends(act):
        for part, there, r in ((1, has_down, row + 1), (2, has_up, row - 1)):

            @pl.when(there)
            def _():
                strip_sends(act, part, r)

    first_sends(lambda copy: copy.start())
    rim_sends(lambda copy: copy.start())

    def y_places(length, place):
        y_out = lax.broadcasted_iota(jnp.int32, (span_out, length), 0)
        y_in = place(lax.broadcasted_iota(jnp.int32, (span_out, length), 1))

        def keep(step):
            y_global = y_in + step + row * n_rows
            return (y_global >= 0) & (y_global < rows * n_rows) & (y_out < n_rows)

        return y_in - y_out, keep

    def y_field_weights(length, place):
        return field_weights(*y_places(length, place), 0)

    def y_advect_weights(length, place):
        distance, keep = y_places(length, place)
        return split(gaussian(distance, keep(0)))

    y_all_field = y_field_weights(n_field, lambda k: k - halo)
    y_all_advect = y_advect_weights(span, lambda k: k - R)
    y_own_field = y_field_weights(n_rows, lambda k: k)
    y_own_advect = y_advect_weights(n_rows - 16, lambda k: k + 8)
    y_rim_field = y_field_weights(n_field - n_rows, lambda k: jnp.where(k < halo, k - halo, k - halo + n_rows))
    y_rim_advect = y_advect_weights(
        span - n_rows + 16, lambda k: jnp.where(k < R + 8, k - R, k - R + n_rows - 16)
    )

    west = jnp.int32(0)
    for i in range(tiles):
        west = jnp.where(face_ref[i] == tile, i, west)
    across_seam = jnp.where(at_west, west, face_ref[tile])
    east_turn = turn_ref[tile]
    west_turn = turn_ref[west]
    west_turn = jnp.where(west_turn == 0, 0, 4 - west_turn)
    turn = jnp.where(at_west, west_turn, east_turn)

    def choose(a, b):
        return jnp.where(turn == a, 1.0, jnp.where(turn == b, -1.0, 0.0)).astype(jnp.float32)

    cosine, sine = choose(0, 2), choose(1, 3)

    def derive(field, c, start, length):
        centre = field[c, start : start + length, :]
        grad_x = DERIV_SCALE * (roll(centre, -1) - roll(centre, 1))
        grad_y = DERIV_SCALE * (field[c, start + 1 : start + 1 + length, :] - field[c, start - 1 : start - 1 + length, :])
        return centre, grad_x, grad_y

    def advected(field, start, length):
        u, u_x, u_y = derive(field, 0, start, length)
        v, v_x, v_y = derive(field, 1, start, length)
        return u * u_x + v * u_y, u * v_x + v * v_y

    def along_field(value, weights):
        high, low = split(value)
        return dot(jnp.concatenate([high, low], axis=1), weights[0]) + dot(high, weights[1])

    def along_advect(value, weights):
        both = dot(jnp.concatenate(split(value), axis=1), weights)
        return both[:, :LANES] + both[:, LANES:]

    beside_copy(0, row).wait_recv()
    for part, there in ((1, has_up), (2, has_down)):

        @pl.when(there)
        def _():
            row_copy(part, row).wait_recv()
            beside_copy(part, row).wait_recv()

    def smoothed(value, weights):
        (high, low), (value_high, value_low) = weights, split(value)
        return dot(high, value_high) + (dot(high, value_low) + dot(low, value_high))

    def smooth_field(parts, x_weights, y_weights):
        return [smoothed(along_field(part, x_weights), y_weights) for part in parts]

    def smooth_advect(parts, x_weights, y_weights):
        return smoothed(jnp.concatenate([along_advect(part, x_weights) for part in parts], axis=1), y_weights)

    for c, part in enumerate(smooth_field((ext[0], ext[1]), x_own_field, y_all_field)):
        field_sum[c] = part
    advect_sum[...] = smooth_advect(advected(ext, top, span), x_own_advect, y_all_advect)
    for c in range(2):
        pooled[c] = jnp.zeros((n_rows, LANES), jnp.float32)

    lane = lax.broadcasted_iota(jnp.int32, (n_ext, LANES), 1)
    inner_at = jnp.where(at_west, EDGE, west_lane)
    in_inner = (lane >= inner_at) & (lane < inner_at + RIM)
    for c in range(2):
        own, inner = ext[c, 0:n_ext, :], beside[c]
        inner = jnp.where(at_west, roll(inner, EDGE), roll(inner, west_lane + RIM - n_cols))
        rest = jnp.where(lane >= LANES - EDGE, roll(own, -EDGE), jnp.where(in_inner, inner, 0.0))
        ring[c, 0:n_ext, :] = jnp.where(lane < EDGE, roll(own, EDGE - n_cols), rest)
        ring[c, n_ext:, :] = jnp.zeros((8, LANES), jnp.float32)

    outer_at = jnp.where(at_west, west_lane, EDGE)
    lane = lax.broadcasted_iota(jnp.int32, (8, LANES), 1)
    in_unit = lane < outer_at + R
    in_outer = (lane >= outer_at) & (lane < outer_at + RIM)

    def lines_of(strips):
        held = strips[across_seam]
        held = jnp.where(at_west, roll(held, west_lane), roll(held, EDGE))
        return [held[i * 8 : (i + 1) * 8] for i in range(held.shape[0] // 8)]

    def fill(lines, part, block):
        for d in range(deep):
            uv = []
            for c in range(2):
                (line, unit), (last_line, last) = place_of(part, c * deep + d)
                uv.append(jnp.where(in_unit, roll(lines[line], -unit * R), roll(lines[last_line], R - last)))
            turned = (cosine * uv[0] - sine * uv[1], sine * uv[0] + cosine * uv[1])
            at = slice((block * deep + d) * 8, (block * deep + d + 1) * 8)
            for c in range(2):
                ring[c, at, :] = jnp.where(in_outer, turned[c], ring[c, at, :])

    for slot in range(tiles):
        strip_copy(0, slot, 0, tile, row).wait_recv()
    lines = lines_of(seams)
    fill(lines, "first", 1)
    fill(lines, "middle", 2)
    fill(lines, "last", 3)
    own_rows = [ring[c, halo : halo + n_rows, :] for c in range(2)]
    for c, part in enumerate(smooth_field(own_rows, x_edge_field, y_own_field)):
        field_sum[c] += part
    advect_sum[...] += smooth_advect(advected(ring, halo + 8, n_rows - 16), x_edge_advect, y_own_advect)
    first_sends(lambda copy: copy.wait_send())

    for part, there in ((1, has_up), (2, has_down)):

        @pl.when(there)
        def _():
            for slot in range(tiles):
                strip_copy(part, slot, 0, tile, row).wait_recv()

    fill([None] * group + lines_of(above), "last", 0)
    fill(lines_of(below), "first", 4)
    rim = [jnp.concatenate([ring[c, 0:halo, :], ring[c, halo + n_rows :, :]], axis=0) for c in range(2)]
    smooth = []
    for c, part in enumerate(smooth_field(rim, x_edge_field, y_rim_field)):
        both = field_sum[c] + part
        smooth.append((both[:span_out, :LANES], both[:span_out, LANES:], both[span_out:, :LANES]))
    before = advected(ring, top, R + 8)
    behind = advected(ring, halo + n_rows - 8, span - n_rows + 16 - (R + 8))
    rim = [jnp.concatenate(pair, axis=0) for pair in zip(before, behind)]
    advect = advect_sum[...] + smooth_advect(rim, x_edge_advect, y_rim_advect)
    (u, u_x, u_y), (v, v_x, v_y) = smooth
    fine = (
        advect[:, :LANES] - (u * u_x + v * u_y),
        advect[:, LANES:] - (u * v_x + v * v_y),
    )

    n_out = n_rows // POOL
    m_out = n_cols // POOL
    col = lax.broadcasted_iota(jnp.int32, (LANES, m_out), 0)
    block_at = lax.broadcasted_iota(jnp.int32, (LANES, m_out), 1) * POOL
    mean = jnp.where((col >= block_at) & (col < block_at + POOL), 1.0 / POOL**2, 0.0)
    mean = mean.astype(jnp.bfloat16)
    for c in range(2):
        pooled[c, :, 0:n_cols] = fine[c][:n_rows, :n_cols] * wet
        total = pooled[c, pl.ds(0, n_out, stride=POOL), :]
        for k in range(1, POOL):
            total = total + pooled[c, pl.ds(k, n_out, stride=POOL), :]
        high, low = split(total)
        out_ref[c] = dot(high, mean) + dot(low, mean)

    rim_sends(lambda copy: copy.wait_send())


def on_device(velocity, wet_bits, east_face, seam_turn):
    _, n_rows, n_cols = velocity.shape
    tiles = lax.axis_size("tile")
    halo = ceil_to(RIM, 8)
    assert n_rows == 3 * halo and lax.axis_size("sub") == 2
    assert 2 * RIM <= n_cols <= LANES and LANES % R == 0
    per_row, units = LANES // R, 2 * halo // 8
    group_rows = ceil_to(units + 2, per_row) // per_row * 8
    strip_rows = 2 * group_rows + ceil_to(units - 2, per_row) // per_row * 8
    assert units % per_row < per_row - 1 and 2 * units <= R
    n_ext = n_rows + 2 * halo
    f32 = jnp.float32
    return pl.pallas_call(
        kernel,
        out_shape=pltpu.VMEM((2, n_rows // POOL, n_cols // POOL), f32),
        in_specs=[pl.BlockSpec(memory_space=pltpu.HBM)] * 4,
        out_specs=pl.BlockSpec(memory_space=pltpu.VMEM),
        scratch_shapes=[
            pltpu.SMEM(east_face.shape, jnp.int32),
            pltpu.SMEM(seam_turn.shape, jnp.int32),
            pltpu.VMEM(velocity.shape, f32),
            pltpu.VMEM(wet_bits.shape, jnp.int32),
            pltpu.VMEM((2, n_ext + 8, LANES), f32),
            pltpu.VMEM((strip_rows, LANES), f32),
            pltpu.VMEM((tiles, strip_rows, LANES), f32),
            pltpu.VMEM((tiles, group_rows, LANES), f32),
            pltpu.VMEM((tiles, group_rows, LANES), f32),
            pltpu.VMEM((2, n_ext, LANES), f32),
            pltpu.VMEM((2, n_ext + 8, LANES), f32),
            pltpu.VMEM((2, 2 * ceil_to(n_rows, 16), 2 * LANES), f32),
            pltpu.VMEM((ceil_to(n_rows, 16), 2 * LANES), f32),
            pltpu.VMEM((2, n_rows, LANES), f32),
            pltpu.SemaphoreType.DMA((4,)),
            pltpu.SemaphoreType.DMA((2,)),
            pltpu.SemaphoreType.DMA((2,)),
            pltpu.SemaphoreType.DMA((3,)),
            pltpu.SemaphoreType.DMA((3,)),
        ]
        + [pltpu.SemaphoreType.DMA((3, tiles))] * 2,
        compiler_params=pltpu.CompilerParams(
            collective_id=0, has_side_effects=True, vmem_limit_bytes=60 * 1024 * 1024
        ),
    )(east_face, seam_turn, velocity, wet_bits)


def solution(mesh):
    placed = (
        P(None, ("grp", "row"), ("tile", "sub")),
        P(("grp", "row"), ("tile", "sub")),
        P(),
        P(),
    )
    return jax.shard_map(
        on_device,
        mesh=mesh,
        in_specs=placed,
        out_specs=P(None, ("grp", "row"), ("tile", "sub")),
        check_vma=False,
    )
```

```python
import functools
import math

import jax
import jax.numpy as jnp
from jax import lax
from jax.experimental import pallas as pl
from jax.experimental.pallas import tpu as pltpu
from jax.sharding import PartitionSpec as P

R = 32
RIM = R + 1
LANES = 128
EDGE = 2
DERIV_SCALE = 8.0
POOL = 4
WORD_ROWS = 30
MESH = pl.DeviceIdType.MESH

WEIGHT_SUM = sum(math.exp(-0.5 * (k / R) ** 2) for k in range(-R, R + 1))


def ceil_to(value, step):
    return -(-value // step) * step


def gaussian(distance, keep):
    d = distance.astype(jnp.float32) * (1.0 / R)
    weight = jnp.exp(-0.5 * d * d) * (1.0 / WEIGHT_SUM)
    return jnp.where(keep & (jnp.abs(distance) <= R), weight, 0.0)


def split(value):
    high = value.astype(jnp.bfloat16)
    low = (value - high.astype(jnp.float32)).astype(jnp.bfloat16)
    return high, low


def dot(a, b):
    return jnp.dot(a, b, preferred_element_type=jnp.float32)


def roll(value, shift, axis=1):
    size = value.shape[axis]
    shift = shift % size
    return value if shift == 0 else pltpu.roll(value, shift, axis)


def kernel(
    face_hbm, turn_hbm, vel_hbm, bits_hbm, out_ref,
    face_ref, turn_ref, vel, bits, ext, strip, seams, above, below, beside,
    ring, field_sum, advect_sum, pooled,
    load_sem, row_send, row_recv, beside_send, beside_recv, strip_send, strip_recv,
):
    tiles, rows = lax.axis_size("tile"), lax.axis_size("row")
    grp, tile, row, sub = (lax.axis_index(a) for a in ("grp", "tile", "row", "sub"))
    n_rows, n_cols = vel.shape[1], vel.shape[2]
    halo = ceil_to(RIM, 8)
    has_up, has_down = row > 0, row < rows - 1
    other = 1 - sub

    barrier = pltpu.get_barrier_semaphore()

    def greet(t, r, s):
        pl.semaphore_signal(barrier, inc=1, device_id=(grp, t, r, s), device_id_type=MESH)

    in_left = tile < tiles // 2
    far_first = [jnp.where(in_left, tiles - 1 - k, k) for k in range(tiles)]
    for t in far_first:
        greet(t, row, other)
        for there, r in ((has_up, row - 1), (has_down, row + 1)):

            @pl.when(there)
            def _():
                greet(t, r, other)

    for there, r in ((has_up, row - 1), (has_down, row + 1)):

        @pl.when(there)
        def _():
            greet(tile, r, sub)

    loads = [
        pltpu.make_async_copy(vel_hbm, vel, load_sem.at[0]),
        pltpu.make_async_copy(bits_hbm, bits, load_sem.at[1]),
        pltpu.make_async_copy(face_hbm, face_ref, load_sem.at[2]),
        pltpu.make_async_copy(turn_hbm, turn_ref, load_sem.at[3]),
    ]
    for load in loads:
        load.start()

    west_lane = LANES - EDGE - RIM
    place = lax.broadcasted_iota(jnp.int32, (LANES, LANES), 0)
    x_out = lax.broadcasted_iota(jnp.int32, (LANES, LANES), 1)

    def field_weights(distance, keep, axis):
        weight = gaussian(distance, keep(0))
        slope = DERIV_SCALE * (gaussian(distance - 1, keep(-1)) - gaussian(distance + 1, keep(1)))
        return split(jnp.concatenate([weight, slope], axis=axis))

    def x_field_weights(x_in, keep):
        high, low = field_weights(x_in - x_out, lambda step: keep & (x_out < n_cols), 1)
        return jnp.concatenate([high, high], axis=0), low

    def x_advect_weights(x_in, keep):
        high, low = split(gaussian(x_in - x_out, keep & (x_out < n_cols)))
        above = jnp.concatenate([high, low], axis=1)
        below = jnp.concatenate([high, jnp.zeros_like(low)], axis=1)
        return jnp.concatenate([above, below], axis=0)

    x_own_field = x_field_weights(place, place < n_cols)
    x_own_advect = x_advect_weights(place, (place >= 1) & (place <= n_cols - 2))
    at_east = place < LANES // 2
    x_edge = jnp.where(at_east, place + (n_cols - EDGE), place - (west_lane + RIM))
    x_edge_field = x_field_weights(
        x_edge, ((place >= EDGE) & (place <= RIM + 1)) | ((place >= west_lane) & (place < west_lane + RIM))
    )
    x_edge_advect = x_advect_weights(
        x_edge, ((place >= 1) & (place <= RIM)) | ((place > west_lane) & (place <= west_lane + RIM))
    )
    top = halo - R
    span = ceil_to(n_rows + 2 * R, 16)
    n_ext = n_rows + 2 * halo
    n_field = ext.shape[1]
    span_out = ceil_to(n_rows, 16)

    for load in loads:
        load.wait()

    row_id = lax.broadcasted_iota(jnp.int32, (n_rows, n_cols), 0)
    words = bits[...]
    word = jnp.broadcast_to(words[0:1], (n_rows, n_cols))
    bit = row_id
    for j in range(1, words.shape[0]):
        here = row_id >= j * WORD_ROWS
        word = jnp.where(here, words[j : j + 1], word)
        bit = jnp.where(here, row_id - j * WORD_ROWS, bit)
    wet = (jnp.right_shift(word, bit) & 1).astype(jnp.float32)
    for c in range(2):
        ext[c, halo : halo + n_rows, :] = jnp.zeros((n_rows, LANES), jnp.float32)
        ext[c, halo : halo + n_rows, 0:n_cols] = vel[c] * wet
        ext[c, n_rows + 2 * halo :, :] = jnp.zeros((8, LANES), jnp.float32)

    per_row = LANES // R
    deep = halo // 8
    units = 2 * deep
    group = ceil_to(units + 2, per_row) // per_row
    group_rows = group * 8
    strip_rows = strip.shape[0]
    lane = lax.broadcasted_iota(jnp.int32, (8, LANES), 1)

    def place_of(part, i):
        last = (group - 1, units % per_row * R + i)
        if part == "first":
            return divmod(i, per_row), last
        if part == "last":
            at, unit = divmod(i, per_row)
            return (group + at, unit), (group + last[0], last[1])
        last = (last[0], last[1] + units)
        if i < 2:
            return (i * group + group - 1, units % per_row + 1), last
        at, unit = divmod(i - 2, per_row)
        return (2 * group + at, unit), last

    at_west = sub == 0
    lines = [jnp.zeros((8, LANES), jnp.float32)] * (strip_rows // 8)
    for c in range(2):
        own = ext[c, halo : halo + n_rows, :]
        own = jnp.where(at_west, own, roll(own, RIM - n_cols))
        for p, part in enumerate(("first", "middle", "last")):
            for d in range(deep):
                unit = own[(p * deep + d) * 8 : (p * deep + d + 1) * 8]
                (line, at), (last_line, last) = place_of(part, c * deep + d)
                lines[line] = jnp.where(lane // R == at, roll(unit, at * R), lines[line])
                lines[last_line] = jnp.where(lane == last, roll(unit, last - R), lines[last_line])
    for i, line in enumerate(lines):
        strip[i * 8 : (i + 1) * 8, :] = line

    @pl.when(jnp.logical_not(has_up))
    def _():
        ext[:, 0:halo, :] = jnp.zeros((2, halo, LANES), jnp.float32)
        beside[:, 0:halo, :] = jnp.zeros((2, halo, LANES), jnp.float32)
        above[...] = jnp.zeros((tiles, group_rows, LANES), jnp.float32)

    @pl.when(jnp.logical_not(has_down))
    def _():
        ext[:, halo + n_rows : n_rows + 2 * halo, :] = jnp.zeros((2, halo, LANES), jnp.float32)
        beside[:, halo + n_rows :, :] = jnp.zeros((2, halo, LANES), jnp.float32)
        below[...] = jnp.zeros((tiles, group_rows, LANES), jnp.float32)

    n_beside = has_up.astype(jnp.int32) + has_down.astype(jnp.int32)
    pl.semaphore_wait(barrier, tiles + n_beside * (tiles + 1))

    def strip_copy(part, slot, k, t, r):
        source, size = ((0, strip_rows), (group_rows, group_rows), (0, group_rows))[part]
        return pltpu.make_async_remote_copy(
            src_ref=strip.at[pl.ds(source, size)],
            dst_ref=(seams, above, below)[part].at[slot],
            send_sem=strip_send.at[part, k],
            recv_sem=strip_recv.at[part, slot],
            device_id=(grp, t, r, other),
            device_id_type=MESH,
        )

    def beside_copy(part, r):
        source, size = ((halo, n_rows), (n_rows, halo), (halo, halo))[part]
        target = (halo, 0, halo + n_rows)[part]
        return pltpu.make_async_remote_copy(
            src_ref=ext.at[:, pl.ds(source, size)],
            dst_ref=beside.at[:, pl.ds(target, size)],
            send_sem=beside_send.at[part],
            recv_sem=beside_recv.at[part],
            device_id=(grp, tile, r, other),
            device_id_type=MESH,
        )

    def row_copy(part, r):
        source = (halo + n_rows - halo, halo)[part - 1]
        target = (0, halo + n_rows)[part - 1]
        return pltpu.make_async_remote_copy(
            src_ref=ext.at[:, pl.ds(source, halo)],
            dst_ref=ext.at[:, pl.ds(target, halo)],
            send_sem=row_send.at[part - 1],
            recv_sem=row_recv.at[part - 1],
            device_id=(grp, tile, r, sub),
            device_id_type=MESH,
        )

    def strip_sends(act, part, r, ranks):
        for k in ranks:
            act(strip_copy(part, tile, k, far_first[k], r))

    def beside_sends(act):
        act(beside_copy(0, row))
        for part, there, r in ((1, has_down, row + 1), (2, has_up, row - 1)):

            @pl.when(there)
            def _():
                act(row_copy(part, r))
                act(beside_copy(part, r))

    def rim_sends(act, ranks):
        for part, there, r in ((1, has_down, row + 1), (2, has_up, row - 1)):

            @pl.when(there)
            def _():
                strip_sends(act, part, r, ranks)

    far, near = range(tiles // 2), range(tiles // 2, tiles)
    start, sent = (lambda copy: copy.start()), (lambda copy: copy.wait_send())
    strip_sends(start, 0, row, far)
    rim_sends(start, far)
    beside_sends(start)
    strip_sends(start, 0, row, near)
    rim_sends(start, near)

    def y_places(length, place):
        y_out = lax.broadcasted_iota(jnp.int32, (span_out, length), 0)
        y_in = place(lax.broadcasted_iota(jnp.int32, (span_out, length), 1))

        def keep(step):
            y_global = y_in + step + row * n_rows
            return (y_global >= 0) & (y_global < rows * n_rows) & (y_out < n_rows)

        return y_in - y_out, keep

    def y_field_weights(length, place):
        return field_weights(*y_places(length, place), 0)

    def y_advect_weights(length, place):
        distance, keep = y_places(length, place)
        return split(gaussian(distance, keep(0)))

    y_all_field = y_field_weights(n_field, lambda k: k - halo)
    y_all_advect = y_advect_weights(span, lambda k: k - R)
    y_own_field = y_field_weights(n_rows, lambda k: k)
    y_own_advect = y_advect_weights(n_rows - 16, lambda k: k + 8)
    y_rim_field = y_field_weights(n_field - n_rows, lambda k: jnp.where(k < halo, k - halo, k - halo + n_rows))
    y_rim_advect = y_advect_weights(
        span - n_rows + 16, lambda k: jnp.where(k < R + 8, k - R, k - R + n_rows - 16)
    )

    west = jnp.int32(0)
    for i in range(tiles):
        west = jnp.where(face_ref[i] == tile, i, west)
    across_seam = jnp.where(at_west, west, face_ref[tile])
    east_turn = turn_ref[tile]
    west_turn = turn_ref[west]
    west_turn = jnp.where(west_turn == 0, 0, 4 - west_turn)
    turn = jnp.where(at_west, west_turn, east_turn)

    def choose(a, b):
        return jnp.where(turn == a, 1.0, jnp.where(turn == b, -1.0, 0.0)).astype(jnp.float32)

    cosine, sine = choose(0, 2), choose(1, 3)

    def derive(field, c, start, length):
        centre = field[c, start : start + length, :]
        grad_x = DERIV_SCALE * (roll(centre, -1) - roll(centre, 1))
        grad_y = DERIV_SCALE * (field[c, start + 1 : start + 1 + length, :] - field[c, start - 1 : start - 1 + length, :])
        return centre, grad_x, grad_y

    def advected(field, start, length):
        u, u_x, u_y = derive(field, 0, start, length)
        v, v_x, v_y = derive(field, 1, start, length)
        return u * u_x + v * u_y, u * v_x + v * v_y

    def along_field(value, weights):
        high, low = split(value)
        return dot(jnp.concatenate([high, low], axis=1), weights[0]) + dot(high, weights[1])

    def along_advect(value, weights):
        both = dot(jnp.concatenate(split(value), axis=1), weights)
        return both[:, :LANES] + both[:, LANES:]

    beside_copy(0, row).wait_recv()
    for part, there in ((1, has_up), (2, has_down)):

        @pl.when(there)
        def _():
            row_copy(part, row).wait_recv()
            beside_copy(part, row).wait_recv()

    def smoothed(value, weights):
        (high, low), (value_high, value_low) = weights, split(value)
        return dot(high, value_high) + (dot(high, value_low) + dot(low, value_high))

    def smooth_field(parts, x_weights, y_weights):
        return [smoothed(along_field(part, x_weights), y_weights) for part in parts]

    def smooth_advect(parts, x_weights, y_weights):
        return smoothed(jnp.concatenate([along_advect(part, x_weights) for part in parts], axis=1), y_weights)

    for c, part in enumerate(smooth_field((ext[0], ext[1]), x_own_field, y_all_field)):
        field_sum[c] = part
    advect_sum[...] = smooth_advect(advected(ext, top, span), x_own_advect, y_all_advect)
    for c in range(2):
        pooled[c] = jnp.zeros((n_rows, LANES), jnp.float32)

    lane = lax.broadcasted_iota(jnp.int32, (n_ext, LANES), 1)
    inner_at = jnp.where(at_west, EDGE, west_lane)
    in_inner = (lane >= inner_at) & (lane < inner_at + RIM)
    for c in range(2):
        own, inner = ext[c, 0:n_ext, :], beside[c]
        inner = jnp.where(at_west, roll(inner, EDGE), roll(inner, west_lane + RIM - n_cols))
        rest = jnp.where(lane >= LANES - EDGE, roll(own, -EDGE), jnp.where(in_inner, inner, 0.0))
        ring[c, 0:n_ext, :] = jnp.where(lane < EDGE, roll(own, EDGE - n_cols), rest)
        ring[c, n_ext:, :] = jnp.zeros((8, LANES), jnp.float32)

    outer_at = jnp.where(at_west, west_lane, EDGE)
    lane = lax.broadcasted_iota(jnp.int32, (8, LANES), 1)
    in_unit = lane < outer_at + R
    in_outer = (lane >= outer_at) & (lane < outer_at + RIM)

    def lines_of(strips):
        held = strips[across_seam]
        held = jnp.where(at_west, roll(held, west_lane), roll(held, EDGE))
        return [held[i * 8 : (i + 1) * 8] for i in range(held.shape[0] // 8)]

    def fill(lines, part, block):
        for d in range(deep):
            uv = []
            for c in range(2):
                (line, unit), (last_line, last) = place_of(part, c * deep + d)
                uv.append(jnp.where(in_unit, roll(lines[line], -unit * R), roll(lines[last_line], R - last)))
            turned = (cosine * uv[0] - sine * uv[1], sine * uv[0] + cosine * uv[1])
            at = slice((block * deep + d) * 8, (block * deep + d + 1) * 8)
            for c in range(2):
                ring[c, at, :] = jnp.where(in_outer, turned[c], ring[c, at, :])

    for slot in range(tiles):
        strip_copy(0, slot, 0, tile, row).wait_recv()
    lines = lines_of(seams)
    fill(lines, "first", 1)
    fill(lines, "middle", 2)
    fill(lines, "last", 3)
    own_rows = [ring[c, halo : halo + n_rows, :] for c in range(2)]
    for c, part in enumerate(smooth_field(own_rows, x_edge_field, y_own_field)):
        field_sum[c] += part
    advect_sum[...] += smooth_advect(advected(ring, halo + 8, n_rows - 16), x_edge_advect, y_own_advect)
    strip_sends(sent, 0, row, range(tiles))
    beside_sends(sent)

    for part, there in ((1, has_up), (2, has_down)):

        @pl.when(there)
        def _():
            for slot in range(tiles):
                strip_copy(part, slot, 0, tile, row).wait_recv()

    fill([None] * group + lines_of(above), "last", 0)
    fill(lines_of(below), "first", 4)
    rim = [jnp.concatenate([ring[c, 0:halo, :], ring[c, halo + n_rows :, :]], axis=0) for c in range(2)]
    smooth = []
    for c, part in enumerate(smooth_field(rim, x_edge_field, y_rim_field)):
        both = field_sum[c] + part
        smooth.append((both[:span_out, :LANES], both[:span_out, LANES:], both[span_out:, :LANES]))
    before = advected(ring, top, R + 8)
    behind = advected(ring, halo + n_rows - 8, span - n_rows + 16 - (R + 8))
    rim = [jnp.concatenate(pair, axis=0) for pair in zip(before, behind)]
    advect = advect_sum[...] + smooth_advect(rim, x_edge_advect, y_rim_advect)
    (u, u_x, u_y), (v, v_x, v_y) = smooth
    fine = (
        advect[:, :LANES] - (u * u_x + v * u_y),
        advect[:, LANES:] - (u * v_x + v * v_y),
    )

    n_out = n_rows // POOL
    m_out = n_cols // POOL
    col = lax.broadcasted_iota(jnp.int32, (LANES, m_out), 0)
    block_at = lax.broadcasted_iota(jnp.int32, (LANES, m_out), 1) * POOL
    mean = jnp.where((col >= block_at) & (col < block_at + POOL), 1.0 / POOL**2, 0.0)
    mean = mean.astype(jnp.bfloat16)
    for c in range(2):
        pooled[c, :, 0:n_cols] = fine[c][:n_rows, :n_cols] * wet
        total = pooled[c, pl.ds(0, n_out, stride=POOL), :]
        for k in range(1, POOL):
            total = total + pooled[c, pl.ds(k, n_out, stride=POOL), :]
        high, low = split(total)
        out_ref[c] = dot(high, mean) + dot(low, mean)

    rim_sends(sent, range(tiles))


def on_device(velocity, wet_bits, east_face, seam_turn):
    _, n_rows, n_cols = velocity.shape
    tiles = lax.axis_size("tile")
    halo = ceil_to(RIM, 8)
    assert n_rows == 3 * halo and lax.axis_size("sub") == 2
    assert 2 * RIM <= n_cols <= LANES and LANES % R == 0
    per_row, units = LANES // R, 2 * halo // 8
    group_rows = ceil_to(units + 2, per_row) // per_row * 8
    strip_rows = 2 * group_rows + ceil_to(units - 2, per_row) // per_row * 8
    assert units % per_row < per_row - 1 and 2 * units <= R
    n_ext = n_rows + 2 * halo
    f32 = jnp.float32
    return pl.pallas_call(
        kernel,
        out_shape=pltpu.VMEM((2, n_rows // POOL, n_cols // POOL), f32),
        in_specs=[pl.BlockSpec(memory_space=pltpu.HBM)] * 4,
        out_specs=pl.BlockSpec(memory_space=pltpu.VMEM),
        scratch_shapes=[
            pltpu.SMEM(east_face.shape, jnp.int32),
            pltpu.SMEM(seam_turn.shape, jnp.int32),
            pltpu.VMEM(velocity.shape, f32),
            pltpu.VMEM(wet_bits.shape, jnp.int32),
            pltpu.VMEM((2, n_ext + 8, LANES), f32),
            pltpu.VMEM((strip_rows, LANES), f32),
            pltpu.VMEM((tiles, strip_rows, LANES), f32),
            pltpu.VMEM((tiles, group_rows, LANES), f32),
            pltpu.VMEM((tiles, group_rows, LANES), f32),
            pltpu.VMEM((2, n_ext, LANES), f32),
            pltpu.VMEM((2, n_ext + 8, LANES), f32),
            pltpu.VMEM((2, 2 * ceil_to(n_rows, 16), 2 * LANES), f32),
            pltpu.VMEM((ceil_to(n_rows, 16), 2 * LANES), f32),
            pltpu.VMEM((2, n_rows, LANES), f32),
            pltpu.SemaphoreType.DMA((4,)),
            pltpu.SemaphoreType.DMA((2,)),
            pltpu.SemaphoreType.DMA((2,)),
            pltpu.SemaphoreType.DMA((3,)),
            pltpu.SemaphoreType.DMA((3,)),
        ]
        + [pltpu.SemaphoreType.DMA((3, tiles))] * 2,
        compiler_params=pltpu.CompilerParams(
            collective_id=0, has_side_effects=True, vmem_limit_bytes=60 * 1024 * 1024
        ),
    )(east_face, seam_turn, velocity, wet_bits)


def solution(mesh):
    placed = (
        P(None, ("grp", "row"), ("tile", "sub")),
        P(("grp", "row"), ("tile", "sub")),
        P(),
        P(),
    )
    return jax.shard_map(
        on_device,
        mesh=mesh,
        in_specs=placed,
        out_specs=P(None, ("grp", "row"), ("tile", "sub")),
        check_vma=False,
    )
```

```python
import functools
import math

import jax
import jax.numpy as jnp
from jax import lax
from jax.experimental import pallas as pl
from jax.experimental.pallas import tpu as pltpu
from jax.sharding import PartitionSpec as P

R = 32
RIM = R + 1
LANES = 128
EDGE = 2
DERIV_SCALE = 8.0
POOL = 4
WORD_ROWS = 30
MESH = pl.DeviceIdType.MESH

WEIGHT_SUM = sum(math.exp(-0.5 * (k / R) ** 2) for k in range(-R, R + 1))


def ceil_to(value, step):
    return -(-value // step) * step


def gaussian(distance, keep):
    d = distance.astype(jnp.float32) * (1.0 / R)
    weight = jnp.exp(-0.5 * d * d) * (1.0 / WEIGHT_SUM)
    return jnp.where(keep & (jnp.abs(distance) <= R), weight, 0.0)


def split(value):
    high = value.astype(jnp.bfloat16)
    low = (value - high.astype(jnp.float32)).astype(jnp.bfloat16)
    return high, low


def dot(a, b):
    return jnp.dot(a, b, preferred_element_type=jnp.float32)


def roll(value, shift, axis=1):
    size = value.shape[axis]
    shift = shift % size
    return value if shift == 0 else pltpu.roll(value, shift, axis)


def kernel(
    face_hbm, turn_hbm, vel_hbm, bits_hbm, out_ref,
    face_ref, turn_ref, vel, bits, ext, strip, seams, above, below, beside,
    ring, field_sum, advect_sum, pooled,
    load_sem, row_send, row_recv, beside_send, beside_recv, strip_send, strip_recv,
):
    tiles, rows = lax.axis_size("tile"), lax.axis_size("row")
    grp, tile, row, sub = (lax.axis_index(a) for a in ("grp", "tile", "row", "sub"))
    n_rows, n_cols = vel.shape[1], vel.shape[2]
    halo = ceil_to(RIM, 8)
    has_up, has_down = row > 0, row < rows - 1
    other = 1 - sub

    barrier = pltpu.get_barrier_semaphore()

    def greet(t, r, s):
        pl.semaphore_signal(barrier, inc=1, device_id=(grp, t, r, s), device_id_type=MESH)

    in_left = tile < tiles // 2
    far_first = [jnp.where(in_left, tiles - 1 - k, k) for k in range(tiles)]
    for t in far_first:
        greet(t, row, other)
        for there, r in ((has_up, row - 1), (has_down, row + 1)):

            @pl.when(there)
            def _():
                greet(t, r, other)

    for there, r in ((has_up, row - 1), (has_down, row + 1)):

        @pl.when(there)
        def _():
            greet(tile, r, sub)

    loads = [
        pltpu.make_async_copy(vel_hbm, vel, load_sem.at[0]),
        pltpu.make_async_copy(bits_hbm, bits, load_sem.at[1]),
        pltpu.make_async_copy(face_hbm, face_ref, load_sem.at[2]),
        pltpu.make_async_copy(turn_hbm, turn_ref, load_sem.at[3]),
    ]
    for load in loads:
        load.start()

    west_lane = LANES - EDGE - RIM
    place = lax.broadcasted_iota(jnp.int32, (LANES, LANES), 0)
    x_out = lax.broadcasted_iota(jnp.int32, (LANES, LANES), 1)

    def field_weights(distance, keep, axis):
        weight = gaussian(distance, keep(0))
        slope = DERIV_SCALE * (gaussian(distance - 1, keep(-1)) - gaussian(distance + 1, keep(1)))
        return split(jnp.concatenate([weight, slope], axis=axis))

    def x_field_weights(x_in, keep):
        high, low = field_weights(x_in - x_out, lambda step: keep & (x_out < n_cols), 1)
        return jnp.concatenate([high, high], axis=0), low

    def x_advect_weights(x_in, keep):
        high, low = split(gaussian(x_in - x_out, keep & (x_out < n_cols)))
        above = jnp.concatenate([high, low], axis=1)
        below = jnp.concatenate([high, jnp.zeros_like(low)], axis=1)
        return jnp.concatenate([above, below], axis=0)

    x_own_field = x_field_weights(place, place < n_cols)
    x_own_advect = x_advect_weights(place, (place >= 1) & (place <= n_cols - 2))
    at_east = place < LANES // 2
    x_edge = jnp.where(at_east, place + (n_cols - EDGE), place - (west_lane + RIM))
    x_edge_field = x_field_weights(
        x_edge, ((place >= EDGE) & (place <= RIM + 1)) | ((place >= west_lane) & (place < west_lane + RIM))
    )
    x_edge_advect = x_advect_weights(
        x_edge, ((place >= 1) & (place <= RIM)) | ((place > west_lane) & (place <= west_lane + RIM))
    )
    top = halo - R
    span = ceil_to(n_rows + 2 * R, 16)
    n_ext = n_rows + 2 * halo
    n_field = ext.shape[1]
    span_out = ceil_to(n_rows, 16)

    for load in loads[:2]:
        load.wait()

    row_id = lax.broadcasted_iota(jnp.int32, (n_rows, n_cols), 0)
    words = bits[...]
    word = jnp.broadcast_to(words[0:1], (n_rows, n_cols))
    bit = row_id
    for j in range(1, words.shape[0]):
        here = row_id >= j * WORD_ROWS
        word = jnp.where(here, words[j : j + 1], word)
        bit = jnp.where(here, row_id - j * WORD_ROWS, bit)
    wet = (jnp.right_shift(word, bit) & 1).astype(jnp.float32)
    for c in range(2):
        ext[c, halo : halo + n_rows, :] = jnp.zeros((n_rows, LANES), jnp.float32)
        ext[c, halo : halo + n_rows, 0:n_cols] = vel[c] * wet
        ext[c, n_rows + 2 * halo :, :] = jnp.zeros((8, LANES), jnp.float32)

    per_row = LANES // R
    deep = halo // 8
    units = 2 * deep
    group = ceil_to(units + 2, per_row) // per_row
    group_rows = group * 8
    strip_rows = strip.shape[0]
    lane = lax.broadcasted_iota(jnp.int32, (8, LANES), 1)

    def place_of(part, i):
        last = (group - 1, units % per_row * R + i)
        if part == "first":
            return divmod(i, per_row), last
        if part == "last":
            at, unit = divmod(i, per_row)
            return (group + at, unit), (group + last[0], last[1])
        last = (last[0], last[1] + units)
        if i < 2:
            return (i * group + group - 1, units % per_row + 1), last
        at, unit = divmod(i - 2, per_row)
        return (2 * group + at, unit), last

    at_west = sub == 0
    lines = [jnp.zeros((8, LANES), jnp.float32)] * (strip_rows // 8)
    for c in range(2):
        own = ext[c, halo : halo + n_rows, :]
        own = jnp.where(at_west, own, roll(own, RIM - n_cols))
        for p, part in enumerate(("first", "middle", "last")):
            for d in range(deep):
                unit = own[(p * deep + d) * 8 : (p * deep + d + 1) * 8]
                (line, at), (last_line, last) = place_of(part, c * deep + d)
                lines[line] = jnp.where(lane // R == at, roll(unit, at * R), lines[line])
                lines[last_line] = jnp.where(lane == last, roll(unit, last - R), lines[last_line])
    for i, line in enumerate(lines):
        strip[i * 8 : (i + 1) * 8, :] = line

    @pl.when(jnp.logical_not(has_up))
    def _():
        ext[:, 0:halo, :] = jnp.zeros((2, halo, LANES), jnp.float32)
        beside[:, 0:halo, :] = jnp.zeros((2, halo, LANES), jnp.float32)
        above[...] = jnp.zeros((tiles, group_rows, LANES), jnp.float32)

    @pl.when(jnp.logical_not(has_down))
    def _():
        ext[:, halo + n_rows : n_rows + 2 * halo, :] = jnp.zeros((2, halo, LANES), jnp.float32)
        beside[:, halo + n_rows :, :] = jnp.zeros((2, halo, LANES), jnp.float32)
        below[...] = jnp.zeros((tiles, group_rows, LANES), jnp.float32)

    n_beside = has_up.astype(jnp.int32) + has_down.astype(jnp.int32)
    pl.semaphore_wait(barrier, tiles + n_beside * (tiles + 1))

    def strip_copy(part, slot, k, t, r):
        source, size = ((0, strip_rows), (group_rows, group_rows), (0, group_rows))[part]
        return pltpu.make_async_remote_copy(
            src_ref=strip.at[pl.ds(source, size)],
            dst_ref=(seams, above, below)[part].at[slot],
            send_sem=strip_send.at[part, k],
            recv_sem=strip_recv.at[part, slot],
            device_id=(grp, t, r, other),
            device_id_type=MESH,
        )

    def beside_copy(part, r):
        source, size = ((halo, n_rows), (n_rows, halo), (halo, halo))[part]
        target = (halo, 0, halo + n_rows)[part]
        return pltpu.make_async_remote_copy(
            src_ref=ext.at[:, pl.ds(source, size)],
            dst_ref=beside.at[:, pl.ds(target, size)],
            send_sem=beside_send.at[part],
            recv_sem=beside_recv.at[part],
            device_id=(grp, tile, r, other),
            device_id_type=MESH,
        )

    def row_copy(part, r):
        source = (halo + n_rows - halo, halo)[part - 1]
        target = (0, halo + n_rows)[part - 1]
        return pltpu.make_async_remote_copy(
            src_ref=ext.at[:, pl.ds(source, halo)],
            dst_ref=ext.at[:, pl.ds(target, halo)],
            send_sem=row_send.at[part - 1],
            recv_sem=row_recv.at[part - 1],
            device_id=(grp, tile, r, sub),
            device_id_type=MESH,
        )

    def strip_sends(act, part, r, ranks):
        for k in ranks:
            act(strip_copy(part, tile, k, far_first[k], r))

    def beside_sends(act):
        act(beside_copy(0, row))
        for part, there, r in ((1, has_down, row + 1), (2, has_up, row - 1)):

            @pl.when(there)
            def _():
                act(row_copy(part, r))
                act(beside_copy(part, r))

    def rim_sends(act, ranks):
        for part, there, r in ((1, has_down, row + 1), (2, has_up, row - 1)):

            @pl.when(there)
            def _():
                strip_sends(act, part, r, ranks)

    far, near = range(tiles // 2), range(tiles // 2, tiles)
    start, sent = (lambda copy: copy.start()), (lambda copy: copy.wait_send())
    strip_sends(start, 0, row, far)
    rim_sends(start, far)
    beside_sends(start)
    strip_sends(start, 0, row, near)
    rim_sends(start, near)

    def y_places(length, place):
        y_out = lax.broadcasted_iota(jnp.int32, (span_out, length), 0)
        y_in = place(lax.broadcasted_iota(jnp.int32, (span_out, length), 1))

        def keep(step):
            y_global = y_in + step + row * n_rows
            return (y_global >= 0) & (y_global < rows * n_rows) & (y_out < n_rows)

        return y_in - y_out, keep

    def y_field_weights(length, place):
        return field_weights(*y_places(length, place), 0)

    def y_advect_weights(length, place):
        distance, keep = y_places(length, place)
        return split(gaussian(distance, keep(0)))

    y_all_field = y_field_weights(n_field, lambda k: k - halo)
    y_all_advect = y_advect_weights(span, lambda k: k - R)
    y_own_field = y_field_weights(n_rows, lambda k: k)
    y_own_advect = y_advect_weights(n_rows - 16, lambda k: k + 8)
    y_rim_field = y_field_weights(n_field - n_rows, lambda k: jnp.where(k < halo, k - halo, k - halo + n_rows))
    y_rim_advect = y_advect_weights(
        span - n_rows + 16, lambda k: jnp.where(k < R + 8, k - R, k - R + n_rows - 16)
    )

    for load in loads[2:]:
        load.wait()

    west = jnp.int32(0)
    for i in range(tiles):
        west = jnp.where(face_ref[i] == tile, i, west)
    across_seam = jnp.where(at_west, west, face_ref[tile])
    east_turn = turn_ref[tile]
    west_turn = turn_ref[west]
    west_turn = jnp.where(west_turn == 0, 0, 4 - west_turn)
    turn = jnp.where(at_west, west_turn, east_turn)

    def choose(a, b):
        return jnp.where(turn == a, 1.0, jnp.where(turn == b, -1.0, 0.0)).astype(jnp.float32)

    cosine, sine = choose(0, 2), choose(1, 3)

    def derive(field, c, start, length):
        centre = field[c, start : start + length, :]
        grad_x = DERIV_SCALE * (roll(centre, -1) - roll(centre, 1))
        grad_y = DERIV_SCALE * (field[c, start + 1 : start + 1 + length, :] - field[c, start - 1 : start - 1 + length, :])
        return centre, grad_x, grad_y

    def advected(field, start, length):
        u, u_x, u_y = derive(field, 0, start, length)
        v, v_x, v_y = derive(field, 1, start, length)
        return u * u_x + v * u_y, u * v_x + v * v_y

    def along_field(value, weights):
        high, low = split(value)
        return dot(jnp.concatenate([high, low], axis=1), weights[0]) + dot(high, weights[1])

    def along_advect(value, weights):
        both = dot(jnp.concatenate(split(value), axis=1), weights)
        return both[:, :LANES] + both[:, LANES:]

    beside_copy(0, row).wait_recv()
    for part, there in ((1, has_up), (2, has_down)):

        @pl.when(there)
        def _():
            row_copy(part, row).wait_recv()
            beside_copy(part, row).wait_recv()

    def smoothed(value, weights):
        (high, low), (value_high, value_low) = weights, split(value)
        return dot(high, value_high) + (dot(high, value_low) + dot(low, value_high))

    def smooth_field(parts, x_weights, y_weights):
        return [smoothed(along_field(part, x_weights), y_weights) for part in parts]

    def smooth_advect(parts, x_weights, y_weights):
        return smoothed(jnp.concatenate([along_advect(part, x_weights) for part in parts], axis=1), y_weights)

    for c, part in enumerate(smooth_field((ext[0], ext[1]), x_own_field, y_all_field)):
        field_sum[c] = part
    advect_sum[...] = smooth_advect(advected(ext, top, span), x_own_advect, y_all_advect)
    for c in range(2):
        pooled[c] = jnp.zeros((n_rows, LANES), jnp.float32)

    lane = lax.broadcasted_iota(jnp.int32, (n_ext, LANES), 1)
    inner_at = jnp.where(at_west, EDGE, west_lane)
    in_inner = (lane >= inner_at) & (lane < inner_at + RIM)
    for c in range(2):
        own, inner = ext[c, 0:n_ext, :], beside[c]
        inner = jnp.where(at_west, roll(inner, EDGE), roll(inner, west_lane + RIM - n_cols))
        rest = jnp.where(lane >= LANES - EDGE, roll(own, -EDGE), jnp.where(in_inner, inner, 0.0))
        ring[c, 0:n_ext, :] = jnp.where(lane < EDGE, roll(own, EDGE - n_cols), rest)
        ring[c, n_ext:, :] = jnp.zeros((8, LANES), jnp.float32)

    outer_at = jnp.where(at_west, west_lane, EDGE)
    lane = lax.broadcasted_iota(jnp.int32, (8, LANES), 1)
    in_unit = lane < outer_at + R
    in_outer = (lane >= outer_at) & (lane < outer_at + RIM)

    def lines_of(strips):
        held = strips[across_seam]
        held = jnp.where(at_west, roll(held, west_lane), roll(held, EDGE))
        return [held[i * 8 : (i + 1) * 8] for i in range(held.shape[0] // 8)]

    def fill(lines, part, block):
        for d in range(deep):
            uv = []
            for c in range(2):
                (line, unit), (last_line, last) = place_of(part, c * deep + d)
                uv.append(jnp.where(in_unit, roll(lines[line], -unit * R), roll(lines[last_line], R - last)))
            turned = (cosine * uv[0] - sine * uv[1], sine * uv[0] + cosine * uv[1])
            at = slice((block * deep + d) * 8, (block * deep + d + 1) * 8)
            for c in range(2):
                ring[c, at, :] = jnp.where(in_outer, turned[c], ring[c, at, :])

    for slot in range(tiles):
        strip_copy(0, slot, 0, tile, row).wait_recv()
    lines = lines_of(seams)
    fill(lines, "first", 1)
    fill(lines, "middle", 2)
    fill(lines, "last", 3)
    own_rows = [ring[c, halo : halo + n_rows, :] for c in range(2)]
    for c, part in enumerate(smooth_field(own_rows, x_edge_field, y_own_field)):
        field_sum[c] += part
    advect_sum[...] += smooth_advect(advected(ring, halo + 8, n_rows - 16), x_edge_advect, y_own_advect)
    strip_sends(sent, 0, row, range(tiles))
    beside_sends(sent)

    for part, there in ((1, has_up), (2, has_down)):

        @pl.when(there)
        def _():
            for slot in range(tiles):
                strip_copy(part, slot, 0, tile, row).wait_recv()

    fill([None] * group + lines_of(above), "last", 0)
    fill(lines_of(below), "first", 4)
    rim = [jnp.concatenate([ring[c, 0:halo, :], ring[c, halo + n_rows :, :]], axis=0) for c in range(2)]
    smooth = []
    for c, part in enumerate(smooth_field(rim, x_edge_field, y_rim_field)):
        both = field_sum[c] + part
        smooth.append((both[:span_out, :LANES], both[:span_out, LANES:], both[span_out:, :LANES]))
    before = advected(ring, top, R + 8)
    behind = advected(ring, halo + n_rows - 8, span - n_rows + 16 - (R + 8))
    rim = [jnp.concatenate(pair, axis=0) for pair in zip(before, behind)]
    advect = advect_sum[...] + smooth_advect(rim, x_edge_advect, y_rim_advect)
    (u, u_x, u_y), (v, v_x, v_y) = smooth
    fine = (
        advect[:, :LANES] - (u * u_x + v * u_y),
        advect[:, LANES:] - (u * v_x + v * v_y),
    )

    n_out = n_rows // POOL
    m_out = n_cols // POOL
    col = lax.broadcasted_iota(jnp.int32, (LANES, m_out), 0)
    block_at = lax.broadcasted_iota(jnp.int32, (LANES, m_out), 1) * POOL
    mean = jnp.where((col >= block_at) & (col < block_at + POOL), 1.0 / POOL**2, 0.0)
    mean = mean.astype(jnp.bfloat16)
    for c in range(2):
        pooled[c, :, 0:n_cols] = fine[c][:n_rows, :n_cols] * wet
        total = pooled[c, pl.ds(0, n_out, stride=POOL), :]
        for k in range(1, POOL):
            total = total + pooled[c, pl.ds(k, n_out, stride=POOL), :]
        high, low = split(total)
        out_ref[c] = dot(high, mean) + dot(low, mean)

    rim_sends(sent, range(tiles))


def on_device(velocity, wet_bits, east_face, seam_turn):
    _, n_rows, n_cols = velocity.shape
    tiles = lax.axis_size("tile")
    halo = ceil_to(RIM, 8)
    assert n_rows == 3 * halo and lax.axis_size("sub") == 2
    assert 2 * RIM <= n_cols <= LANES and LANES % R == 0
    per_row, units = LANES // R, 2 * halo // 8
    group_rows = ceil_to(units + 2, per_row) // per_row * 8
    strip_rows = 2 * group_rows + ceil_to(units - 2, per_row) // per_row * 8
    assert units % per_row < per_row - 1 and 2 * units <= R
    n_ext = n_rows + 2 * halo
    f32 = jnp.float32
    return pl.pallas_call(
        kernel,
        out_shape=pltpu.VMEM((2, n_rows // POOL, n_cols // POOL), f32),
        in_specs=[pl.BlockSpec(memory_space=pltpu.HBM)] * 4,
        out_specs=pl.BlockSpec(memory_space=pltpu.VMEM),
        scratch_shapes=[
            pltpu.SMEM(east_face.shape, jnp.int32),
            pltpu.SMEM(seam_turn.shape, jnp.int32),
            pltpu.VMEM(velocity.shape, f32),
            pltpu.VMEM(wet_bits.shape, jnp.int32),
            pltpu.VMEM((2, n_ext + 8, LANES), f32),
            pltpu.VMEM((strip_rows, LANES), f32),
            pltpu.VMEM((tiles, strip_rows, LANES), f32),
            pltpu.VMEM((tiles, group_rows, LANES), f32),
            pltpu.VMEM((tiles, group_rows, LANES), f32),
            pltpu.VMEM((2, n_ext, LANES), f32),
            pltpu.VMEM((2, n_ext + 8, LANES), f32),
            pltpu.VMEM((2, 2 * ceil_to(n_rows, 16), 2 * LANES), f32),
            pltpu.VMEM((ceil_to(n_rows, 16), 2 * LANES), f32),
            pltpu.VMEM((2, n_rows, LANES), f32),
            pltpu.SemaphoreType.DMA((4,)),
            pltpu.SemaphoreType.DMA((2,)),
            pltpu.SemaphoreType.DMA((2,)),
            pltpu.SemaphoreType.DMA((3,)),
            pltpu.SemaphoreType.DMA((3,)),
        ]
        + [pltpu.SemaphoreType.DMA((3, tiles))] * 2,
        compiler_params=pltpu.CompilerParams(
            collective_id=0, has_side_effects=True, vmem_limit_bytes=60 * 1024 * 1024
        ),
    )(east_face, seam_turn, velocity, wet_bits)


def solution(mesh):
    placed = (
        P(None, ("grp", "row"), ("tile", "sub")),
        P(("grp", "row"), ("tile", "sub")),
        P(),
        P(),
    )
    return jax.shard_map(
        on_device,
        mesh=mesh,
        in_specs=placed,
        out_specs=P(None, ("grp", "row"), ("tile", "sub")),
        check_vma=False,
    )
```
